32 devices in a mesh: fluid: 8 (over z, y), sub: 4 (over x, core).
Axes of the slice: x: 2, y: 2, z: 4, core: 2. Of those that a mesh axis runs over, the one named last changes fastest.
Arguments:
- positions: float32 [3, 65536], P(None, ('fluid', 'sub')), may hold values from 0 to 1
- particle_temp: float32 [65536], P(('fluid', 'sub')), may hold values from -6 to 6
- pair_list: int32 [8192, 2], P(('fluid', 'sub')), may hold values from 0 to 31, as said below
- pair_count: int32 [32], P(('fluid', 'sub')), may hold values from 16 to 256, as said below
- ghost_particle: int32 [65536], P(('fluid', 'sub')), may hold values from 0 to 2047
- ghost_owner: int32 [65536, 1], P(('fluid', 'sub')), may hold values from 0 to 31; in each aligned block of 2048 rows (0 to 2047, 2048 to 4095, ...) at most 128 rows name the same one
- ghost_cell: int32 [65536], P(('fluid', 'sub')), may hold values from 0 to 32767
- wall_seen: float32 [65536], P(('fluid', 'sub')), may hold values from -6 to 6
- solid_temp: float32 [32, 512, 2048], P(None, ('fluid', 'sub')), may hold values from -6 to 6
- conduct: float32 [32, 512, 2048], P(None, ('fluid', 'sub')), may hold values from 0.03 to 0.16
Outputs:
- particle_out: float32 [65536], P(('fluid', 'sub'))
- solid_out: float32 [32, 512, 2048], P(None, ('fluid', 'sub'))
- ghost_temp: float32 [65536], P(('fluid', 'sub'))
The draws below stay inside these ranges and needn't reach their ends.
Inputs may be any that keep to these rules, and one draw needn't show every extreme that they name: `pair_list`: column 0 names one of the device's own tiles; column 1 names own tile t below 16, or tile t - 16 of the next device along sub, cyclically. `pair_count`: rows of a device's block beyond its count are not used; some device uses all 256. `ghost_owner`: among the 2048 ghosts of one device, at most 128 name the same owner.
All inputs are finite; a program needn't handle non-finite values.
Results may differ from the reference program's by a relative error of at most 0.0003.
Values sent between devices are 32-bit elements; how exact they have to be, the bound alone decides.
No kernel may reach another device: no remote copies, remote signals or barrier semaphores. Data moves between devices by JAX's collectives and lax.ppermute only.
A program may use at most 128 MiB of HBM per device.

```python
import math
import jax
import jax.numpy as jnp
import numpy as np
from jax import lax

TILE = 128
TILES = 16
PAIRS = 256
GHOST_DEV = 2048
SX = 16
NZS = 2048
DEPTH = 32
SUBSTEPS = 6
DEVICES_ALL = 32
CAP = 128
PARTICLES = 65536
PAIR_ROWS = 8192
GHOSTS = 65536
NXS = 512
N_FLUID = 8
N_SUB = 4


def draw_pair_list(key, part):
    first_key, second_key = jax.random.split(jax.random.fold_in(key, 11))
    first_tile = jax.random.randint(first_key, (PAIR_ROWS,), 0, TILES)
    second_tile = jax.random.randint(second_key, (PAIR_ROWS,), 0, 2 * TILES)
    return jnp.stack([first_tile, second_tile], axis=1).astype(jnp.int32)


def draw_pair_count(key, part):
    count_key, chosen_key = jax.random.split(jax.random.fold_in(key, 23))
    devices = PAIR_ROWS // PAIRS
    counts = jax.random.randint(count_key, (devices,), PAIRS // 16, PAIRS + 1)
    chosen = jax.random.randint(chosen_key, (), 0, devices)
    return counts.at[chosen].set(PAIRS).astype(jnp.int32)


def set_ends(array, rng, low, largest):
    index_at = [jax.random.randint(jax.random.fold_in(rng, axis), (), 0, length) for axis, length in enumerate(array.shape)]
    main_axis = array.shape.index(max(array.shape))
    neighbour = index_at[:main_axis] + [(index_at[main_axis] + 1) % array.shape[main_axis]] + index_at[main_axis + 1:]
    return array.at[tuple(index_at)].set(low).at[tuple(neighbour)].set(largest)


def steps_of(own_key, dims, cuts, least, high):
    def one(dim, blocks):
        heights = jax.random.uniform(jax.random.fold_in(jax.random.fold_in(own_key, 6), dim), (blocks,), jnp.float32, least / len(cuts), high / len(cuts))
        return jnp.repeat(jnp.exp(heights), dims[dim] // blocks).reshape((-1,) + (1,) * (len(dims) - dim - 1))

    level = one(*cuts[0])
    for cut in cuts[1:]:
        level = level * one(*cut)
    return level


def deal_out(rng, own, number, rows, count, top, bound, lean):
    ranking = jax.random.permutation(rng, count)
    packed, common = load_shares(count, rows * top, bound, lean, True), load_shares(count, rows * top, bound, lean, False)
    places = jnp.arange(count)

    def named(lengths, offset_by):
        used = int((lengths > 0).sum())
        fixed = max(1, used // 4)
        passed = fixed + (places - fixed + offset_by * (used - fixed)) % max(1, count - fixed)
        return jnp.zeros((count,), jnp.int32).at[ranking[jnp.where(places < fixed, places, passed)]].set(jnp.asarray(lengths, jnp.int32))

    lengths = jnp.where(number % 4 == 0, named(packed, number // 4), named(common, number - number // 4 - 1))
    mixed = jax.random.permutation(jax.random.fold_in(own, 3), count)
    donor, sink = mixed[0:count // 2 * 2:2], mixed[1:count // 2 * 2:2]
    slack = jnp.minimum(lengths[donor] - 1, bound - lengths[sink]) // 2
    slack = jnp.where((donor == ranking[0]) | (sink == ranking[0]) | (lengths[sink] == 0), 0, jnp.maximum(slack, 0))
    passed = jax.random.randint(jax.random.fold_in(own, 4), (count // 2,), 0, 1 << 20) % (slack + 1)
    lengths = lengths.at[donor].add(-passed).at[sink].add(passed)
    labels = jnp.searchsorted(jnp.cumsum(lengths), jnp.arange(rows * top), side="right").astype(jnp.int32)
    grid = labels.reshape(top, rows).T
    grid = grid[jax.random.permutation(jax.random.fold_in(own, 1), rows)]
    offset_by = jax.random.randint(jax.random.fold_in(own, 2), (rows, 1), 0, top)
    return jnp.take_along_axis(grid, (jnp.arange(top)[None, :] + offset_by) % top, axis=1)


def load_shares(count, total, reach, slope, full):
    weights = [(1 << 20) // math.isqrt(grade ** slope) + 1 for grade in range(1, count + 1)]
    largest = reach if full else min(reach, max(-(-total // count), total * weights[0] // sum(weights)))
    least = 1 if total - largest >= count - 1 else 0
    given, surplus = [largest] + [least] * (count - 1), total - largest - least * (count - 1)
    while surplus > 0:
        free = [i for i in range(1, count) if given[i] < largest] or [i for i in range(1, count) if given[i] < reach]
        mass, budget = sum([weights[i] for i in free]), surplus
        for i in free:
            extra = min(reach - given[i], max(1, budget * weights[i] // mass), surplus)
            given[i] = given[i] + extra
            surplus = surplus - extra
    return np.array(given)


def scatter_about(own_key, dims, scale, limit, cuts=(), held_as=jnp.bfloat16):
    values = scale * jax.random.normal(own_key, dims, jnp.float32)
    if cuts:
        values = values * steps_of(own_key, dims, cuts, -0.22, 0.18)
    return jnp.clip(values, -limit, limit).astype(held_as)


def setup_inputs(seed: int = 0) -> dict:
    keys = jax.random.split(jax.random.key(seed), 11)
    positions = jnp.clip(1.0 * jax.random.uniform(keys[0], (3, PARTICLES), jnp.float32) ** steps_of(keys[0], (3, PARTICLES), ((1, 32),), -0.2, 0.2), 0.0, 1.0)
    particle_temp = scatter_about(keys[1], (PARTICLES,), 1.0, 6.0, ((0, 32),), jnp.float32)
    pair_list = draw_pair_list(jax.random.fold_in(keys[10], 71), 0)
    pair_count = draw_pair_count(jax.random.fold_in(keys[10], 71), 0)
    ghost_particle = set_ends(jax.random.randint(keys[4], (GHOSTS,), 0, TILES * TILE), jax.random.fold_in(keys[4], 1), 0, (TILES * TILE) - 1).astype(jnp.int32)
    ghost_owner_keys = jax.random.split(jax.random.fold_in(keys[5], 1), GHOSTS // GHOST_DEV)
    ghost_owner_turns = jax.random.permutation(jax.random.fold_in(keys[5], 3), GHOSTS // GHOST_DEV)
    ghost_owner = jax.vmap(lambda own, number: deal_out(jax.random.fold_in(keys[5], 2), own, number, GHOST_DEV, DEVICES_ALL, 1, CAP, 2))(ghost_owner_keys, ghost_owner_turns).reshape((GHOSTS, 1))
    ghost_cell = set_ends(jax.random.randint(keys[6], (GHOSTS,), 0, SX * NZS), jax.random.fold_in(keys[6], 1), 0, (SX * NZS) - 1).astype(jnp.int32)
    wall_seen = scatter_about(keys[7], (GHOSTS,), 1.0, 6.0, ((0, 32),), jnp.float32)
    solid_temp = scatter_about(keys[8], (DEPTH, NXS, NZS), 1.0, 6.0, ((1, 32),), jnp.float32)
    conduct = jnp.clip(jnp.exp(math.log(0.16) - 1.6739764 * jax.random.uniform(keys[9], (DEPTH, NXS, NZS), jnp.float32) ** steps_of(keys[9], (DEPTH, NXS, NZS), ((1, 32),), -0.2, 0.2)), 0.03, 0.16)
    return dict(positions=positions, particle_temp=particle_temp, pair_list=pair_list, pair_count=pair_count, ghost_particle=ghost_particle, ghost_owner=ghost_owner, ghost_cell=ghost_cell, wall_seen=wall_seen, solid_temp=solid_temp, conduct=conduct)


heat_rate = 0.004
wall_heat = 0.5


def tile_heat(own_pos, own_temp, near_pos, near_temp, pairs, live_count, blocks):
    all_pos = jnp.concatenate([own_pos, near_pos], axis=1)
    all_temp = jnp.concatenate([own_temp, near_temp], axis=0)
    block_rows = 16

    def pair_block(number, accrued):
        pair_rows = lax.dynamic_slice_in_dim(pairs, number * block_rows, block_rows, 0)
        first_tile = pair_rows[:, 0]
        second_tile = pair_rows[:, 1]
        live_rows = (number * block_rows + jnp.arange(block_rows, dtype=jnp.int32)) < live_count
        left_pos = all_pos[:, first_tile, :]
        right_pos = all_pos[:, second_tile, :]
        distance = jnp.zeros((block_rows, left_pos.shape[2], right_pos.shape[2]), jnp.float32)
        for component in range(3):
            offset = left_pos[component][:, :, None] - right_pos[component][:, None, :]
            distance = distance + offset * offset
        kernel = jnp.square(jnp.maximum(0.0, 1.0 - distance))
        gained = jnp.sum(kernel * (all_temp[second_tile][:, None, :] - all_temp[first_tile][:, :, None]), axis=2)
        gained = jnp.where(live_rows[:, None], gained, 0.0)
        return accrued.at[first_tile].add(gained)

    accrued = lax.fori_loop(0, blocks, pair_block, jnp.zeros(own_temp.shape, jnp.float32))
    return own_temp + heat_rate * accrued


def solid_step(padded, coef, source):
    center = padded[1:-1, 1:-1, 1:-1]
    beside = padded[2:, 1:-1, 1:-1] + padded[:-2, 1:-1, 1:-1]
    beside = beside + padded[1:-1, 2:, 1:-1] + padded[1:-1, :-2, 1:-1]
    beside = beside + padded[1:-1, 1:-1, 2:] + padded[1:-1, 1:-1, :-2]
    result = center + coef * (beside - 6.0 * center)
    return result.at[0].add(source)


def reference(positions, particle_temp, pair_list, pair_count, ghost_particle, ghost_owner, ghost_cell, wall_seen, solid_temp, conduct):
    devices = N_FLUID * N_SUB
    per_device = TILES * TILE
    pos_tiles = positions.reshape(3, N_FLUID, N_SUB, TILES, TILE)
    temp_tiles = particle_temp.reshape(N_FLUID, N_SUB, TILES, TILE)
    near_pos = jnp.roll(pos_tiles, -1, axis=2)
    near_temp = jnp.roll(temp_tiles, -1, axis=1)
    own_pos = jnp.moveaxis(pos_tiles.reshape(3, devices, TILES, TILE), 1, 0)
    near_pos = jnp.moveaxis(near_pos.reshape(3, devices, TILES, TILE), 1, 0)
    own_temp = temp_tiles.reshape(devices, TILES, TILE)
    near_temp = near_temp.reshape(devices, TILES, TILE)
    pairs = pair_list.reshape(devices, PAIRS, 2)

    def one_device(items):
        return tile_heat(items[0], items[1], items[2], items[3], items[4], items[5], PAIRS // 16)

    heated = lax.map(one_device, (own_pos, own_temp, near_pos, near_temp, pairs, pair_count))
    particle_out = heated.reshape(-1)
    owner = ghost_owner[:, 0]
    source_index = ghost_particle + (jnp.arange(GHOSTS, dtype=jnp.int32) // GHOST_DEV) * per_device
    flux = wall_heat * (particle_out[source_index] - wall_seen)
    wall_index = owner * (SX * NZS) + ghost_cell
    surface = jnp.zeros((NXS * NZS,), jnp.float32).at[wall_index].add(flux).reshape(NXS, NZS)
    source = surface / SUBSTEPS
    temp = solid_temp
    for turn in range(SUBSTEPS):
        temp = solid_step(jnp.pad(temp, 1), conduct, source)
    ghost_temp = temp[0].reshape(-1)[wall_index]
    return particle_out, temp, ghost_temp
```

```python
import functools

import jax
import jax.numpy as jnp
from jax import lax
from jax.experimental import pallas as pl
from jax.experimental.pallas import tpu as pltpu
from jax.sharding import PartitionSpec as P

TILE = 128
SUBSTEPS = 6
LANES = 128
SUB = 8
WIDTH = 2
AXES = ("fluid", "sub")
MIB = 1 << 20

heat_rate = 0.004
wall_heat = 0.5

f32 = jnp.float32
bf16 = jnp.bfloat16
i32 = jnp.int32


def params(mib):
    return pltpu.CompilerParams(vmem_limit_bytes=mib * MIB)


def cost(flops, moved):
    return pl.CostEstimate(flops=int(flops), bytes_accessed=int(moved), transcendentals=0)


def vmem():
    return pl.BlockSpec(memory_space=pltpu.VMEM)


def hbm():
    return pl.BlockSpec(memory_space=pl.ANY)


def parts_of(value, count):
    parts = []
    for _ in range(count):
        part = value.astype(bf16).astype(f32)
        parts.append(part)
        value = value - part
    return parts


def dot(left, right):
    return lax.dot_general(left, right, (((1,), (0,)), ((), ())), preferred_element_type=f32)


def dot_lanes(left, right):
    return lax.dot_general(left, right, (((1,), (1,)), ((), ())), preferred_element_type=f32)


def sublane_is(row, count):
    return lax.broadcasted_iota(i32, (count, row.shape[1]), 0) == row


def z_sum(cur, lane_first, lane_last, sub_first, sub_last):
    left, right = cur[:, :LANES], cur[:, LANES:]
    left_up, right_up = pltpu.roll(left, 1, 1), pltpu.roll(right, 1, 1)
    left_down, right_down = pltpu.roll(left, LANES - 1, 1), pltpu.roll(right, LANES - 1, 1)
    carry_up = jnp.where(sub_first, 0.0, pltpu.roll(right_up, 1, 0))
    carry_down = jnp.where(sub_last, 0.0, pltpu.roll(left_down, SUB - 1, 0))
    first = jnp.where(lane_first, carry_up, left_up) + jnp.where(lane_last, right_down, left_down)
    second = jnp.where(lane_first, left_up, right_up) + jnp.where(lane_last, carry_down, right_down)
    return jnp.concatenate([first, second], axis=1)


def masks():
    lane = lax.broadcasted_iota(i32, (SUB, LANES), 1)
    sub = lax.broadcasted_iota(i32, (SUB, LANES), 0)
    return lane == 0, lane == LANES - 1, sub == 0, sub == SUB - 1


def row_step(src, coef, row, coef_row, depth, emit):
    marks = masks()
    before, cur = None, src[row, 0]
    for layer in range(depth):
        after = src[row, layer + 1] if layer + 1 < depth else None
        total = src[row - 1, layer] + src[row + 1, layer] + z_sum(cur, *marks)
        if before is not None:
            total = total + before
        if after is not None:
            total = total + after
        emit(layer, cur + coef[coef_row, layer] * (total - 6.0 * cur))
        before, cur = cur, after


def spread_kernel(width, extra, x_rows, layers, temp_ref, coef_ref, temp_out, coef_out, low_out, high_out):
    step = pl.program_id(0)
    depth = layers * pl.num_programs(0)
    per_layer = temp_ref.shape[0] // layers
    per_half = per_layer * SUB // x_rows
    halves = temp_out.shape[3] // LANES

    def taken(ref, layer, row):
        start = layer * per_layer + (row // SUB) * per_half + row % SUB
        found = [ref[pl.ds(start + half * SUB, SUB, stride=SUB * halves), :] for half in range(halves)]
        return jnp.concatenate(found, axis=1)

    for layer in range(layers):
        at = step * layers + layer
        for row in range(x_rows):
            temp = taken(temp_ref, layer, row)
            coef = taken(coef_ref, layer, row)
            temp_out[row, layer] = temp
            coef_out[row, layer] = coef
            far = x_rows - 1 - row
            if row < width:
                low_out[row * depth + at] = temp
            if far < width:
                high_out[(width - 1 - far) * depth + at] = temp
            if row < width - 1:
                low_out[(width + row) * depth + at] = coef
            if far < width - 1:
                high_out[(width + width - 2 - far) * depth + at] = coef
            deep = SUBSTEPS - width
            base = (2 * width - 1) * depth
            if extra and width - 1 <= row < SUBSTEPS - 2:

                @pl.when(at < deep)
                def _():
                    low_out[base + (row - width + 1) * deep + at] = coef

            if extra and width - 1 <= far < SUBSTEPS - 2:

                @pl.when(at < deep)
                def _():
                    high_out[base + (SUBSTEPS - 3 - far) * deep + at] = coef


def spread(temp, coef, width):
    depth, x_rows, span = temp.shape

    def rows_of(value):
        value = value.reshape(depth, x_rows // SUB, SUB, span // LANES, LANES)
        return value.transpose(0, 1, 3, 2, 4).reshape(-1, LANES)

    layers = 4
    per_layer = x_rows * span // LANES
    deep = SUBSTEPS - width
    extra = max(0, SUBSTEPS - 1 - width)
    tiles = (2 * width - 1) * depth + extra * deep
    lanes = span // SUB
    form = jax.ShapeDtypeStruct((x_rows, depth, SUB, lanes), f32)
    face = jax.ShapeDtypeStruct((tiles, SUB, lanes), f32)
    rows = pl.BlockSpec((layers * per_layer, LANES), lambda i: (i, 0))
    slab = pl.BlockSpec((x_rows, layers, SUB, lanes), lambda i: (0, i, 0, 0))
    whole = pl.BlockSpec((tiles, SUB, lanes), lambda i: (0, 0, 0))
    return pl.pallas_call(
        functools.partial(spread_kernel, width, extra, x_rows, layers),
        grid=(depth // layers,),
        in_specs=[rows, rows],
        out_specs=[slab, slab, whole, whole],
        out_shape=[form, form, face, face],
        compiler_params=params(24),
        cost_estimate=cost(1e6, 20 * MIB),
        name="spread",
    )(rows_of(temp), rows_of(coef))


def load_window(width, depth, x_rows, temp, low, high, coef, low_c, high_c, buf, cbuf, sem, csem):
    for row in range(width):
        pltpu.make_async_copy(low.at[pl.ds(row * depth, depth)], buf.at[row], sem.at[row]).start()
    for row in range(width - 1):
        start = (width + row) * depth
        pltpu.make_async_copy(low_c.at[pl.ds(start, depth)], cbuf.at[row], csem.at[row]).start()

    @pl.loop(0, x_rows)
    def _(row):
        pltpu.make_async_copy(temp.at[row], buf.at[row + width], sem.at[row + width]).start()
        pltpu.make_async_copy(coef.at[row], cbuf.at[row + width - 1], csem.at[row + width - 1]).start()

    for row in range(width):
        at = x_rows + width + row
        pltpu.make_async_copy(high.at[pl.ds(row * depth, depth)], buf.at[at], sem.at[at]).start()
    for row in range(width - 1):
        at = x_rows + width - 1 + row
        start = (width + row) * depth
        pltpu.make_async_copy(high_c.at[pl.ds(start, depth)], cbuf.at[at], csem.at[at]).start()


def early_steps(width, depth, x_rows, temp, coef, first, second, cbuf, sem, csem, last):
    def arrived(row):
        pltpu.make_async_copy(temp.at[0], first.at[row], sem.at[row]).wait()

    arrived(0)
    arrived(1)
    src, dst = first, second
    for step in range(1, width + 1):

        def one(row, carry, src=src, dst=dst, step=step):
            if step == 1:
                arrived(row + 1)
                pltpu.make_async_copy(coef.at[0], cbuf.at[row - 1], csem.at[row - 1]).wait()
            if step == width:
                last(src, dst, row)
            else:

                def emit(layer, value):
                    dst[row, layer] = value

                row_step(src, cbuf, row, row - 1, depth, emit)
            return carry

        lax.fori_loop(step, x_rows + 2 * width - step, one, 0)
        src, dst = dst, src
    return src


def advance_kernel(
    width, temp, low, high, coef, low_c, high_c, out, low_out, high_out, first, second, cbuf, sem, csem, out_sem
):
    x_rows, depth = temp.shape[:2]
    load_window(width, depth, x_rows, temp, low, high, coef, low_c, high_c, first, cbuf, sem, csem)

    def last(src, dst, row):
        def emit(layer, value):
            dst[row, layer] = value

        row_step(src, cbuf, row, row - 1, depth, emit)
        pltpu.make_async_copy(dst.at[row], out.at[row - width], out_sem.at[row - width]).start()

    end = early_steps(width, depth, x_rows, temp, coef, first, second, cbuf, sem, csem, last)
    for row in range(width):
        for base, ref, slot in ((width, low_out, x_rows), (x_rows, high_out, x_rows + width)):
            pltpu.make_async_copy(
                end.at[base + row], ref.at[pl.ds(row * depth, depth)], out_sem.at[slot + row]
            ).start()
    for row in range(x_rows + 2 * width):
        pltpu.make_async_copy(end.at[0], out.at[0], out_sem.at[row]).wait()


def window_scratch(width, x_rows, depth, lanes):
    return [
        pltpu.VMEM((x_rows + 2 * width, depth, SUB, lanes), f32),
        pltpu.VMEM((x_rows + 2 * width, depth, SUB, lanes), f32),
        pltpu.VMEM((x_rows + 2 * width - 2, depth, SUB, lanes), f32),
        pltpu.SemaphoreType.DMA((x_rows + 2 * width,)),
        pltpu.SemaphoreType.DMA((x_rows + 2 * width - 2,)),
    ]


def advance(temp, low, high, coef, low_c, high_c, width):
    x_rows, depth, _, lanes = temp.shape
    face = jax.ShapeDtypeStruct((width * depth, SUB, lanes), f32)
    return pl.pallas_call(
        functools.partial(advance_kernel, width),
        in_specs=[hbm()] * 6,
        out_specs=[hbm()] * 3,
        out_shape=[jax.ShapeDtypeStruct(temp.shape, f32), face, face],
        scratch_shapes=window_scratch(width, x_rows, depth, lanes)
        + [pltpu.SemaphoreType.DMA((x_rows + 2 * width,))],
        compiler_params=params(24),
        cost_estimate=cost(12 * width * temp.size, 16 * MIB),
        name="advance",
    )(temp, low, high, coef, low_c, high_c)


def finish_kernel(
    width, temp, low, high, coef, low_c, high_c, reply, out, wall, first, second, cbuf, staged, sem, csem, out_sem
):
    x_rows, depth = temp.shape[:2]
    halves = temp.shape[3] // LANES
    load_window(width, depth, x_rows, temp, low, high, coef, low_c, high_c, first, cbuf, sem, csem)

    def last(src, dst, row):
        at = row - width
        group, place = lax.div(at, SUB), lax.rem(at, SUB)

        def emit(layer, value):
            if layer < SUBSTEPS:
                value = value + reply[at, layer]
            if layer == 0:
                wall[at] = value
            for half in range(halves):
                staged[layer, group, pl.ds(half * SUB + place, SUB, stride=SUB * halves), :] = value[
                    :, half * LANES : (half + 1) * LANES
                ]

        row_step(src, cbuf, row, row - 1, depth, emit)

        @pl.when(place == SUB - 1)
        def _():
            pltpu.make_async_copy(staged.at[:, group], out.at[:, group], out_sem.at[group]).start()

    early_steps(width, depth, x_rows, temp, coef, first, second, cbuf, sem, csem, last)
    for group in range(x_rows // SUB):
        pltpu.make_async_copy(staged.at[:, 0], out.at[:, 0], out_sem.at[group]).wait()


def finish(temp, low, high, coef, low_c, high_c, reply, width):
    x_rows, depth, _, lanes = temp.shape
    span = lanes * SUB
    groups = x_rows // SUB
    scratch = window_scratch(width, x_rows, depth, lanes)
    form = (depth, groups, span // LANES * SUB, LANES)
    out, wall = pl.pallas_call(
        functools.partial(finish_kernel, width),
        in_specs=[hbm()] * 6 + [vmem()],
        out_specs=[hbm(), vmem()],
        out_shape=[
            jax.ShapeDtypeStruct(form, f32),
            jax.ShapeDtypeStruct((x_rows, SUB, lanes), f32),
        ],
        scratch_shapes=scratch[:3] + [pltpu.VMEM(form, f32)] + scratch[3:] + [pltpu.SemaphoreType.DMA((groups,))],
        compiler_params=params(32),
        cost_estimate=cost(12 * width * temp.size, 16 * MIB),
        name="finish",
    )(temp, low, high, coef, low_c, high_c, reply)
    out = out.reshape(depth, groups, span // LANES, SUB, LANES).transpose(0, 1, 3, 2, 4)
    return out.reshape(depth, x_rows, span), wall


def reply_kernel(width, source, s_low, s_high, coef, low_c, high_c, out, first, second, held, cbuf, sem):
    x_rows, depth = coef.shape[:2]
    far = SUBSTEPS - 1
    deep = SUBSTEPS - width
    copies = [(coef.at[:, pl.ds(0, SUBSTEPS)], cbuf.at[pl.ds(far - 1, x_rows)])]
    for dist in range(1, far):
        for ref, place, is_low in ((low_c, far - 1 - dist, True), (high_c, far - 2 + x_rows + dist, False)):
            if dist < width:
                start = (width + (width - 1 - dist if is_low else dist - 1)) * depth
                count = SUBSTEPS
            else:
                start = (2 * width - 1) * depth + (far - 1 - dist if is_low else dist - width) * deep
                count = deep
            copies.append((ref.at[pl.ds(start, count)], cbuf.at[place, pl.ds(0, count)]))
    started = [pltpu.make_async_copy(a, b, sem.at[i]) for i, (a, b) in enumerate(copies)]
    for copy in started:
        copy.start()
    for row in range(far):
        held[row] = s_low[row]
        held[far + x_rows + row] = s_high[row]
    for row in range(x_rows):
        held[far + row] = source[row]
    for row in range(x_rows + 2 * far):
        first[row, 0] = held[row]
    for copy in started:
        copy.wait()
    src, dst = first, second
    for step in range(2, SUBSTEPS + 1):

        def one(row, carry, src=src, dst=dst, step=step):
            marks = masks()
            before = None
            for layer in range(step):
                scale = cbuf[row - 1, layer]
                if layer == step - 1:
                    value = scale * before
                else:
                    cur = src[row, layer]
                    total = src[row - 1, layer] + src[row + 1, layer] + z_sum(cur, *marks)
                    if before is not None:
                        total = total + before
                    if layer < step - 2:
                        total = total + src[row, layer + 1]
                    value = cur + scale * (total - 6.0 * cur)
                    before = cur
                if layer == 0:
                    value = value + held[row]
                if step == SUBSTEPS:
                    out[row - far, layer] = value
                else:
                    dst[row, layer] = value
            return carry

        lax.fori_loop(step - 1, x_rows + 2 * far - step + 1, one, 0)
        src, dst = dst, src


def reply_of(source, s_low, s_high, coef, low_c, high_c, width):
    x_rows, depth, _, lanes = coef.shape
    far = SUBSTEPS - 1
    return pl.pallas_call(
        functools.partial(reply_kernel, width),
        in_specs=[vmem()] * 3 + [hbm()] * 3,
        out_specs=vmem(),
        out_shape=jax.ShapeDtypeStruct((x_rows, SUBSTEPS, SUB, lanes), f32),
        scratch_shapes=[
            pltpu.VMEM((x_rows + 2 * far, SUBSTEPS, SUB, lanes), f32),
            pltpu.VMEM((x_rows + 2 * far, SUBSTEPS, SUB, lanes), f32),
            pltpu.VMEM((x_rows + 2 * far, SUB, lanes), f32),
            pltpu.VMEM((x_rows + 2 * far - 2, SUBSTEPS, SUB, lanes), f32),
            pltpu.SemaphoreType.DMA((2 * far - 1,)),
        ],
        compiler_params=params(16),
        cost_estimate=cost(12 * 380 * SUB * lanes, 4 * MIB),
        name="reply",
    )(source, s_low, s_high, coef, low_c, high_c)


def rank_kernel(devices, owner_ref, rank_ref):
    ghosts = owner_ref.shape[1]
    block = 256
    before = lax.broadcasted_iota(i32, (block, block), 0) < lax.broadcasted_iota(i32, (block, block), 1)
    ramp = before.astype(f32).astype(bf16)
    carried = jnp.zeros((devices, 1), f32)
    for start in range(0, ghosts, block):
        named = sublane_is(owner_ref[:, start : start + block], devices)
        ones = named.astype(f32)
        counted = dot(ones.astype(bf16), ramp) + carried
        rank = jnp.sum(jnp.where(named, counted, 0.0), axis=0, keepdims=True)
        rank_ref[:, start : start + block] = rank.astype(i32)
        carried = carried + jnp.sum(ones, axis=1, keepdims=True)


def rank_of(owner, devices):
    return pl.pallas_call(
        functools.partial(rank_kernel, devices),
        in_specs=[vmem()],
        out_specs=vmem(),
        out_shape=jax.ShapeDtypeStruct(owner.shape, i32),
        compiler_params=params(16),
        cost_estimate=cost(4e6, 1e5),
        name="rank",
    )(owner)


def heat_kernel(
    devices, slots, pairs, live, own, near, particle, owner, rank, cell, seen, out, send, rows, cols, total
):
    tiles = own.shape[1]
    comps = 5
    for side, ref in enumerate((own, near)):
        x, y, z, temp = ref[0], ref[1], ref[2], ref[3]
        square = x * x + y * y + z * z
        lead = (2.0 * x, 2.0 * y, 2.0 * z, -square, temp) if side else (x, y, z, 1.0 - square, temp)
        right = (2.0 * x, 2.0 * y, 2.0 * z, -square, temp)
        for tile in range(tiles):
            for comp in range(comps):
                rows[side * tiles + tile, comp : comp + 1, :] = right[comp][tile : tile + 1, :]
        if side == 0:
            for comp in range(comps):
                turned = jnp.transpose(lead[comp])
                for tile in range(tiles):
                    cols[tile, comp] = jnp.broadcast_to(turned[:, tile : tile + 1], (TILE, TILE))

    @pl.loop(0, tiles)
    def _(tile):
        total[tile] = jnp.zeros((TILE, TILE), f32)

    def pair(number, carry):
        first, second = pairs[2 * number], pairs[2 * number + 1]
        near_rows = rows[second]
        x, y, z, square, temp = [near_rows[comp : comp + 1, :] for comp in range(comps)]
        for part in range(TILE // SUB):
            at = pl.ds(part * SUB, SUB)
            inside = (cols[first, 3, at, :] + square) + cols[first, 0, at, :] * x
            inside = inside + cols[first, 1, at, :] * y + cols[first, 2, at, :] * z
            inside = jnp.maximum(inside, 0.0)
            gained = (inside * inside) * (temp - cols[first, 4, at, :])
            total[first, at, :] += gained
        return carry

    lax.fori_loop(0, live[0], pair, 0)

    ones = jnp.ones((SUB, TILE), bf16)
    for tile in range(tiles):
        gained = jnp.zeros((SUB, TILE), f32)
        for part in parts_of(total[tile], 3):
            gained = gained + dot_lanes(ones, part.astype(bf16))
        out[tile : tile + 1, :] = own[3, tile : tile + 1, :] + heat_rate * gained[0:1, :]

    pieces = [part.astype(bf16) for part in parts_of(jnp.transpose(out[...]), 3)]
    table = jnp.concatenate(pieces, axis=1)
    ghosts = particle.shape[1]
    packed = [jnp.zeros((2 * devices, slots), f32) for _ in range(3)]
    block = 512
    for start in range(0, ghosts, block):
        at = slice(start, start + block)
        mirrored = particle[:, at]
        high = sublane_is(mirrored // TILE, tiles).astype(f32).astype(bf16)
        picked = dot(table, jnp.concatenate([high] * 3, axis=0))
        low = sublane_is(mirrored % TILE, TILE)
        value = jnp.sum(jnp.where(low, picked, 0.0), axis=0, keepdims=True)
        flux = wall_heat * (value - seen[:, at])
        cells = cell[:, at]
        cell_parts = [((cells // 256) * 256).astype(f32), (cells % 256).astype(f32), jnp.zeros_like(flux)]
        line = lax.broadcasted_iota(i32, (2 * devices, block), 0)
        named = line // 2 == owner[:, at]
        is_cell = line % 2 == 1
        slot = sublane_is(rank[:, at], slots).astype(f32).astype(bf16)
        for number, part in enumerate(parts_of(flux, 3)):
            chosen = jnp.where(named, jnp.where(is_cell, cell_parts[number], part), 0.0)
            packed[number] = packed[number] + dot_lanes(chosen.astype(bf16), slot)
    send[...] = packed[0] + packed[1] + packed[2]


def heat(pairs, live, own, near, particle, owner, rank, cell, seen, devices, slots):
    tiles = own.shape[1]
    smem = pl.BlockSpec(memory_space=pltpu.SMEM)
    return pl.pallas_call(
        functools.partial(heat_kernel, devices, slots),
        in_specs=[smem, smem] + [vmem()] * 7,
        out_specs=[vmem(), vmem()],
        out_shape=[
            jax.ShapeDtypeStruct((tiles, TILE), f32),
            jax.ShapeDtypeStruct((2 * devices, slots), f32),
        ],
        scratch_shapes=[
            pltpu.VMEM((2 * tiles, SUB, TILE), f32),
            pltpu.VMEM((tiles, 5, TILE, TILE), f32),
            pltpu.VMEM((tiles, TILE, TILE), f32),
        ],
        compiler_params=params(24),
        cost_estimate=cost(12 * 4.2e6, 1 * MIB),
        name="heat",
    )(pairs, live, own, near, particle, owner, rank, cell, seen)


def surface_kernel(received, out):
    devices = received.shape[0] // 2
    high_count, low_count = out.shape
    total = jnp.zeros((2 * high_count, low_count), f32)
    for device in range(devices):
        flux = received[2 * device : 2 * device + 1, :]
        cells = received[2 * device + 1 : 2 * device + 2, :].astype(i32)
        high = sublane_is(cells // low_count, high_count)
        low = sublane_is(cells % low_count, low_count).astype(f32).astype(bf16)
        chosen = [jnp.where(high, part, 0.0).astype(bf16) for part in parts_of(flux, 2)]
        total = total + dot_lanes(jnp.concatenate(chosen, axis=0), low)
    out[...] = (total[:high_count] + total[high_count:]) * (1.0 / SUBSTEPS)


def surface_of(received, high_count, low_count):
    return pl.pallas_call(
        surface_kernel,
        in_specs=[vmem()],
        out_specs=vmem(),
        out_shape=jax.ShapeDtypeStruct((high_count, low_count), f32),
        compiler_params=params(16),
        cost_estimate=cost(6e7, 2e5),
        name="surface",
    )(received)


def wall_kernel(received, wall, out):
    devices = received.shape[0] // 2
    high_count, low_count = wall.shape
    pieces = [part.astype(bf16) for part in parts_of(jnp.transpose(wall[...]), 2)]
    table = jnp.concatenate(pieces, axis=1)
    for device in range(devices):
        cells = received[2 * device + 1 : 2 * device + 2, :].astype(i32)
        high = sublane_is(cells // low_count, high_count).astype(f32).astype(bf16)
        picked = dot(table, jnp.concatenate([high, high], axis=0))
        low = sublane_is(cells % low_count, low_count)
        out[device : device + 1, :] = jnp.sum(jnp.where(low, picked, 0.0), axis=0, keepdims=True)


def wall_of(received, wall):
    return pl.pallas_call(
        wall_kernel,
        in_specs=[vmem()] * 2,
        out_specs=vmem(),
        out_shape=jax.ShapeDtypeStruct((received.shape[0] // 2, received.shape[1]), f32),
        compiler_params=params(16),
        cost_estimate=cost(6e7, 2e5),
        name="wall",
    )(received, wall)


def back_kernel(returned, owner, rank, out):
    devices, slots = returned.shape
    pieces = [part.astype(bf16) for part in parts_of(jnp.transpose(returned[...]), 3)]
    table = jnp.concatenate(pieces, axis=1)
    block = 512
    for start in range(0, owner.shape[1], block):
        at = slice(start, start + block)
        named = sublane_is(owner[:, at], devices).astype(f32).astype(bf16)
        picked = dot(table, jnp.concatenate([named] * 3, axis=0))
        slot = sublane_is(rank[:, at], slots)
        out[:, at] = jnp.sum(jnp.where(slot, picked, 0.0), axis=0, keepdims=True)


def back_of(returned, owner, rank):
    return pl.pallas_call(
        back_kernel,
        in_specs=[vmem()] * 3,
        out_specs=vmem(),
        out_shape=jax.ShapeDtypeStruct(owner.shape, f32),
        compiler_params=params(16),
        cost_estimate=cost(6e6, 1e5),
        name="back",
    )(returned, owner, rank)


def between(low_face, high_face):
    count = lax.axis_size(AXES)
    upward = [(i, i + 1) for i in range(count - 1)]
    downward = [(target, source) for source, target in upward]
    return lax.ppermute(high_face, AXES, upward), lax.ppermute(low_face, AXES, downward)


def on_device(
    positions,
    particle_temp,
    pair_list,
    pair_count,
    ghost_particle,
    ghost_owner,
    ghost_cell,
    wall_seen,
    solid_temp,
    conduct,
):
    width = WIDTH
    depth, x_rows, span = solid_temp.shape
    tiles = positions.shape[1] // TILE
    devices = lax.axis_size(AXES)
    ghosts = ghost_cell.shape[0]
    slots = max(2, 2 * ghosts // devices)
    sub_count = lax.axis_size("sub")

    own = jnp.concatenate([positions, particle_temp[None, :]], axis=0).reshape(4, tiles, TILE)
    near = lax.ppermute(own, "sub", [(i, (i - 1) % sub_count) for i in range(sub_count)])

    temp, coef, low_face, high_face = spread(solid_temp, conduct, width)
    low_c, high_c = between(low_face, high_face)

    owner = ghost_owner.reshape(1, ghosts)
    rank = rank_of(owner, devices)
    particle_out, send = heat(
        pair_list.reshape(-1),
        pair_count,
        own,
        near,
        ghost_particle.reshape(1, ghosts),
        owner,
        rank,
        ghost_cell.reshape(1, ghosts),
        wall_seen.reshape(1, ghosts),
        devices,
        slots,
    )
    received = lax.all_to_all(
        send.reshape(devices, 2 * slots), AXES, split_axis=0, concat_axis=0, tiled=True
    ).reshape(2 * devices, slots)
    lanes = span // SUB
    source = surface_of(received, x_rows * SUB, lanes).reshape(x_rows, SUB, lanes)
    far = SUBSTEPS - 1
    s_low, s_high = between(source[:far], source[x_rows - far :])
    reply = reply_of(source, s_low, s_high, coef, low_c, high_c, width)

    low, high = low_c, high_c
    for _ in range(SUBSTEPS // width - 1):
        temp, low_face, high_face = advance(temp, low, high, coef, low_c, high_c, width)
        low, high = between(low_face, high_face)
    solid_out, wall = finish(temp, low, high, coef, low_c, high_c, reply, width)

    answer = wall_of(received, wall.reshape(x_rows * SUB, lanes))
    returned = lax.all_to_all(answer, AXES, split_axis=0, concat_axis=0, tiled=True)
    ghost_temp = back_of(returned, owner, rank)
    return (particle_out.reshape(-1), solid_out, ghost_temp.reshape(-1))


def solution(mesh):
    placed = (
        P(None, AXES),
        P(AXES),
        P(AXES, None),
        P(AXES),
        P(AXES),
        P(AXES, None),
        P(AXES),
        P(AXES),
        P(None, AXES, None),
        P(None, AXES, None),
    )
    return jax.shard_map(
        on_device,
        mesh=mesh,
        in_specs=placed,
        out_specs=(P(AXES), P(None, AXES, None), P(AXES)),
        check_vma=False,
    )
```

```python
import functools

import jax
import jax.numpy as jnp
from jax import lax
from jax.experimental import pallas as pl
from jax.experimental.pallas import tpu as pltpu
from jax.sharding import PartitionSpec as P

TILE = 128
SUBSTEPS = 6
LANES = 128
SUB = 8
WIDTH = 2
AXES = ("fluid", "sub")
MIB = 1 << 20

heat_rate = 0.004
wall_heat = 0.5

f32 = jnp.float32
bf16 = jnp.bfloat16
i32 = jnp.int32


def params(mib):
    return pltpu.CompilerParams(vmem_limit_bytes=mib * MIB)


def cost(flops, moved):
    return pl.CostEstimate(flops=int(flops), bytes_accessed=int(moved), transcendentals=0)


def vmem():
    return pl.BlockSpec(memory_space=pltpu.VMEM)


def hbm():
    return pl.BlockSpec(memory_space=pl.ANY)


def parts_of(value, count):
    parts = []
    for _ in range(count):
        part = value.astype(bf16).astype(f32)
        parts.append(part)
        value = value - part
    return parts


def dot(left, right):
    return lax.dot_general(left, right, (((1,), (0,)), ((), ())), preferred_element_type=f32)


def dot_lanes(left, right):
    return lax.dot_general(left, right, (((1,), (1,)), ((), ())), preferred_element_type=f32)


def sublane_is(row, count):
    return lax.broadcasted_iota(i32, (count, row.shape[1]), 0) == row


def z_sum(cur, lane_first, lane_last, sub_first, sub_last):
    left, right = cur[:, :LANES], cur[:, LANES:]
    left_up, right_up = pltpu.roll(left, 1, 1), pltpu.roll(right, 1, 1)
    left_down, right_down = pltpu.roll(left, LANES - 1, 1), pltpu.roll(right, LANES - 1, 1)
    carry_up = jnp.where(sub_first, 0.0, pltpu.roll(right_up, 1, 0))
    carry_down = jnp.where(sub_last, 0.0, pltpu.roll(left_down, SUB - 1, 0))
    first = jnp.where(lane_first, carry_up, left_up) + jnp.where(lane_last, right_down, left_down)
    second = jnp.where(lane_first, left_up, right_up) + jnp.where(lane_last, carry_down, right_down)
    return jnp.concatenate([first, second], axis=1)


def masks():
    lane = lax.broadcasted_iota(i32, (SUB, LANES), 1)
    sub = lax.broadcasted_iota(i32, (SUB, LANES), 0)
    return lane == 0, lane == LANES - 1, sub == 0, sub == SUB - 1


class Rows:
    def __init__(self, depth, *pieces):
        self.depth = depth
        self.pieces = pieces

    def find(self, row):
        for piece in self.pieces:
            if piece[0] <= row < piece[1]:
                return piece
        return None

    def tile(self, piece, row, layer):
        start, _, ref, base = piece
        if base is None:
            return ref[row - start, layer]
        return ref[base + (row - start) * self.depth + layer]


def sweep(temp, coef, start, stop, emit):
    def one(row, above, here, below, scale):
        marks = masks()
        depth = temp.depth
        before, cur = None, temp.tile(here, row, 0)
        for layer in range(depth):
            after = temp.tile(here, row, layer + 1) if layer + 1 < depth else None
            total = temp.tile(above, row - 1, layer) + temp.tile(below, row + 1, layer) + z_sum(cur, *marks)
            if before is not None:
                total = total + before
            if after is not None:
                total = total + after
            emit(row, layer, cur + coef.tile(scale, row, layer) * (total - 6.0 * cur))
            before, cur = cur, after

    row = start
    while row < stop:
        found = (temp.find(row - 1), temp.find(row), temp.find(row + 1), coef.find(row))
        end = row + 1
        while end < stop and found == (temp.find(end - 1), temp.find(end), temp.find(end + 1), coef.find(end)):
            end += 1
        if end - row > 1:

            def body(at, carry, found=found):
                one(at, *found)
                return carry

            lax.fori_loop(row, end, body, 0)
        else:
            one(row, *found)
        row = end


def several(temp, coef, width, start, stop, mids, emit):
    for step in range(1, width):
        first, last = start - (width - step), stop + (width - step)
        mid = mids[(step - 1) % len(mids)]

        def keep(row, layer, value, mid=mid, first=first):
            mid[row - first, layer] = value

        sweep(temp, coef, first, last, keep)
        temp = Rows(temp.depth, (first, last, mid, None))
    sweep(temp, coef, start, stop, emit)


def mids_for(width, rows, depth, lanes):
    return [pltpu.VMEM((max(rows, 1), depth, SUB, lanes), f32) for _ in range(min(2, width - 1))]


class Face:
    def __init__(self, width, depth):
        self.coef = width * depth
        at = (2 * width - 1) * depth
        self.temp_cone, self.coef_cone = {}, {}
        for dist in range(width + 1, SUBSTEPS + 1):
            self.temp_cone[dist] = at
            at += SUBSTEPS + 1 - dist
        for dist in range(width, SUBSTEPS):
            self.coef_cone[dist] = at
            at += SUBSTEPS - dist
        self.tiles = at


def spread_kernel(width, depth, layers, temp_ref, coef_ref, _, temp_out, coef_out, low_out, high_out):
    step = pl.program_id(0)
    x_rows = temp_out.shape[0]
    face = Face(width, depth)
    per_layer = temp_ref.shape[0] // layers
    per_half = per_layer * SUB // x_rows
    halves = temp_out.shape[3] // LANES

    def taken(ref, layer, row):
        start = layer * per_layer + (row // SUB) * per_half + row % SUB
        found = [ref[pl.ds(start + half * SUB, SUB, stride=SUB * halves), :] for half in range(halves)]
        return jnp.concatenate(found, axis=1)

    def put(ref, place, value, at, count):
        @pl.when(at < count)
        def _():
            ref[place + at] = value

    for layer in range(layers):
        at = step * layers + layer
        for row in range(x_rows):
            temp = taken(temp_ref, layer, row)
            coef = taken(coef_ref, layer, row)
            temp_out[row, layer] = temp
            coef_out[row, layer] = coef
            for ref, dist, upward in ((low_out, row + 1, False), (high_out, x_rows - row, True)):
                if dist <= width:
                    place = width - dist if upward else dist - 1
                    ref[place * depth + at] = temp
                elif dist <= SUBSTEPS:
                    put(ref, face.temp_cone[dist], temp, at, SUBSTEPS + 1 - dist)
                if dist < width:
                    place = width - 1 - dist if upward else dist - 1
                    ref[face.coef + place * depth + at] = coef
                elif dist < SUBSTEPS:
                    put(ref, face.coef_cone[dist], coef, at, SUBSTEPS - dist)


def spread(temp, coef, after, width):
    depth, x_rows, span = temp.shape

    def rows_of(value):
        value = value.reshape(depth, x_rows // SUB, SUB, span // LANES, LANES)
        return value.transpose(0, 1, 3, 2, 4).reshape(-1, LANES)

    layers = 4
    per_layer = x_rows * span // LANES
    tiles = Face(width, depth).tiles
    lanes = span // SUB
    form = jax.ShapeDtypeStruct((x_rows, depth, SUB, lanes), f32)
    face = jax.ShapeDtypeStruct((tiles, SUB, lanes), f32)
    rows = pl.BlockSpec((layers * per_layer, LANES), lambda i: (i, 0))
    slab = pl.BlockSpec((x_rows, layers, SUB, lanes), lambda i: (0, i, 0, 0))
    whole = pl.BlockSpec((tiles, SUB, lanes), lambda i: (0, 0, 0))
    return pl.pallas_call(
        functools.partial(spread_kernel, width, depth, layers),
        grid=(depth // layers,),
        in_specs=[rows, rows, hbm()],
        out_specs=[slab, slab, whole, whole],
        out_shape=[form, form, face, face],
        compiler_params=params(24),
        cost_estimate=cost(1e6, 20 * MIB),
        name="spread",
    )(rows_of(temp), rows_of(coef), after)


def plate_rows(refs, x_rows, depth, width):
    if len(refs) == 1:
        return [(0, x_rows, refs[0], None)]
    low, inner, high = refs
    return [(0, width, low, 0), (width, x_rows - width, inner, None), (x_rows - width, x_rows, high, 0)]


def coef_rows(coef, low_c, high_c, width):
    x_rows, depth = coef.shape[:2]
    base = Face(width, depth).coef
    return Rows(
        depth,
        (1 - width, 0, low_c, base),
        (0, x_rows, coef, None),
        (x_rows, x_rows + width - 1, high_c, base),
    )


def edge_kernel(width, owned, with_source, *refs):
    own, refs = refs[:owned], refs[owned:]
    low, high, coef, low_c, high_c = refs[:5]
    refs = refs[5:]
    x_rows, depth = coef.shape[:2]
    if with_source:
        source, refs = refs[0], refs[1:]
    low_out, high_out = refs[:2]
    mids = refs[2:]
    temp = Rows(
        depth,
        (-width, 0, low, 0),
        *plate_rows(own, x_rows, depth, width),
        (x_rows, x_rows + width, high, 0),
    )
    scale = coef_rows(coef, low_c, high_c, width)
    for out, start in ((low_out, 0), (high_out, x_rows - width)):

        def emit(row, layer, value, out=out, start=start):
            out[(row - start) * depth + layer] = value

        several(temp, scale, width, start, start + width, mids, emit)
    if with_source:
        for row in range(SUBSTEPS - 1):
            low_out[width * depth + row] = source[row]
            high_out[width * depth + row] = source[x_rows - (SUBSTEPS - 1) + row]


def edge(own, low, high, coef, low_c, high_c, width, source=None):
    x_rows, depth, _, lanes = coef.shape
    extra = [] if source is None else [source]
    tiles = width * depth + (SUBSTEPS - 1 if extra else 0)
    face = jax.ShapeDtypeStruct((tiles, SUB, lanes), f32)
    operands = [*own, low, high, coef, low_c, high_c, *extra]
    return pl.pallas_call(
        functools.partial(edge_kernel, width, len(own), bool(extra)),
        in_specs=[vmem()] * len(operands),
        out_specs=[vmem()] * 2,
        out_shape=[face, face],
        scratch_shapes=mids_for(width, 3 * width - 2, depth, lanes),
        compiler_params=params(16),
        cost_estimate=cost(12 * 12 * depth * SUB * lanes, 4 * MIB),
        name="edge",
    )(*operands)


def inner_kernel(width, owned, *refs):
    own, (coef, out), mids = refs[:owned], refs[owned : owned + 2], refs[owned + 2 :]
    x_rows, depth = coef.shape[:2]
    temp = Rows(depth, *plate_rows(own, x_rows, depth, width))
    scale = Rows(depth, (0, x_rows, coef, None))

    def emit(row, layer, value):
        out[row - width, layer] = value

    several(temp, scale, width, width, x_rows - width, mids, emit)


def inner(own, coef, width):
    x_rows, depth, _, lanes = coef.shape
    operands = [*own, coef]
    return pl.pallas_call(
        functools.partial(inner_kernel, width, len(own)),
        in_specs=[vmem()] * len(operands),
        out_specs=vmem(),
        out_shape=jax.ShapeDtypeStruct((x_rows - 2 * width, depth, SUB, lanes), f32),
        scratch_shapes=mids_for(width, x_rows - 2, depth, lanes),
        compiler_params=params(16),
        cost_estimate=cost(12 * 26 * depth * SUB * lanes, 12 * MIB),
        name="inner",
    )(*operands)


def finish_kernel(width, owned, *refs):
    own, refs = refs[:owned], refs[owned:]
    low, high, coef, low_c, high_c, reply, _, out, staged, out_sem = refs[:10]
    mids = refs[10:]
    x_rows, depth = coef.shape[:2]
    halves = coef.shape[3] // LANES
    temp = Rows(
        depth,
        (-width, 0, low, 0),
        *plate_rows(own, x_rows, depth, width),
        (x_rows, x_rows + width, high, 0),
    )

    def emit(row, layer, value):
        if layer < SUBSTEPS:
            value = value + reply[row, layer]
        group, place = row // SUB, row % SUB
        for half in range(halves):
            staged[layer, group, pl.ds(half * SUB + place, SUB, stride=SUB * halves), :] = value[
                :, half * LANES : (half + 1) * LANES
            ]

    several(temp, coef_rows(coef, low_c, high_c, width), width, 0, x_rows, mids, emit)
    copy = pltpu.make_async_copy(staged, out, out_sem)
    copy.start()
    copy.wait()


def finish(own, low, high, coef, low_c, high_c, reply, after, width):
    x_rows, depth, _, lanes = coef.shape
    span = lanes * SUB
    groups = x_rows // SUB
    form = (depth, groups, span // LANES * SUB, LANES)
    operands = [*own, low, high, coef, low_c, high_c, reply]
    out = pl.pallas_call(
        functools.partial(finish_kernel, width, len(own)),
        in_specs=[vmem()] * len(operands) + [hbm()],
        out_specs=hbm(),
        out_shape=jax.ShapeDtypeStruct(form, f32),
        scratch_shapes=[pltpu.VMEM(form, f32), pltpu.SemaphoreType.DMA]
        + mids_for(width, x_rows + 2 * width - 2, depth, lanes),
        compiler_params=params(24),
        cost_estimate=cost(12 * 34 * depth * SUB * lanes, 16 * MIB),
        name="finish",
    )(*operands, after)
    out = out.reshape(depth, groups, span // LANES, SUB, LANES).transpose(0, 1, 3, 2, 4)
    return out.reshape(depth, x_rows, span)


def grouped(start, stop, size, body):
    full = (stop - start) // size

    def several_rows(number, carry):
        for step in range(size):
            body(start + number * size + step)
        return carry

    if full > 1:
        lax.fori_loop(0, full, several_rows, 0)
        start += full * size
    for row in range(start, stop):
        body(row)


def cone_step(src, scale, row, coef_row, layers, deepest, emit):
    marks = masks()
    before = None
    for layer in range(layers):
        factor = scale[coef_row, layer]
        if layer >= deepest:
            emit(layer, factor * before)
            continue
        cur = src[row, layer]
        total = src[row - 1, layer] + src[row + 1, layer] + z_sum(cur, *marks)
        if before is not None:
            total = total + before
        if layer + 1 < deepest:
            total = total + src[row, layer + 1]
        emit(layer, cur + factor * (total - 6.0 * cur))
        before = cur


def cone_kernel(width, temp, coef, low_c, high_c, wall, scale, first, second):
    x_rows, depth = temp.shape[:2]
    face = Face(width, depth)
    reach = SUBSTEPS

    @pl.loop(0, x_rows)
    def _(row):
        for layer in range(SUBSTEPS + 1):
            first[row + reach, layer] = temp[row, layer]
        for layer in range(SUBSTEPS):
            scale[row + reach - 1, layer] = coef[row, layer]

    for dist in range(1, reach + 1):
        for ref, upward, at in ((low_c, True, reach - dist), (high_c, False, x_rows + reach - 1 + dist)):
            place = (width - dist if upward else dist - 1) * depth if dist <= width else face.temp_cone[dist]
            for layer in range(reach + 1 - dist):
                first[at, layer] = ref[place + layer]
            if dist == reach:
                continue
            place = (
                face.coef + (width - 1 - dist if upward else dist - 1) * depth
                if dist < width
                else face.coef_cone[dist]
            )
            for layer in range(reach - dist):
                scale[at - 1, layer] = ref[place + layer]

    src, dst = first, second
    for step in range(1, SUBSTEPS + 1):

        def one(row, dist=0, src=src, dst=dst, step=step):
            def emit(layer, value):
                if step == SUBSTEPS:
                    wall[row - reach] = value
                else:
                    dst[row, layer] = value

            cone_step(src, scale, row, row - 1, SUBSTEPS + 1 - step - dist, depth, emit)

        grouped(reach, reach + x_rows, 4, one)
        for dist in range(1, SUBSTEPS + 1 - step):
            one(reach - dist, dist)
            one(reach + x_rows - 1 + dist, dist)
        src, dst = dst, src


def cone_of(temp, coef, low_c, high_c, width):
    x_rows, depth, _, lanes = coef.shape
    long = x_rows + 2 * SUBSTEPS
    return pl.pallas_call(
        functools.partial(cone_kernel, width),
        in_specs=[vmem()] * 4,
        out_specs=[vmem()] * 2,
        out_shape=[
            jax.ShapeDtypeStruct((x_rows, SUB, lanes), f32),
            jax.ShapeDtypeStruct((long - 2, SUBSTEPS, SUB, lanes), f32),
        ],
        scratch_shapes=[pltpu.VMEM((long, SUBSTEPS + 1, SUB, lanes), f32)] * 2,
        compiler_params=params(16),
        cost_estimate=cost(12 * 406 * SUB * lanes, 4 * MIB),
        name="cone",
    )(temp, coef, low_c, high_c)


def reply_kernel(base, source, low, high, scale, cone, _, out, wall, first, second, held):
    x_rows = source.shape[0]
    far = SUBSTEPS - 1
    for row in range(far):
        held[row] = low[base + row]
        held[far + x_rows + row] = high[base + row]
    for row in range(x_rows):
        held[far + row] = source[row]
    for row in range(x_rows + 2 * far):
        first[row, 0] = held[row]
    src, dst = first, second
    for step in range(2, SUBSTEPS + 1):

        def one(row, src=src, dst=dst, step=step):
            def emit(layer, value):
                if layer == 0:
                    value = value + held[row]
                if step < SUBSTEPS:
                    dst[row, layer] = value
                    return
                out[row - far, layer] = value
                if layer == 0:
                    wall[row - far] = value + cone[row - far]

            cone_step(src, scale, row, row, step, step - 1, emit)

        grouped(step - 1, x_rows + 2 * far - step + 1, 4, one)
        src, dst = dst, src


def reply_of(source, low, high, scale, cone, after, base):
    x_rows, _, lanes = source.shape
    far = SUBSTEPS - 1
    return pl.pallas_call(
        functools.partial(reply_kernel, base),
        in_specs=[vmem()] * 5 + [hbm()],
        out_specs=[vmem()] * 2,
        out_shape=[
            jax.ShapeDtypeStruct((x_rows, SUBSTEPS, SUB, lanes), f32),
            jax.ShapeDtypeStruct((x_rows, SUB, lanes), f32),
        ],
        scratch_shapes=[
            pltpu.VMEM((x_rows + 2 * far, SUBSTEPS, SUB, lanes), f32),
            pltpu.VMEM((x_rows + 2 * far, SUBSTEPS, SUB, lanes), f32),
            pltpu.VMEM((x_rows + 2 * far, SUB, lanes), f32),
        ],
        compiler_params=params(16),
        cost_estimate=cost(12 * 380 * SUB * lanes, 4 * MIB),
        name="reply",
    )(source, low, high, scale, cone, after)


def pack_kernel(devices, positions, temps, owner_ref, own_ref, rank_ref):
    for tile in range(own_ref.shape[1]):
        at = slice(tile * TILE, (tile + 1) * TILE)
        for comp in range(3):
            own_ref[comp, tile : tile + 1, :] = positions[comp : comp + 1, at]
        own_ref[3, tile : tile + 1, :] = temps[:, at]

    ghosts = owner_ref.shape[1]
    block = 256
    before = lax.broadcasted_iota(i32, (block, block), 0) < lax.broadcasted_iota(i32, (block, block), 1)
    ramp = before.astype(f32).astype(bf16)
    carried = jnp.zeros((devices, 1), f32)
    for start in range(0, ghosts, block):
        named = sublane_is(owner_ref[:, start : start + block], devices)
        ones = named.astype(f32)
        counted = dot(ones.astype(bf16), ramp) + carried
        rank = jnp.sum(jnp.where(named, counted, 0.0), axis=0, keepdims=True)
        rank_ref[:, start : start + block] = rank.astype(i32)
        carried = carried + jnp.sum(ones, axis=1, keepdims=True)


def pack(positions, temps, owner, devices):
    return pl.pallas_call(
        functools.partial(pack_kernel, devices),
        in_specs=[vmem()] * 3,
        out_specs=[vmem()] * 2,
        out_shape=[
            jax.ShapeDtypeStruct((4, positions.shape[1] // TILE, TILE), f32),
            jax.ShapeDtypeStruct(owner.shape, i32),
        ],
        compiler_params=params(16),
        cost_estimate=cost(4e6, 1e5),
        name="pack",
    )(positions, temps, owner)


def heat_kernel(
    devices, slots, pairs, live, own, near, particle, owner, rank, cell, seen, out, send, rows, cols, total
):
    tiles = own.shape[1]
    comps = 5
    for side, ref in enumerate((own, near)):
        x, y, z, temp = ref[0], ref[1], ref[2], ref[3]
        square = x * x + y * y + z * z
        lead = (2.0 * x, 2.0 * y, 2.0 * z, -square, temp) if side else (x, y, z, 1.0 - square, temp)
        right = (2.0 * x, 2.0 * y, 2.0 * z, -square, temp)
        for tile in range(tiles):
            for comp in range(comps):
                rows[side * tiles + tile, comp : comp + 1, :] = right[comp][tile : tile + 1, :]
        if side == 0:
            for comp in range(comps):
                turned = jnp.transpose(lead[comp])
                for tile in range(tiles):
                    cols[tile, comp] = jnp.broadcast_to(turned[:, tile : tile + 1], (TILE, TILE))

    @pl.loop(0, tiles)
    def _(tile):
        total[tile] = jnp.zeros((TILE, TILE), f32)

    def pair(number, carry):
        first, second = pairs[0, number], pairs[1, number]
        near_rows = rows[second]
        x, y, z, square, temp = [near_rows[comp : comp + 1, :] for comp in range(comps)]
        for part in range(TILE // SUB):
            at = pl.ds(part * SUB, SUB)
            inside = (cols[first, 3, at, :] + square) + cols[first, 0, at, :] * x
            inside = inside + cols[first, 1, at, :] * y + cols[first, 2, at, :] * z
            inside = jnp.maximum(inside, 0.0)
            gained = (inside * inside) * (temp - cols[first, 4, at, :])
            total[first, at, :] += gained
        return carry

    lax.fori_loop(0, live[0], pair, 0)

    ones = jnp.ones((SUB, TILE), bf16)
    for tile in range(tiles):
        gained = jnp.zeros((SUB, TILE), f32)
        for part in parts_of(total[tile], 3):
            gained = gained + dot_lanes(ones, part.astype(bf16))
        out[tile : tile + 1, :] = own[3, tile : tile + 1, :] + heat_rate * gained[0:1, :]

    pieces = [part.astype(bf16) for part in parts_of(jnp.transpose(out[...]), 3)]
    table = jnp.concatenate(pieces, axis=1)
    ghosts = particle.shape[1]
    packed = [jnp.zeros((2 * devices, slots), f32) for _ in range(3)]
    block = 512
    for start in range(0, ghosts, block):
        at = slice(start, start + block)
        mirrored = particle[:, at]
        high = sublane_is(mirrored // TILE, tiles).astype(f32).astype(bf16)
        picked = dot(table, jnp.concatenate([high] * 3, axis=0))
        low = sublane_is(mirrored % TILE, TILE)
        value = jnp.sum(jnp.where(low, picked, 0.0), axis=0, keepdims=True)
        flux = wall_heat * (value - seen[:, at])
        cells = cell[:, at]
        cell_parts = [((cells // 256) * 256).astype(f32), (cells % 256).astype(f32), jnp.zeros_like(flux)]
        line = lax.broadcasted_iota(i32, (2 * devices, block), 0)
        named = line // 2 == owner[:, at]
        is_cell = line % 2 == 1
        slot = sublane_is(rank[:, at], slots).astype(f32).astype(bf16)
        for number, part in enumerate(parts_of(flux, 3)):
            chosen = jnp.where(named, jnp.where(is_cell, cell_parts[number], part), 0.0)
            packed[number] = packed[number] + dot_lanes(chosen.astype(bf16), slot)
    send[...] = packed[0] + packed[1] + packed[2]


def heat(pairs, live, own, near, particle, owner, rank, cell, seen, devices, slots):
    tiles = own.shape[1]
    smem = pl.BlockSpec(memory_space=pltpu.SMEM)
    return pl.pallas_call(
        functools.partial(heat_kernel, devices, slots),
        in_specs=[smem, smem] + [vmem()] * 7,
        out_specs=[vmem(), vmem()],
        out_shape=[
            jax.ShapeDtypeStruct((tiles, TILE), f32),
            jax.ShapeDtypeStruct((2 * devices, slots), f32),
        ],
        scratch_shapes=[
            pltpu.VMEM((2 * tiles, SUB, TILE), f32),
            pltpu.VMEM((tiles, 5, TILE, TILE), f32),
            pltpu.VMEM((tiles, TILE, TILE), f32),
        ],
        compiler_params=params(24),
        cost_estimate=cost(12 * 4.2e6, 1 * MIB),
        name="heat",
    )(pairs, live, own, near, particle, owner, rank, cell, seen)


def surface_kernel(received, out):
    devices = received.shape[0] // 2
    high_count, low_count = out.shape
    total = jnp.zeros((2 * high_count, low_count), f32)
    for device in range(devices):
        flux = received[2 * device : 2 * device + 1, :]
        cells = received[2 * device + 1 : 2 * device + 2, :].astype(i32)
        high = sublane_is(cells // low_count, high_count)
        low = sublane_is(cells % low_count, low_count).astype(f32).astype(bf16)
        chosen = [jnp.where(high, part, 0.0).astype(bf16) for part in parts_of(flux, 2)]
        total = total + dot_lanes(jnp.concatenate(chosen, axis=0), low)
    out[...] = (total[:high_count] + total[high_count:]) * (1.0 / SUBSTEPS)


def surface_of(received, high_count, low_count):
    return pl.pallas_call(
        surface_kernel,
        in_specs=[vmem()],
        out_specs=vmem(),
        out_shape=jax.ShapeDtypeStruct((high_count, low_count), f32),
        compiler_params=params(16),
        cost_estimate=cost(6e7, 2e5),
        name="surface",
    )(received)


def wall_kernel(received, wall, out):
    devices = received.shape[0] // 2
    high_count, low_count = wall.shape
    pieces = [part.astype(bf16) for part in parts_of(jnp.transpose(wall[...]), 2)]
    table = jnp.concatenate(pieces, axis=1)
    for device in range(devices):
        cells = received[2 * device + 1 : 2 * device + 2, :].astype(i32)
        high = sublane_is(cells // low_count, high_count).astype(f32).astype(bf16)
        picked = dot(table, jnp.concatenate([high, high], axis=0))
        low = sublane_is(cells % low_count, low_count)
        out[device : device + 1, :] = jnp.sum(jnp.where(low, picked, 0.0), axis=0, keepdims=True)


def wall_of(received, wall):
    return pl.pallas_call(
        wall_kernel,
        in_specs=[vmem()] * 2,
        out_specs=vmem(),
        out_shape=jax.ShapeDtypeStruct((received.shape[0] // 2, received.shape[1]), f32),
        compiler_params=params(16),
        cost_estimate=cost(6e7, 2e5),
        name="wall",
    )(received, wall)


def back_kernel(returned, owner, rank, out):
    devices, slots = returned.shape
    pieces = [part.astype(bf16) for part in parts_of(jnp.transpose(returned[...]), 3)]
    table = jnp.concatenate(pieces, axis=1)
    block = 512
    for start in range(0, owner.shape[1], block):
        at = slice(start, start + block)
        named = sublane_is(owner[:, at], devices).astype(f32).astype(bf16)
        picked = dot(table, jnp.concatenate([named] * 3, axis=0))
        slot = sublane_is(rank[:, at], slots)
        out[:, at] = jnp.sum(jnp.where(slot, picked, 0.0), axis=0, keepdims=True)


def back_of(returned, owner, rank):
    return pl.pallas_call(
        back_kernel,
        in_specs=[vmem()] * 3,
        out_specs=vmem(),
        out_shape=jax.ShapeDtypeStruct(owner.shape, f32),
        compiler_params=params(16),
        cost_estimate=cost(6e6, 1e5),
        name="back",
    )(returned, owner, rank)


def between(low_face, high_face):
    count = lax.axis_size(AXES)
    upward = [(i, i + 1) for i in range(count - 1)]
    downward = [(target, source) for source, target in upward]
    return lax.ppermute(high_face, AXES, upward), lax.ppermute(low_face, AXES, downward)


def on_device(
    positions,
    particle_temp,
    pair_list,
    pair_count,
    ghost_particle,
    ghost_owner,
    ghost_cell,
    wall_seen,
    solid_temp,
    conduct,
):
    width = WIDTH
    depth, x_rows, span = solid_temp.shape
    particles = positions.shape[1]
    devices = lax.axis_size(AXES)
    ghosts = ghost_cell.shape[0]
    slots = max(2, 2 * ghosts // devices)
    sub_count = lax.axis_size("sub")
    lanes = span // SUB

    owner = ghost_owner.reshape(1, ghosts)
    own, rank = pack(positions, particle_temp.reshape(1, particles), owner, devices)
    near = lax.ppermute(own, "sub", [(i, (i - 1) % sub_count) for i in range(sub_count)])

    temp, coef, low_face, high_face = spread(solid_temp, conduct, near, width)
    low_c, high_c = between(low_face, high_face)

    particle_out, send = heat(
        pair_list.T,
        pair_count,
        own,
        near,
        ghost_particle.reshape(1, ghosts),
        owner,
        rank,
        ghost_cell.reshape(1, ghosts),
        wall_seen.reshape(1, ghosts),
        devices,
        slots,
    )
    received = lax.all_to_all(
        send.reshape(devices, 2 * slots), AXES, split_axis=0, concat_axis=0, tiled=True
    ).reshape(2 * devices, slots)
    source = surface_of(received, x_rows * SUB, lanes).reshape(x_rows, SUB, lanes)

    own_rows, low, high = [temp], low_c, high_c
    rounds = SUBSTEPS // width
    ghost_temp = None
    for turn in range(rounds - 1):
        low_face, high_face = edge(
            own_rows, low, high, coef, low_c, high_c, width, source if turn == 0 else None
        )
        low, high = between(low_face, high_face)
        if turn == 0:
            cone, scale = cone_of(temp, coef, low_c, high_c, width)
            source_low, source_high = low, high
        if turn == min(1, rounds - 2):
            reply, wall = reply_of(source, source_low, source_high, scale, cone, low_face, width * depth)
            answer = wall_of(received, wall.reshape(x_rows * SUB, lanes))
            returned = lax.all_to_all(answer, AXES, split_axis=0, concat_axis=0, tiled=True)
            ghost_temp = back_of(returned, owner, rank)
        own_rows = [low_face, inner(own_rows, coef, width), high_face]
    solid_out = finish(own_rows, low, high, coef, low_c, high_c, reply, ghost_temp, width)
    return (particle_out.reshape(-1), solid_out, ghost_temp.reshape(-1))


def solution(mesh):
    placed = (
        P(None, AXES),
        P(AXES),
        P(AXES, None),
        P(AXES),
        P(AXES),
        P(AXES, None),
        P(AXES),
        P(AXES),
        P(None, AXES, None),
        P(None, AXES, None),
    )
    return jax.shard_map(
        on_device,
        mesh=mesh,
        in_specs=placed,
        out_specs=(P(AXES), P(None, AXES, None), P(AXES)),
        check_vma=False,
    )
```

```python
import functools

import jax
import jax.numpy as jnp
from jax import lax
from jax.experimental import pallas as pl
from jax.experimental.pallas import tpu as pltpu
from jax.sharding import PartitionSpec as P

TILE = 128
SUBSTEPS = 6
LANES = 128
SUB = 8
WIDTH = 2
FEATURES = 32
AXES = ("fluid", "sub")
MIB = 1 << 20

heat_rate = 0.004
wall_heat = 0.5

f32 = jnp.float32
bf16 = jnp.bfloat16
i32 = jnp.int32


def params(mib):
    return pltpu.CompilerParams(vmem_limit_bytes=mib * MIB)


def cost(flops, moved):
    return pl.CostEstimate(flops=int(flops), bytes_accessed=int(moved), transcendentals=0)


def vmem():
    return pl.BlockSpec(memory_space=pltpu.VMEM)


def hbm():
    return pl.BlockSpec(memory_space=pl.ANY)


def parts_of(value, count):
    parts = []
    for _ in range(count):
        part = value.astype(bf16).astype(f32)
        parts.append(part)
        value = value - part
    return parts


def dot(left, right):
    return lax.dot_general(left, right, (((1,), (0,)), ((), ())), preferred_element_type=f32)


def dot_lanes(left, right):
    return lax.dot_general(left, right, (((1,), (1,)), ((), ())), preferred_element_type=f32)


def sublane_is(row, count):
    return lax.broadcasted_iota(i32, (count, row.shape[1]), 0) == row


def z_sum(cur, lane_first, lane_last, sub_first, sub_last):
    left, right = cur[:, :LANES], cur[:, LANES:]
    left_up, right_up = pltpu.roll(left, 1, 1), pltpu.roll(right, 1, 1)
    left_down, right_down = pltpu.roll(left, LANES - 1, 1), pltpu.roll(right, LANES - 1, 1)
    carry_up = jnp.where(sub_first, 0.0, pltpu.roll(right_up, 1, 0))
    carry_down = jnp.where(sub_last, 0.0, pltpu.roll(left_down, SUB - 1, 0))
    first = jnp.where(lane_first, carry_up, left_up) + jnp.where(lane_last, right_down, left_down)
    second = jnp.where(lane_first, left_up, right_up) + jnp.where(lane_last, carry_down, right_down)
    return jnp.concatenate([first, second], axis=1)


def masks():
    lane = lax.broadcasted_iota(i32, (SUB, LANES), 1)
    sub = lax.broadcasted_iota(i32, (SUB, LANES), 0)
    return lane == 0, lane == LANES - 1, sub == 0, sub == SUB - 1


class Rows:
    def __init__(self, depth, *pieces):
        self.depth = depth
        self.pieces = pieces

    def find(self, row):
        for piece in self.pieces:
            if piece[0] <= row < piece[1]:
                return piece
        return None

    def tile(self, piece, row, layer):
        start, _, ref, base = piece
        if base is None:
            return ref[row - start, layer]
        return ref[base + (row - start) * self.depth + layer]


def sweep(temp, coef, start, stop, emit):
    def one(row, above, here, below, scale):
        marks = masks()
        depth = temp.depth
        before, cur = None, temp.tile(here, row, 0)
        for layer in range(depth):
            after = temp.tile(here, row, layer + 1) if layer + 1 < depth else None
            total = temp.tile(above, row - 1, layer) + temp.tile(below, row + 1, layer) + z_sum(cur, *marks)
            if before is not None:
                total = total + before
            if after is not None:
                total = total + after
            emit(row, layer, cur + coef.tile(scale, row, layer) * (total - 6.0 * cur))
            before, cur = cur, after

    row = start
    while row < stop:
        found = (temp.find(row - 1), temp.find(row), temp.find(row + 1), coef.find(row))
        end = row + 1
        while end < stop and found == (temp.find(end - 1), temp.find(end), temp.find(end + 1), coef.find(end)):
            end += 1
        if end - row > 1:

            def body(at, carry, found=found):
                one(at, *found)
                return carry

            lax.fori_loop(row, end, body, 0)
        else:
            one(row, *found)
        row = end


def several(temp, coef, width, start, stop, mids, emit, done=None):
    for step in range(1, width):
        first, last = start - (width - step), stop + (width - step)
        mid = mids[(step - 1) % len(mids)]

        def keep(row, layer, value, mid=mid, first=first):
            mid[row - first, layer] = value

        sweep(temp, coef, first, last, keep)
        temp = Rows(temp.depth, (first, last, mid, None))
    if done is None:
        sweep(temp, coef, start, stop, emit)
        return
    for row in range(start, stop, SUB):
        sweep(temp, coef, row, row + SUB, emit)
        done(row + SUB)


def mids_for(width, rows, depth, lanes):
    return [pltpu.VMEM((max(rows, 1), depth, SUB, lanes), f32) for _ in range(min(2, width - 1))]


class Face:
    def __init__(self, width, depth):
        self.coef = width * depth
        at = (2 * width - 1) * depth
        self.temp_cone, self.coef_cone = {}, {}
        for dist in range(width + 1, SUBSTEPS + 1):
            self.temp_cone[dist] = at
            at += SUBSTEPS + 1 - dist
        for dist in range(width, SUBSTEPS):
            self.coef_cone[dist] = at
            at += SUBSTEPS - dist
        self.tiles = at


def spread_kernel(
    width,
    layers,
    temp_in,
    coef_in,
    _,
    temp_far,
    coef_far,
    low_out,
    high_out,
    temp_buf,
    coef_buf,
    temp_out,
    coef_out,
    sems,
    out_sems,
):
    x_rows, depth = temp_out.shape[:2]
    face = Face(width, depth)
    halves = temp_out.shape[3] // LANES
    per_half = temp_in.shape[1]
    chunks = depth // layers

    def copies(number):
        per_chunk = layers * x_rows // SUB
        at = pl.ds(number * per_chunk, per_chunk)
        return [
            pltpu.make_async_copy(source.at[at], buf.at[at], sems.at[which, number])
            for which, (source, buf) in enumerate(((temp_in, temp_buf), (coef_in, coef_buf)))
        ]

    def results(number):
        at = pl.ds(number * layers, layers)
        return [
            pltpu.make_async_copy(held.at[:, at], out.at[:, at], out_sems.at[which, number])
            for which, (held, out) in enumerate(((temp_out, temp_far), (coef_out, coef_far)))
        ]

    for number in range(chunks):
        for copy in copies(number):
            copy.start()

    def taken(ref, layer, row):
        group = layer * (x_rows // SUB) + row // SUB
        found = [
            ref[group, pl.ds(half * SUB + row % SUB, SUB, stride=SUB * halves), :] for half in range(halves)
        ]
        return jnp.concatenate(found, axis=1)

    def shallow(ref, place, value, layer, count):
        @pl.when(layer < count)
        def _():
            ref[place + layer] = value

    def chunk(number, cone):
        for copy in copies(number):
            copy.wait()
        for step in range(layers):
            layer = number * layers + step
            for row in range(x_rows):
                temp = taken(temp_buf, layer, row)
                coef = taken(coef_buf, layer, row)
                temp_out[row, layer] = temp
                coef_out[row, layer] = coef
                for ref, dist, upward in ((low_out, row + 1, False), (high_out, x_rows - row, True)):
                    if dist <= width:
                        place = width - dist if upward else dist - 1
                        ref[place * depth + layer] = temp
                    elif cone and dist <= SUBSTEPS:
                        shallow(ref, face.temp_cone[dist], temp, layer, SUBSTEPS + 1 - dist)
                    if dist < width:
                        place = width - 1 - dist if upward else dist - 1
                        ref[face.coef + place * depth + layer] = coef
                    elif cone and dist < SUBSTEPS:
                        shallow(ref, face.coef_cone[dist], coef, layer, SUBSTEPS - dist)
        for copy in results(number):
            copy.start()

    shallow_chunks = -(-SUBSTEPS // layers)

    @pl.loop(0, shallow_chunks)
    def _(number):
        chunk(number, True)

    @pl.loop(shallow_chunks, chunks)
    def _(number):
        chunk(number, False)

    for number in range(chunks):
        for copy in results(number):
            copy.wait()


def spread(temp, coef, after, width):
    depth, x_rows, span = temp.shape

    def rows_of(value):
        value = value.reshape(depth, x_rows // SUB, SUB, span // LANES, LANES)
        return value.transpose(0, 1, 3, 2, 4).reshape(depth * x_rows // SUB, span // LANES * SUB, LANES)

    layers = 4
    tiles = Face(width, depth).tiles
    lanes = span // SUB
    form = jax.ShapeDtypeStruct((x_rows, depth, SUB, lanes), f32)
    face = jax.ShapeDtypeStruct((tiles, SUB, lanes), f32)
    raw = pltpu.VMEM((depth * x_rows // SUB, span // LANES * SUB, LANES), f32)
    far = pl.BlockSpec(memory_space=pltpu.HBM)
    return pl.pallas_call(
        functools.partial(spread_kernel, width, layers),
        in_specs=[far, far, hbm()],
        out_specs=[hbm()] * 2 + [vmem()] * 2,
        out_shape=[form, form, face, face],
        scratch_shapes=[raw, raw]
        + [pltpu.VMEM(form.shape, f32)] * 2
        + [pltpu.SemaphoreType.DMA((2, depth // layers))] * 2,
        compiler_params=params(52),
        cost_estimate=cost(1e6, 20 * MIB),
        name="spread",
    )(rows_of(temp), rows_of(coef), after)


def plate_rows(refs, x_rows, depth, width):
    if len(refs) == 1:
        return [(0, x_rows, refs[0], None)]
    low, inner, high = refs
    return [(0, width, low, 0), (width, x_rows - width, inner, None), (x_rows - width, x_rows, high, 0)]


def coef_rows(coef, low_c, high_c, width):
    x_rows, depth = coef.shape[:2]
    base = Face(width, depth).coef
    return Rows(
        depth,
        (1 - width, 0, low_c, base),
        (0, x_rows, coef, None),
        (x_rows, x_rows + width - 1, high_c, base),
    )


def edge_kernel(width, owned, with_source, *refs):
    own, refs = refs[:owned], refs[owned:]
    low, high, coef, low_c, high_c = refs[:5]
    refs = refs[5:]
    x_rows, depth = coef.shape[:2]
    extra, refs = refs[0], refs[1:]
    low_out, high_out = refs[:2]
    mids = refs[2:]
    temp = Rows(
        depth,
        (-width, 0, low, 0),
        *plate_rows(own, x_rows, depth, width),
        (x_rows, x_rows + width, high, 0),
    )
    scale = coef_rows(coef, low_c, high_c, width)
    for out, start in ((low_out, 0), (high_out, x_rows - width)):

        def emit(row, layer, value, out=out, start=start):
            out[(row - start) * depth + layer] = value

        several(temp, scale, width, start, start + width, mids, emit)
    if with_source:
        for row in range(SUBSTEPS - 1):
            low_out[width * depth + row] = extra[row]
            high_out[width * depth + row] = extra[x_rows - (SUBSTEPS - 1) + row]


def edge(own, low, high, coef, low_c, high_c, width, extra, with_source):
    x_rows, depth, _, lanes = coef.shape
    tiles = width * depth + (SUBSTEPS - 1 if with_source else 0)
    face = jax.ShapeDtypeStruct((tiles, SUB, lanes), f32)
    operands = [*own, low, high, coef, low_c, high_c, extra]
    return pl.pallas_call(
        functools.partial(edge_kernel, width, len(own), with_source),
        in_specs=[vmem()] * len(operands),
        out_specs=[vmem()] * 2,
        out_shape=[face, face],
        scratch_shapes=mids_for(width, 3 * width - 2, depth, lanes),
        compiler_params=params(16),
        cost_estimate=cost(12 * 12 * depth * SUB * lanes, 4 * MIB),
        name="edge",
    )(*operands)


def inner_kernel(width, owned, *refs):
    own, (coef, out), mids = refs[:owned], refs[owned : owned + 2], refs[owned + 2 :]
    x_rows, depth = coef.shape[:2]
    temp = Rows(depth, *plate_rows(own, x_rows, depth, width))
    scale = Rows(depth, (0, x_rows, coef, None))

    def emit(row, layer, value):
        out[row - width, layer] = value

    several(temp, scale, width, width, x_rows - width, mids, emit)


def inner(own, coef, width):
    x_rows, depth, _, lanes = coef.shape
    operands = [*own, coef]
    return pl.pallas_call(
        functools.partial(inner_kernel, width, len(own)),
        in_specs=[vmem()] * len(operands),
        out_specs=vmem(),
        out_shape=jax.ShapeDtypeStruct((x_rows - 2 * width, depth, SUB, lanes), f32),
        scratch_shapes=mids_for(width, x_rows - 2, depth, lanes),
        compiler_params=params(16),
        cost_estimate=cost(12 * 26 * depth * SUB * lanes, 12 * MIB),
        name="inner",
    )(*operands)


def finish_kernel(width, owned, *refs):
    own, refs = refs[:owned], refs[owned:]
    low, high, coef, low_c, high_c, reply, out, flag, staged, out_sem = refs[:10]
    mids = refs[10:]
    flag[...] = jnp.zeros(flag.shape, f32)
    x_rows, depth = coef.shape[:2]
    halves = coef.shape[3] // LANES
    temp = Rows(
        depth,
        (-width, 0, low, 0),
        *plate_rows(own, x_rows, depth, width),
        (x_rows, x_rows + width, high, 0),
    )

    def emit(row, layer, value):
        if layer < SUBSTEPS:
            value = value + reply[row, layer]
        group, place = row // SUB, row % SUB
        for half in range(halves):
            staged[layer, group, pl.ds(half * SUB + place, SUB, stride=SUB * halves), :] = value[
                :, half * LANES : (half + 1) * LANES
            ]

    copies = [
        pltpu.make_async_copy(staged.at[:, group], out.at[:, group], out_sem.at[group])
        for group in range(x_rows // SUB)
    ]

    def done(row):
        if row % SUB == 0:
            copies[row // SUB - 1].start()

    several(temp, coef_rows(coef, low_c, high_c, width), width, 0, x_rows, mids, emit, done)
    for copy in copies:
        copy.wait()


def finish(own, low, high, coef, low_c, high_c, reply, width):
    x_rows, depth, _, lanes = coef.shape
    span = lanes * SUB
    groups = x_rows // SUB
    form = (depth, groups, span // LANES * SUB, LANES)
    operands = [*own, low, high, coef, low_c, high_c, reply]
    out, flag = pl.pallas_call(
        functools.partial(finish_kernel, width, len(own)),
        in_specs=[vmem()] * len(operands),
        out_specs=[hbm(), vmem()],
        out_shape=[jax.ShapeDtypeStruct(form, f32), jax.ShapeDtypeStruct((SUB, LANES), f32)],
        scratch_shapes=[pltpu.VMEM(form, f32), pltpu.SemaphoreType.DMA((groups,))]
        + mids_for(width, x_rows + 2 * width - 2, depth, lanes),
        compiler_params=params(24),
        cost_estimate=cost(12 * 34 * depth * SUB * lanes, 16 * MIB),
        name="finish",
    )(*operands)
    out = out.reshape(depth, groups, span // LANES, SUB, LANES).transpose(0, 1, 3, 2, 4)
    return out.reshape(depth, x_rows, span), flag


def grouped(start, stop, size, body):
    full = (stop - start) // size

    def several_rows(number, carry):
        for step in range(size):
            body(start + number * size + step)
        return carry

    if full > 1:
        lax.fori_loop(0, full, several_rows, 0)
        start += full * size
    for row in range(start, stop):
        body(row)


def cone_step(src, scale, row, coef_row, layers, deepest, emit):
    marks = masks()
    before = None
    for layer in range(layers):
        factor = scale[coef_row, layer]
        if layer >= deepest:
            emit(layer, factor * before)
            continue
        cur = src[row, layer]
        total = src[row - 1, layer] + src[row + 1, layer] + z_sum(cur, *marks)
        if before is not None:
            total = total + before
        if layer + 1 < deepest:
            total = total + src[row, layer + 1]
        emit(layer, cur + factor * (total - 6.0 * cur))
        before = cur


def cone_kernel(width, temp, coef, low_c, high_c, wall, scale, first, second):
    x_rows, depth = temp.shape[:2]
    face = Face(width, depth)
    reach = SUBSTEPS

    @pl.loop(0, x_rows)
    def _(row):
        for layer in range(SUBSTEPS + 1):
            first[row + reach, layer] = temp[row, layer]
        for layer in range(SUBSTEPS):
            scale[row + reach - 1, layer] = coef[row, layer]

    for dist in range(1, reach + 1):
        for ref, upward, at in ((low_c, True, reach - dist), (high_c, False, x_rows + reach - 1 + dist)):
            place = (width - dist if upward else dist - 1) * depth if dist <= width else face.temp_cone[dist]
            for layer in range(reach + 1 - dist):
                first[at, layer] = ref[place + layer]
            if dist == reach:
                continue
            place = (
                face.coef + (width - 1 - dist if upward else dist - 1) * depth
                if dist < width
                else face.coef_cone[dist]
            )
            for layer in range(reach - dist):
                scale[at - 1, layer] = ref[place + layer]

    src, dst = first, second
    for step in range(1, SUBSTEPS + 1):

        def one(row, dist=0, src=src, dst=dst, step=step):
            def emit(layer, value):
                if step == SUBSTEPS:
                    wall[row - reach] = value
                else:
                    dst[row, layer] = value

            cone_step(src, scale, row, row - 1, SUBSTEPS + 1 - step - dist, depth, emit)

        grouped(reach, reach + x_rows, 4, one)
        for dist in range(1, SUBSTEPS + 1 - step):
            one(reach - dist, dist)
            one(reach + x_rows - 1 + dist, dist)
        src, dst = dst, src


def cone_of(temp, coef, low_c, high_c, width):
    x_rows, depth, _, lanes = coef.shape
    long = x_rows + 2 * SUBSTEPS
    return pl.pallas_call(
        functools.partial(cone_kernel, width),
        in_specs=[vmem()] * 4,
        out_specs=[vmem()] * 2,
        out_shape=[
            jax.ShapeDtypeStruct((x_rows, SUB, lanes), f32),
            jax.ShapeDtypeStruct((long - 2, SUBSTEPS, SUB, lanes), f32),
        ],
        scratch_shapes=[pltpu.VMEM((long, SUBSTEPS + 1, SUB, lanes), f32)] * 2,
        compiler_params=params(16),
        cost_estimate=cost(12 * 406 * SUB * lanes, 4 * MIB),
        name="cone",
    )(temp, coef, low_c, high_c)


def reply_kernel(base, source, low, high, scale, cone, _, out, wall, first, second, held):
    x_rows = source.shape[0]
    far = SUBSTEPS - 1
    for row in range(far):
        held[row] = low[base + row]
        held[far + x_rows + row] = high[base + row]
    for row in range(x_rows):
        held[far + row] = source[row]
    for row in range(x_rows + 2 * far):
        first[row, 0] = held[row]
    src, dst = first, second
    for step in range(2, SUBSTEPS + 1):

        def one(row, src=src, dst=dst, step=step):
            def emit(layer, value):
                if layer == 0:
                    value = value + held[row]
                if step < SUBSTEPS:
                    dst[row, layer] = value
                    return
                out[row - far, layer] = value
                if layer == 0:
                    wall[row - far] = value + cone[row - far]

            cone_step(src, scale, row, row, step, step - 1, emit)

        grouped(step - 1, x_rows + 2 * far - step + 1, 4, one)
        src, dst = dst, src


def reply_of(source, low, high, scale, cone, after, base):
    x_rows, _, lanes = source.shape
    far = SUBSTEPS - 1
    return pl.pallas_call(
        functools.partial(reply_kernel, base),
        in_specs=[vmem()] * 5 + [hbm()],
        out_specs=[vmem()] * 2,
        out_shape=[
            jax.ShapeDtypeStruct((x_rows, SUBSTEPS, SUB, lanes), f32),
            jax.ShapeDtypeStruct((x_rows, SUB, lanes), f32),
        ],
        scratch_shapes=[
            pltpu.VMEM((x_rows + 2 * far, SUBSTEPS, SUB, lanes), f32),
            pltpu.VMEM((x_rows + 2 * far, SUBSTEPS, SUB, lanes), f32),
            pltpu.VMEM((x_rows + 2 * far, SUB, lanes), f32),
        ],
        compiler_params=params(16),
        cost_estimate=cost(12 * 380 * SUB * lanes, 4 * MIB),
        name="reply",
    )(source, low, high, scale, cone, after)


def pack_kernel(devices, far_pos, far_temps, far_owner, own_ref, rank_ref, positions, temps, owner_ref, sems):
    copies = [
        pltpu.make_async_copy(source, held, sems.at[number])
        for number, (source, held) in enumerate(
            ((far_pos, positions), (far_temps, temps), (far_owner, owner_ref))
        )
    ]
    for copy in copies:
        copy.start()
    for copy in copies:
        copy.wait()
    for tile in range(own_ref.shape[1]):
        at = slice(tile * TILE, (tile + 1) * TILE)
        for comp in range(3):
            own_ref[comp, tile : tile + 1, :] = positions[comp : comp + 1, at]
        own_ref[3, tile : tile + 1, :] = temps[:, at]

    ghosts = owner_ref.shape[1]
    block = 256
    before = lax.broadcasted_iota(i32, (block, block), 0) < lax.broadcasted_iota(i32, (block, block), 1)
    ramp = before.astype(f32).astype(bf16)
    carried = jnp.zeros((devices, 1), f32)
    for start in range(0, ghosts, block):
        named = sublane_is(owner_ref[:, start : start + block], devices)
        ones = named.astype(f32)
        counted = dot(ones.astype(bf16), ramp) + carried
        rank = jnp.sum(jnp.where(named, counted, 0.0), axis=0, keepdims=True)
        rank_ref[:, start : start + block] = rank.astype(i32)
        carried = carried + jnp.sum(ones, axis=1, keepdims=True)


def pack(positions, temps, owner, devices):
    return pl.pallas_call(
        functools.partial(pack_kernel, devices),
        in_specs=[pl.BlockSpec(memory_space=pltpu.HBM)] * 3,
        out_specs=[vmem()] * 2,
        out_shape=[
            jax.ShapeDtypeStruct((4, positions.shape[1] // TILE, TILE), f32),
            jax.ShapeDtypeStruct(owner.shape, i32),
        ],
        scratch_shapes=[
            pltpu.VMEM(positions.shape, f32),
            pltpu.VMEM(temps.shape, f32),
            pltpu.VMEM(owner.shape, i32),
            pltpu.SemaphoreType.DMA((3,)),
        ],
        compiler_params=params(16),
        cost_estimate=cost(4e6, 1e5),
        name="pack",
    )(positions, temps, owner)


def heat_kernel(
    devices,
    slots,
    together,
    pairs,
    live,
    own,
    near,
    particle,
    owner,
    rank,
    cell,
    seen,
    out,
    send,
    left,
    right,
    turned,
    warm,
    total,
):
    tiles = own.shape[1]
    for side, ref in enumerate((own, near)):
        comps = [ref[comp] for comp in range(3)]
        square = comps[0] * comps[0] + comps[1] * comps[1] + comps[2] * comps[2]
        ones = jnp.ones_like(square)
        first, second = [], []
        for comp in comps:
            a, b, c = parts_of(comp, 3)
            first += [a, a, b, b, a, c]
            second += [2.0 * a, 2.0 * b, 2.0 * a, 2.0 * b, 2.0 * c, 2.0 * a]
        first += parts_of(1.0 - square, 3) + [ones] * 3
        second += [ones] * 3 + parts_of(-square, 3)
        blank = [jnp.zeros_like(square)] * (FEATURES - len(first))
        for number, row in enumerate(second + blank):
            right[pl.ds(side * tiles * FEATURES + number, tiles, stride=FEATURES), :] = row
        if side == 0:
            for number, row in enumerate(first + blank):
                left[pl.ds(number, tiles, stride=FEATURES), :] = row
        across = jnp.transpose(ref[3])
        for tile in range(tiles):
            warm[side * tiles + tile] = jnp.broadcast_to(across[:, tile : tile + 1], (TILE, TILE))
    for tile in range(2 * tiles):
        block = right[tile * FEATURES : (tile + 1) * FEATURES, :]
        turned[tile] = jnp.transpose(block).astype(bf16)
    total[...] = jnp.zeros(total.shape, f32)

    def several_pairs(number, carry):
        for step in range(together):
            at = number * together + step
            first, second = pairs[0, at], pairs[1, at]
            features = left[pl.ds(pl.multiple_of(first * FEATURES, FEATURES), FEATURES), :].astype(bf16)
            inside = jnp.maximum(dot(turned[second], features), 0.0)
            gained = (inside * inside) * (warm[second] - own[3, pl.ds(first, 1), :])
            gained = jnp.sum(gained.reshape(TILE // SUB, SUB, TILE), axis=0)
            place = jnp.where(at < live[0], first, tiles)
            total[place] += gained
        return carry

    lax.fori_loop(0, (live[0] + together - 1) // together, several_pairs, 0)
    out[...] = own[3] + heat_rate * jnp.sum(total[:tiles], axis=1)

    pieces = [part.astype(bf16) for part in parts_of(jnp.transpose(out[...]), 3)]
    table = jnp.concatenate(pieces, axis=1)
    ghosts = particle.shape[1]
    packed = [jnp.zeros((2 * devices, slots), f32) for _ in range(3)]
    block = 512
    for start in range(0, ghosts, block):
        at = slice(start, start + block)
        mirrored = particle[:, at]
        high = sublane_is(mirrored // TILE, tiles).astype(f32).astype(bf16)
        picked = dot(table, jnp.concatenate([high] * 3, axis=0))
        low = sublane_is(mirrored % TILE, TILE)
        value = jnp.sum(jnp.where(low, picked, 0.0), axis=0, keepdims=True)
        flux = wall_heat * (value - seen[:, at])
        cells = cell[:, at]
        cell_parts = [((cells // 256) * 256).astype(f32), (cells % 256).astype(f32), jnp.zeros_like(flux)]
        line = lax.broadcasted_iota(i32, (2 * devices, block), 0)
        named = line // 2 == owner[:, at]
        is_cell = line % 2 == 1
        slot = sublane_is(rank[:, at], slots).astype(f32).astype(bf16)
        for number, part in enumerate(parts_of(flux, 3)):
            chosen = jnp.where(named, jnp.where(is_cell, cell_parts[number], part), 0.0)
            packed[number] = packed[number] + dot_lanes(chosen.astype(bf16), slot)
    send[...] = packed[0] + packed[1] + packed[2]


def heat(pairs, live, own, near, particle, owner, rank, cell, seen, devices, slots):
    tiles = own.shape[1]
    together = 4 if pairs.shape[1] % 4 == 0 else 1
    smem = pl.BlockSpec(memory_space=pltpu.SMEM)
    return pl.pallas_call(
        functools.partial(heat_kernel, devices, slots, together),
        in_specs=[smem, smem] + [vmem()] * 7,
        out_specs=[vmem(), vmem()],
        out_shape=[
            jax.ShapeDtypeStruct((tiles, TILE), f32),
            jax.ShapeDtypeStruct((2 * devices, slots), f32),
        ],
        scratch_shapes=[
            pltpu.VMEM((tiles * FEATURES, TILE), f32),
            pltpu.VMEM((2 * tiles * FEATURES, TILE), f32),
            pltpu.VMEM((2 * tiles, TILE, FEATURES), bf16),
            pltpu.VMEM((2 * tiles, TILE, TILE), f32),
            pltpu.VMEM((tiles + 1, SUB, TILE), f32),
        ],
        compiler_params=params(16),
        cost_estimate=cost(12 * 4.2e6, 1 * MIB),
        name="heat",
    )(pairs, live, own, near, particle, owner, rank, cell, seen)


def surface_kernel(received, out):
    devices = received.shape[0] // 2
    high_count, low_count = out.shape
    total = jnp.zeros((2 * high_count, low_count), f32)
    for device in range(devices):
        flux = received[2 * device : 2 * device + 1, :]
        cells = received[2 * device + 1 : 2 * device + 2, :].astype(i32)
        high = sublane_is(cells // low_count, high_count)
        low = sublane_is(cells % low_count, low_count).astype(f32).astype(bf16)
        chosen = [jnp.where(high, part, 0.0).astype(bf16) for part in parts_of(flux, 2)]
        total = total + dot_lanes(jnp.concatenate(chosen, axis=0), low)
    out[...] = (total[:high_count] + total[high_count:]) * (1.0 / SUBSTEPS)


def surface_of(received, high_count, low_count):
    return pl.pallas_call(
        surface_kernel,
        in_specs=[vmem()],
        out_specs=vmem(),
        out_shape=jax.ShapeDtypeStruct((high_count, low_count), f32),
        compiler_params=params(16),
        cost_estimate=cost(6e7, 2e5),
        name="surface",
    )(received)


def wall_kernel(received, wall, out):
    devices = received.shape[0] // 2
    high_count, low_count = wall.shape
    pieces = [part.astype(bf16) for part in parts_of(jnp.transpose(wall[...]), 2)]
    table = jnp.concatenate(pieces, axis=1)
    for device in range(devices):
        cells = received[2 * device + 1 : 2 * device + 2, :].astype(i32)
        high = sublane_is(cells // low_count, high_count).astype(f32).astype(bf16)
        picked = dot(table, jnp.concatenate([high, high], axis=0))
        low = sublane_is(cells % low_count, low_count)
        out[device : device + 1, :] = jnp.sum(jnp.where(low, picked, 0.0), axis=0, keepdims=True)


def wall_of(received, wall):
    return pl.pallas_call(
        wall_kernel,
        in_specs=[vmem()] * 2,
        out_specs=vmem(),
        out_shape=jax.ShapeDtypeStruct((received.shape[0] // 2, received.shape[1]), f32),
        compiler_params=params(16),
        cost_estimate=cost(6e7, 2e5),
        name="wall",
    )(received, wall)


def back_kernel(devices, answers, owner, rank, _, out):
    slots = answers.shape[1]
    me = lax.axis_index(AXES[0]) * lax.axis_size(AXES[1]) + lax.axis_index(AXES[1])
    returned = answers[pl.ds(me, devices, stride=devices), :]
    pieces = [part.astype(bf16) for part in parts_of(jnp.transpose(returned), 3)]
    table = jnp.concatenate(pieces, axis=1)
    block = 512
    for start in range(0, owner.shape[1], block):
        at = slice(start, start + block)
        named = sublane_is(owner[:, at], devices).astype(f32).astype(bf16)
        picked = dot(table, jnp.concatenate([named] * 3, axis=0))
        slot = sublane_is(rank[:, at], slots)
        out[:, at] = jnp.sum(jnp.where(slot, picked, 0.0), axis=0, keepdims=True)


def back_of(answers, owner, rank, after, devices):
    return pl.pallas_call(
        functools.partial(back_kernel, devices),
        in_specs=[vmem()] * 3 + [hbm()],
        out_specs=vmem(),
        out_shape=jax.ShapeDtypeStruct(owner.shape, f32),
        compiler_params=params(16),
        cost_estimate=cost(6e6, 1e5),
        name="back",
    )(answers, owner, rank, after)


def between(low_face, high_face):
    count = lax.axis_size(AXES)
    upward = [(i, i + 1) for i in range(count - 1)]
    downward = [(target, source) for source, target in upward]
    return lax.ppermute(high_face, AXES, upward), lax.ppermute(low_face, AXES, downward)


def on_device(
    positions,
    particle_temp,
    pair_list,
    pair_count,
    ghost_particle,
    ghost_owner,
    ghost_cell,
    wall_seen,
    solid_temp,
    conduct,
):
    width = WIDTH
    depth, x_rows, span = solid_temp.shape
    particles = positions.shape[1]
    devices = lax.axis_size(AXES)
    ghosts = ghost_cell.shape[0]
    slots = max(2, 2 * ghosts // devices)
    sub_count = lax.axis_size("sub")
    lanes = span // SUB

    owner = ghost_owner.reshape(1, ghosts)
    own, rank = pack(positions, particle_temp.reshape(1, particles), owner, devices)
    near = lax.ppermute(own, "sub", [(i, (i - 1) % sub_count) for i in range(sub_count)])

    temp, coef, low_face, high_face = spread(solid_temp, conduct, near, width)
    low_c, high_c = between(low_face, high_face)

    particle_out, send = heat(
        pair_list.T,
        pair_count,
        own,
        near,
        ghost_particle.reshape(1, ghosts),
        owner,
        rank,
        ghost_cell.reshape(1, ghosts),
        wall_seen.reshape(1, ghosts),
        devices,
        slots,
    )
    received = lax.all_to_all(
        send.reshape(devices, 2 * slots), AXES, split_axis=0, concat_axis=0, tiled=True
    ).reshape(2 * devices, slots)
    source = surface_of(received, x_rows * SUB, lanes).reshape(x_rows, SUB, lanes)

    own_rows, low, high = [temp], low_c, high_c
    rounds = SUBSTEPS // width
    for turn in range(rounds - 1):
        low_face, high_face = edge(
            own_rows, low, high, coef, low_c, high_c, width, cone if turn else source, turn == 0
        )
        low, high = between(low_face, high_face)
        if turn == 0:
            cone, scale = cone_of(temp, coef, low_c, high_c, width)
            source_low, source_high = low, high
        if turn == min(1, rounds - 2):
            reply, wall = reply_of(source, source_low, source_high, scale, cone, low_face, width * depth)
            answer = wall_of(received, wall.reshape(x_rows * SUB, lanes))
            answers = lax.all_gather(answer, AXES, axis=0, tiled=True)
        own_rows = [low_face, inner(own_rows, coef, width), high_face]
    solid_out, flag = finish(own_rows, low, high, coef, low_c, high_c, reply, width)
    ghost_temp = back_of(answers, owner, rank, flag, devices)
    return (particle_out.reshape(-1), solid_out, ghost_temp.reshape(-1))


def solution(mesh):
    placed = (
        P(None, AXES),
        P(AXES),
        P(AXES, None),
        P(AXES),
        P(AXES),
        P(AXES, None),
        P(AXES),
        P(AXES),
        P(None, AXES, None),
        P(None, AXES, None),
    )
    return jax.shard_map(
        on_device,
        mesh=mesh,
        in_specs=placed,
        out_specs=(P(AXES), P(None, AXES, None), P(AXES)),
        check_vma=False,
    )
```

```python
import functools

import jax
import jax.numpy as jnp
from jax import lax
from jax.experimental import pallas as pl
from jax.experimental.pallas import tpu as pltpu
from jax.sharding import PartitionSpec as P

TILE = 128
SUBSTEPS = 6
LANES = 128
SUB = 8
WIDTH = 2
FEATURES = 32
AXES = ("fluid", "sub")
MIB = 1 << 20

heat_rate = 0.004
wall_heat = 0.5

f32 = jnp.float32
bf16 = jnp.bfloat16
i32 = jnp.int32


def params(mib):
    return pltpu.CompilerParams(vmem_limit_bytes=mib * MIB)


def cost(flops, moved):
    return pl.CostEstimate(flops=int(flops), bytes_accessed=int(moved), transcendentals=0)


def vmem():
    return pl.BlockSpec(memory_space=pltpu.VMEM)


def hbm():
    return pl.BlockSpec(memory_space=pl.ANY)


def parts_of(value, count):
    parts = []
    for _ in range(count):
        part = value.astype(bf16).astype(f32)
        parts.append(part)
        value = value - part
    return parts


def dot(left, right):
    return lax.dot_general(left, right, (((1,), (0,)), ((), ())), preferred_element_type=f32)


def dot_lanes(left, right):
    return lax.dot_general(left, right, (((1,), (1,)), ((), ())), preferred_element_type=f32)


def sublane_is(row, count):
    return lax.broadcasted_iota(i32, (count, row.shape[1]), 0) == row


def z_sum(cur, lane_first, lane_last, sub_first, sub_last):
    left, right = cur[:, :LANES], cur[:, LANES:]
    left_up, right_up = pltpu.roll(left, 1, 1), pltpu.roll(right, 1, 1)
    left_down, right_down = pltpu.roll(left, LANES - 1, 1), pltpu.roll(right, LANES - 1, 1)
    carry_up = jnp.where(sub_first, 0.0, pltpu.roll(right_up, 1, 0))
    carry_down = jnp.where(sub_last, 0.0, pltpu.roll(left_down, SUB - 1, 0))
    first = jnp.where(lane_first, carry_up, left_up) + jnp.where(lane_last, right_down, left_down)
    second = jnp.where(lane_first, left_up, right_up) + jnp.where(lane_last, carry_down, right_down)
    return jnp.concatenate([first, second], axis=1)


def masks():
    lane = lax.broadcasted_iota(i32, (SUB, LANES), 1)
    sub = lax.broadcasted_iota(i32, (SUB, LANES), 0)
    return lane == 0, lane == LANES - 1, sub == 0, sub == SUB - 1


class Rows:
    def __init__(self, depth, *pieces):
        self.depth = depth
        self.pieces = pieces

    def find(self, row):
        for piece in self.pieces:
            if piece[0] <= row < piece[1]:
                return piece
        return None

    def tile(self, piece, row, layer):
        start, _, ref, base = piece
        if base is None:
            return ref[row - start, layer]
        return ref[base + (row - start) * self.depth + layer]


def sweep(temp, coef, start, stop, emit):
    def one(row, above, here, below, scale):
        marks = masks()
        depth = temp.depth
        before, cur = None, temp.tile(here, row, 0)
        for layer in range(depth):
            after = temp.tile(here, row, layer + 1) if layer + 1 < depth else None
            total = temp.tile(above, row - 1, layer) + temp.tile(below, row + 1, layer) + z_sum(cur, *marks)
            if before is not None:
                total = total + before
            if after is not None:
                total = total + after
            emit(row, layer, cur + coef.tile(scale, row, layer) * (total - 6.0 * cur))
            before, cur = cur, after

    row = start
    while row < stop:
        found = (temp.find(row - 1), temp.find(row), temp.find(row + 1), coef.find(row))
        end = row + 1
        while end < stop and found == (temp.find(end - 1), temp.find(end), temp.find(end + 1), coef.find(end)):
            end += 1
        if end - row > 1:

            def body(at, carry, found=found):
                one(at, *found)
                return carry

            lax.fori_loop(row, end, body, 0)
        else:
            one(row, *found)
        row = end


def several(temp, coef, width, start, stop, mids, emit, done=None):
    for step in range(1, width):
        first, last = start - (width - step), stop + (width - step)
        mid = mids[(step - 1) % len(mids)]

        def keep(row, layer, value, mid=mid, first=first):
            mid[row - first, layer] = value

        sweep(temp, coef, first, last, keep)
        temp = Rows(temp.depth, (first, last, mid, None))
    if done is None:
        sweep(temp, coef, start, stop, emit)
        return
    for row in range(start, stop, SUB):
        sweep(temp, coef, row, row + SUB, emit)
        done(row + SUB)


def mids_for(width, rows, depth, lanes):
    return [pltpu.VMEM((max(rows, 1), depth, SUB, lanes), f32) for _ in range(min(2, width - 1))]


class Face:
    def __init__(self, width, depth):
        self.coef = width * depth
        at = (2 * width - 1) * depth
        self.temp_cone, self.coef_cone = {}, {}
        for dist in range(width + 1, SUBSTEPS + 1):
            self.temp_cone[dist] = at
            at += SUBSTEPS + 1 - dist
        for dist in range(width, SUBSTEPS):
            self.coef_cone[dist] = at
            at += SUBSTEPS - dist
        self.tiles = at


def raw_rows(value):
    depth, x_rows, span = value.shape
    value = value.reshape(depth, x_rows // SUB, SUB, span // LANES, LANES)
    return value.transpose(0, 1, 3, 2, 4).reshape(depth * x_rows // SUB, span // LANES * SUB, LANES)


def chunk_copies(number, layers, groups, pairs, sems):
    at = pl.ds(number * layers * groups, layers * groups)
    return [
        pltpu.make_async_copy(source.at[at], buf.at[at], sems.at[which, number])
        for which, (source, buf) in enumerate(pairs)
    ]


def taken(ref, layer, row, groups):
    halves = ref.shape[1] // (SUB * SUB)
    group = layer * groups + row // SUB
    found = [ref[group, pl.ds(half * SUB + row % SUB, SUB, stride=SUB * halves), :] for half in range(halves)]
    return jnp.concatenate(found, axis=1)


def rim_kernel(width, x_rows, layers, temp_in, coef_in, _, low_out, high_out, temp_buf, coef_buf, sems):
    groups = x_rows // SUB
    depth = temp_in.shape[0] // groups
    face = Face(width, depth)
    chunks = depth // layers
    pairs = ((temp_in, temp_buf), (coef_in, coef_buf))
    for number in range(chunks):
        for copy in chunk_copies(number, layers, groups, pairs, sems):
            copy.start()

    def shallow(ref, place, buf, row, layer, count):
        @pl.when(layer < count)
        def _():
            ref[place + layer] = taken(buf, layer, row, groups)

    def chunk(number, cone):
        for copy in chunk_copies(number, layers, groups, pairs, sems):
            copy.wait()
        for step in range(layers):
            layer = number * layers + step
            for ref, upward in ((low_out, False), (high_out, True)):
                for dist in range(1, SUBSTEPS + 1):
                    row = x_rows - dist if upward else dist - 1
                    if dist <= width:
                        place = width - dist if upward else dist - 1
                        ref[place * depth + layer] = taken(temp_buf, layer, row, groups)
                    elif cone:
                        shallow(ref, face.temp_cone[dist], temp_buf, row, layer, SUBSTEPS + 1 - dist)
                    if dist < width:
                        place = width - 1 - dist if upward else dist - 1
                        ref[face.coef + place * depth + layer] = taken(coef_buf, layer, row, groups)
                    elif cone and dist < SUBSTEPS:
                        shallow(ref, face.coef_cone[dist], coef_buf, row, layer, SUBSTEPS - dist)

    shallow_chunks = -(-SUBSTEPS // layers)

    @pl.loop(0, shallow_chunks)
    def _(number):
        chunk(number, True)

    @pl.loop(shallow_chunks, chunks)
    def _(number):
        chunk(number, False)


def rim(temp, coef, after, width):
    depth, x_rows, span = temp.shape
    layers = 4
    face = jax.ShapeDtypeStruct((Face(width, depth).tiles, SUB, span // SUB), f32)
    raw = pltpu.VMEM((depth * x_rows // SUB, span // LANES * SUB, LANES), f32)
    return pl.pallas_call(
        functools.partial(rim_kernel, width, x_rows, layers),
        in_specs=[hbm()] * 3,
        out_specs=[vmem()] * 2,
        out_shape=[face, face],
        scratch_shapes=[raw, raw, pltpu.SemaphoreType.DMA((2, depth // layers))],
        compiler_params=params(52),
        cost_estimate=cost(1e6, 10 * MIB),
        name="rim",
    )(raw_rows(temp), raw_rows(coef), after)


def spread_kernel(layers, temp_in, coef_in, _, temp_out, coef_out, temp_buf, coef_buf, sems):
    x_rows, depth = temp_out.shape[:2]
    groups = x_rows // SUB
    chunks = depth // layers
    pairs = ((temp_in, temp_buf), (coef_in, coef_buf))
    for number in range(chunks):
        for copy in chunk_copies(number, layers, groups, pairs, sems):
            copy.start()

    @pl.loop(0, chunks)
    def _(number):
        for copy in chunk_copies(number, layers, groups, pairs, sems):
            copy.wait()
        for step in range(layers):
            layer = number * layers + step
            for row in range(x_rows):
                temp_out[row, layer] = taken(temp_buf, layer, row, groups)
                coef_out[row, layer] = taken(coef_buf, layer, row, groups)


def spread(temp, coef, after):
    depth, x_rows, span = temp.shape
    layers = 4
    form = jax.ShapeDtypeStruct((x_rows, depth, SUB, span // SUB), f32)
    raw = pltpu.VMEM((depth * x_rows // SUB, span // LANES * SUB, LANES), f32)
    return pl.pallas_call(
        functools.partial(spread_kernel, layers),
        in_specs=[hbm()] * 3,
        out_specs=[vmem()] * 2,
        out_shape=[form, form],
        scratch_shapes=[raw, raw, pltpu.SemaphoreType.DMA((2, depth // layers))],
        compiler_params=params(44),
        cost_estimate=cost(1e6, 16 * MIB),
        name="spread",
    )(raw_rows(temp), raw_rows(coef), after)


def plate_rows(refs, x_rows, depth, width):
    if len(refs) == 1:
        return [(0, x_rows, refs[0], None)]
    low, inner, high = refs
    return [(0, width, low, 0), (width, x_rows - width, inner, None), (x_rows - width, x_rows, high, 0)]


def coef_rows(coef, low_c, high_c, width):
    x_rows, depth = coef.shape[:2]
    base = Face(width, depth).coef
    return Rows(
        depth,
        (1 - width, 0, low_c, base),
        (0, x_rows, coef, None),
        (x_rows, x_rows + width - 1, high_c, base),
    )


def edge_kernel(width, owned, with_source, *refs):
    own, refs = refs[:owned], refs[owned:]
    low, high, coef, low_c, high_c = refs[:5]
    refs = refs[5:]
    x_rows, depth = coef.shape[:2]
    extra, refs = refs[0], refs[1:]
    low_out, high_out = refs[:2]
    mids = refs[2:]
    temp = Rows(
        depth,
        (-width, 0, low, 0),
        *plate_rows(own, x_rows, depth, width),
        (x_rows, x_rows + width, high, 0),
    )
    scale = coef_rows(coef, low_c, high_c, width)
    for out, start in ((low_out, 0), (high_out, x_rows - width)):

        def emit(row, layer, value, out=out, start=start):
            out[(row - start) * depth + layer] = value

        several(temp, scale, width, start, start + width, mids, emit)
    if with_source:
        for row in range(SUBSTEPS - 1):
            low_out[width * depth + row] = extra[row]
            high_out[width * depth + row] = extra[x_rows - (SUBSTEPS - 1) + row]


def edge(own, low, high, coef, low_c, high_c, width, extra, with_source):
    x_rows, depth, _, lanes = coef.shape
    tiles = width * depth + (SUBSTEPS - 1 if with_source else 0)
    face = jax.ShapeDtypeStruct((tiles, SUB, lanes), f32)
    operands = [*own, low, high, coef, low_c, high_c, extra]
    return pl.pallas_call(
        functools.partial(edge_kernel, width, len(own), with_source),
        in_specs=[vmem()] * len(operands),
        out_specs=[vmem()] * 2,
        out_shape=[face, face],
        scratch_shapes=mids_for(width, 3 * width - 2, depth, lanes),
        compiler_params=params(16),
        cost_estimate=cost(12 * 12 * depth * SUB * lanes, 4 * MIB),
        name="edge",
    )(*operands)


def inner_kernel(width, owned, *refs):
    own, (coef, out), mids = refs[:owned], refs[owned : owned + 2], refs[owned + 2 :]
    x_rows, depth = coef.shape[:2]
    temp = Rows(depth, *plate_rows(own, x_rows, depth, width))
    scale = Rows(depth, (0, x_rows, coef, None))

    def emit(row, layer, value):
        out[row - width, layer] = value

    several(temp, scale, width, width, x_rows - width, mids, emit)


def inner(own, coef, width):
    x_rows, depth, _, lanes = coef.shape
    operands = [*own, coef]
    return pl.pallas_call(
        functools.partial(inner_kernel, width, len(own)),
        in_specs=[vmem()] * len(operands),
        out_specs=vmem(),
        out_shape=jax.ShapeDtypeStruct((x_rows - 2 * width, depth, SUB, lanes), f32),
        scratch_shapes=mids_for(width, x_rows - 2, depth, lanes),
        compiler_params=params(16),
        cost_estimate=cost(12 * 26 * depth * SUB * lanes, 12 * MIB),
        name="inner",
    )(*operands)


def finish_kernel(width, owned, *refs):
    own, refs = refs[:owned], refs[owned:]
    low, high, coef, low_c, high_c, reply, answer, out, answer_out, staged, out_sem = refs[:11]
    mids = refs[11:]
    answer_out[...] = answer[...]
    x_rows, depth = coef.shape[:2]
    halves = coef.shape[3] // LANES
    temp = Rows(
        depth,
        (-width, 0, low, 0),
        *plate_rows(own, x_rows, depth, width),
        (x_rows, x_rows + width, high, 0),
    )

    def emit(row, layer, value):
        if layer < SUBSTEPS:
            value = value + reply[row, layer]
        group, place = row // SUB, row % SUB
        for half in range(halves):
            staged[layer, group, pl.ds(half * SUB + place, SUB, stride=SUB * halves), :] = value[
                :, half * LANES : (half + 1) * LANES
            ]

    copies = [
        pltpu.make_async_copy(staged.at[:, group], out.at[:, group], out_sem.at[group])
        for group in range(x_rows // SUB)
    ]

    def done(row):
        if row % SUB == 0:
            copies[row // SUB - 1].start()

    several(temp, coef_rows(coef, low_c, high_c, width), width, 0, x_rows, mids, emit, done)
    for copy in copies:
        copy.wait()


def finish(own, low, high, coef, low_c, high_c, reply, answer, width):
    x_rows, depth, _, lanes = coef.shape
    span = lanes * SUB
    groups = x_rows // SUB
    form = (depth, groups, span // LANES * SUB, LANES)
    operands = [*own, low, high, coef, low_c, high_c, reply, answer]
    out, answer = pl.pallas_call(
        functools.partial(finish_kernel, width, len(own)),
        in_specs=[vmem()] * len(operands),
        out_specs=[hbm(), vmem()],
        out_shape=[jax.ShapeDtypeStruct(form, f32), jax.ShapeDtypeStruct(answer.shape, f32)],
        scratch_shapes=[pltpu.VMEM(form, f32), pltpu.SemaphoreType.DMA((groups,))]
        + mids_for(width, x_rows + 2 * width - 2, depth, lanes),
        compiler_params=params(24),
        cost_estimate=cost(12 * 34 * depth * SUB * lanes, 16 * MIB),
        name="finish",
    )(*operands)
    out = out.reshape(depth, groups, span // LANES, SUB, LANES).transpose(0, 1, 3, 2, 4)
    return out.reshape(depth, x_rows, span), answer


def grouped(start, stop, size, body):
    full = (stop - start) // size

    def several_rows(number, carry):
        for step in range(size):
            body(start + number * size + step)
        return carry

    if full > 1:
        lax.fori_loop(0, full, several_rows, 0)
        start += full * size
    for row in range(start, stop):
        body(row)


def cone_step(src, scale, row, coef_row, layers, deepest, emit):
    marks = masks()
    before = None
    for layer in range(layers):
        factor = scale[coef_row, layer]
        if layer >= deepest:
            emit(layer, factor * before)
            continue
        cur = src[row, layer]
        total = src[row - 1, layer] + src[row + 1, layer] + z_sum(cur, *marks)
        if before is not None:
            total = total + before
        if layer + 1 < deepest:
            total = total + src[row, layer + 1]
        emit(layer, cur + factor * (total - 6.0 * cur))
        before = cur


def cone_kernel(width, temp, coef, low_c, high_c, wall, scale, first, second):
    x_rows, depth = temp.shape[:2]
    face = Face(width, depth)
    reach = SUBSTEPS

    @pl.loop(0, x_rows)
    def _(row):
        for layer in range(SUBSTEPS + 1):
            first[row + reach, layer] = temp[row, layer]
        for layer in range(SUBSTEPS):
            scale[row + reach - 1, layer] = coef[row, layer]

    for dist in range(1, reach + 1):
        for ref, upward, at in ((low_c, True, reach - dist), (high_c, False, x_rows + reach - 1 + dist)):
            place = (width - dist if upward else dist - 1) * depth if dist <= width else face.temp_cone[dist]
            for layer in range(reach + 1 - dist):
                first[at, layer] = ref[place + layer]
            if dist == reach:
                continue
            place = (
                face.coef + (width - 1 - dist if upward else dist - 1) * depth
                if dist < width
                else face.coef_cone[dist]
            )
            for layer in range(reach - dist):
                scale[at - 1, layer] = ref[place + layer]

    src, dst = first, second
    for step in range(1, SUBSTEPS + 1):

        def one(row, dist=0, src=src, dst=dst, step=step):
            def emit(layer, value):
                if step == SUBSTEPS:
                    wall[row - reach] = value
                else:
                    dst[row, layer] = value

            cone_step(src, scale, row, row - 1, SUBSTEPS + 1 - step - dist, depth, emit)

        grouped(reach, reach + x_rows, 4, one)
        for dist in range(1, SUBSTEPS + 1 - step):
            one(reach - dist, dist)
            one(reach + x_rows - 1 + dist, dist)
        src, dst = dst, src


def cone_of(temp, coef, low_c, high_c, width):
    x_rows, depth, _, lanes = coef.shape
    long = x_rows + 2 * SUBSTEPS
    return pl.pallas_call(
        functools.partial(cone_kernel, width),
        in_specs=[vmem()] * 4,
        out_specs=[vmem()] * 2,
        out_shape=[
            jax.ShapeDtypeStruct((x_rows, SUB, lanes), f32),
            jax.ShapeDtypeStruct((long - 2, SUBSTEPS, SUB, lanes), f32),
        ],
        scratch_shapes=[pltpu.VMEM((long, SUBSTEPS + 1, SUB, lanes), f32)] * 2,
        compiler_params=params(16),
        cost_estimate=cost(12 * 406 * SUB * lanes, 4 * MIB),
        name="cone",
    )(temp, coef, low_c, high_c)


def reply_kernel(base, source, low, high, scale, cone, _, out, wall, first, second, held):
    x_rows = source.shape[0]
    far = SUBSTEPS - 1
    for row in range(far):
        held[row] = low[base + row]
        held[far + x_rows + row] = high[base + row]
    for row in range(x_rows):
        held[far + row] = source[row]
    for row in range(x_rows + 2 * far):
        first[row, 0] = held[row]
    src, dst = first, second
    for step in range(2, SUBSTEPS + 1):

        def one(row, src=src, dst=dst, step=step):
            def emit(layer, value):
                if layer == 0:
                    value = value + held[row]
                if step < SUBSTEPS:
                    dst[row, layer] = value
                    return
                out[row - far, layer] = value
                if layer == 0:
                    wall[row - far] = value + cone[row - far]

            cone_step(src, scale, row, row, step, step - 1, emit)

        grouped(step - 1, x_rows + 2 * far - step + 1, 4, one)
        src, dst = dst, src


def reply_of(source, low, high, scale, cone, after, base):
    x_rows, _, lanes = source.shape
    far = SUBSTEPS - 1
    return pl.pallas_call(
        functools.partial(reply_kernel, base),
        in_specs=[vmem()] * 5 + [hbm()],
        out_specs=[vmem()] * 2,
        out_shape=[
            jax.ShapeDtypeStruct((x_rows, SUBSTEPS, SUB, lanes), f32),
            jax.ShapeDtypeStruct((x_rows, SUB, lanes), f32),
        ],
        scratch_shapes=[
            pltpu.VMEM((x_rows + 2 * far, SUBSTEPS, SUB, lanes), f32),
            pltpu.VMEM((x_rows + 2 * far, SUBSTEPS, SUB, lanes), f32),
            pltpu.VMEM((x_rows + 2 * far, SUB, lanes), f32),
        ],
        compiler_params=params(16),
        cost_estimate=cost(12 * 380 * SUB * lanes, 4 * MIB),
        name="reply",
    )(source, low, high, scale, cone, after)


def pack_kernel(devices, far_pos, far_temps, far_owner, own_ref, rank_ref, positions, temps, owner_ref, sems):
    copies = [
        pltpu.make_async_copy(source, held, sems.at[number])
        for number, (source, held) in enumerate(
            ((far_pos, positions), (far_temps, temps), (far_owner, owner_ref))
        )
    ]
    for copy in copies:
        copy.start()
    for copy in copies:
        copy.wait()
    for tile in range(own_ref.shape[1]):
        at = slice(tile * TILE, (tile + 1) * TILE)
        for comp in range(3):
            own_ref[comp, tile : tile + 1, :] = positions[comp : comp + 1, at]
        own_ref[3, tile : tile + 1, :] = temps[:, at]

    ghosts = owner_ref.shape[1]
    block = 256
    before = lax.broadcasted_iota(i32, (block, block), 0) < lax.broadcasted_iota(i32, (block, block), 1)
    ramp = before.astype(f32).astype(bf16)
    carried = jnp.zeros((devices, 1), f32)
    for start in range(0, ghosts, block):
        named = sublane_is(owner_ref[:, start : start + block], devices)
        ones = named.astype(f32)
        counted = dot(ones.astype(bf16), ramp) + carried
        rank = jnp.sum(jnp.where(named, counted, 0.0), axis=0, keepdims=True)
        rank_ref[:, start : start + block] = rank.astype(i32)
        carried = carried + jnp.sum(ones, axis=1, keepdims=True)


def pack(positions, temps, owner, devices):
    return pl.pallas_call(
        functools.partial(pack_kernel, devices),
        in_specs=[pl.BlockSpec(memory_space=pltpu.HBM)] * 3,
        out_specs=[vmem()] * 2,
        out_shape=[
            jax.ShapeDtypeStruct((4, positions.shape[1] // TILE, TILE), f32),
            jax.ShapeDtypeStruct(owner.shape, i32),
        ],
        scratch_shapes=[
            pltpu.VMEM(positions.shape, f32),
            pltpu.VMEM(temps.shape, f32),
            pltpu.VMEM(owner.shape, i32),
            pltpu.SemaphoreType.DMA((3,)),
        ],
        compiler_params=params(16),
        cost_estimate=cost(4e6, 1e5),
        name="pack",
    )(positions, temps, owner)


def heat_kernel(
    devices,
    slots,
    together,
    pairs,
    live,
    own,
    near,
    particle,
    owner,
    rank,
    cell,
    seen,
    out,
    send,
    plain,
    left,
    right,
    turned,
    warm,
    total,
):
    tiles = own.shape[1]
    for side, ref in enumerate((own, near)):
        comps = [ref[comp] for comp in range(3)]
        square = comps[0] * comps[0] + comps[1] * comps[1] + comps[2] * comps[2]
        ones = jnp.ones_like(square)
        first, second = [], []
        for comp in comps:
            a, b, c = parts_of(comp, 3)
            first += [a, a, b, b, a, c]
            second += [2.0 * a, 2.0 * b, 2.0 * a, 2.0 * b, 2.0 * c, 2.0 * a]
        first += parts_of(1.0 - square, 3) + [ones] * 3
        second += [ones] * 3 + parts_of(-square, 3)
        blank = [jnp.zeros_like(square)] * (FEATURES - len(first))
        for number, row in enumerate(second + blank):
            right[pl.ds(side * tiles * FEATURES + number, tiles, stride=FEATURES), :] = row
        if side == 0:
            for number, row in enumerate(first + blank):
                plain[pl.ds(number, tiles, stride=FEATURES), :] = row
            left[...] = plain[...].astype(bf16)
        across = jnp.transpose(ref[3])
        for tile in range(tiles):
            warm[side * tiles + tile] = jnp.broadcast_to(across[:, tile : tile + 1], (TILE, TILE))
    for tile in range(2 * tiles):
        block = right[tile * FEATURES : (tile + 1) * FEATURES, :]
        turned[tile] = jnp.transpose(block).astype(bf16)
    total[...] = jnp.zeros(total.shape, f32)

    def several_pairs(number, carry):
        found = []
        for step in range(together):
            at = number * together + step
            first, second = pairs[0, at], pairs[1, at]
            features = left[pl.ds(pl.multiple_of(first * FEATURES, FEATURES), FEATURES), :]
            inside = jnp.maximum(dot(turned[second], features), 0.0)
            gained = (inside * inside) * (warm[second] - own[3, pl.ds(first, 1), :])
            gained = jnp.sum(gained.reshape(TILE // SUB, SUB, TILE), axis=0)
            found.append((jnp.where(at < live[0], first, tiles), gained))
        for place, gained in found:
            total[place] += gained
        return carry

    lax.fori_loop(0, (live[0] + together - 1) // together, several_pairs, 0)
    out[...] = own[3] + heat_rate * jnp.sum(total[:tiles], axis=1)

    pieces = [part.astype(bf16) for part in parts_of(jnp.transpose(out[...]), 3)]
    table = jnp.concatenate(pieces, axis=1)
    ghosts = particle.shape[1]
    packed = [jnp.zeros((2 * devices, slots), f32) for _ in range(3)]
    block = 512
    for start in range(0, ghosts, block):
        at = slice(start, start + block)
        mirrored = particle[:, at]
        high = sublane_is(mirrored // TILE, tiles).astype(f32).astype(bf16)
        picked = dot(table, jnp.concatenate([high] * 3, axis=0))
        low = sublane_is(mirrored % TILE, TILE)
        value = jnp.sum(jnp.where(low, picked, 0.0), axis=0, keepdims=True)
        flux = wall_heat * (value - seen[:, at])
        cells = cell[:, at]
        cell_parts = [((cells // 256) * 256).astype(f32), (cells % 256).astype(f32), jnp.zeros_like(flux)]
        line = lax.broadcasted_iota(i32, (2 * devices, block), 0)
        named = line // 2 == owner[:, at]
        is_cell = line % 2 == 1
        slot = sublane_is(rank[:, at], slots).astype(f32).astype(bf16)
        for number, part in enumerate(parts_of(flux, 3)):
            chosen = jnp.where(named, jnp.where(is_cell, cell_parts[number], part), 0.0)
            packed[number] = packed[number] + dot_lanes(chosen.astype(bf16), slot)
    send[...] = packed[0] + packed[1] + packed[2]


def heat(pairs, live, own, near, particle, owner, rank, cell, seen, devices, slots):
    tiles = own.shape[1]
    together = 16 if pairs.shape[1] % 16 == 0 else 1
    smem = pl.BlockSpec(memory_space=pltpu.SMEM)
    return pl.pallas_call(
        functools.partial(heat_kernel, devices, slots, together),
        in_specs=[smem, smem] + [vmem()] * 7,
        out_specs=[vmem(), vmem()],
        out_shape=[
            jax.ShapeDtypeStruct((tiles, TILE), f32),
            jax.ShapeDtypeStruct((2 * devices, slots), f32),
        ],
        scratch_shapes=[
            pltpu.VMEM((tiles * FEATURES, TILE), f32),
            pltpu.VMEM((tiles * FEATURES, TILE), bf16),
            pltpu.VMEM((2 * tiles * FEATURES, TILE), f32),
            pltpu.VMEM((2 * tiles, TILE, FEATURES), bf16),
            pltpu.VMEM((2 * tiles, TILE, TILE), f32),
            pltpu.VMEM((tiles + 1, SUB, TILE), f32),
        ],
        compiler_params=params(16),
        cost_estimate=cost(12 * 4.2e6, 1 * MIB),
        name="heat",
    )(pairs, live, own, near, particle, owner, rank, cell, seen)


def surface_kernel(received, out):
    devices = received.shape[0] // 2
    high_count, low_count = out.shape
    total = jnp.zeros((2 * high_count, low_count), f32)
    for device in range(devices):
        flux = received[2 * device : 2 * device + 1, :]
        cells = received[2 * device + 1 : 2 * device + 2, :].astype(i32)
        high = sublane_is(cells // low_count, high_count)
        low = sublane_is(cells % low_count, low_count).astype(f32).astype(bf16)
        chosen = [jnp.where(high, part, 0.0).astype(bf16) for part in parts_of(flux, 2)]
        total = total + dot_lanes(jnp.concatenate(chosen, axis=0), low)
    out[...] = (total[:high_count] + total[high_count:]) * (1.0 / SUBSTEPS)


def surface_of(received, high_count, low_count):
    return pl.pallas_call(
        surface_kernel,
        in_specs=[vmem()],
        out_specs=vmem(),
        out_shape=jax.ShapeDtypeStruct((high_count, low_count), f32),
        compiler_params=params(16),
        cost_estimate=cost(6e7, 2e5),
        name="surface",
    )(received)


def wall_kernel(received, wall, out):
    devices = received.shape[0] // 2
    high_count, low_count = wall.shape
    pieces = [part.astype(bf16) for part in parts_of(jnp.transpose(wall[...]), 2)]
    table = jnp.concatenate(pieces, axis=1)
    for device in range(devices):
        cells = received[2 * device + 1 : 2 * device + 2, :].astype(i32)
        high = sublane_is(cells // low_count, high_count).astype(f32).astype(bf16)
        picked = dot(table, jnp.concatenate([high, high], axis=0))
        low = sublane_is(cells % low_count, low_count)
        out[device : device + 1, :] = jnp.sum(jnp.where(low, picked, 0.0), axis=0, keepdims=True)


def wall_of(received, wall):
    return pl.pallas_call(
        wall_kernel,
        in_specs=[vmem()] * 2,
        out_specs=vmem(),
        out_shape=jax.ShapeDtypeStruct((received.shape[0] // 2, received.shape[1]), f32),
        compiler_params=params(16),
        cost_estimate=cost(6e7, 2e5),
        name="wall",
    )(received, wall)


def back_kernel(returned, owner, rank, out):
    devices, slots = returned.shape
    pieces = [part.astype(bf16) for part in parts_of(jnp.transpose(returned[...]), 3)]
    table = jnp.concatenate(pieces, axis=1)
    block = 512
    for start in range(0, owner.shape[1], block):
        at = slice(start, start + block)
        named = sublane_is(owner[:, at], devices).astype(f32).astype(bf16)
        picked = dot(table, jnp.concatenate([named] * 3, axis=0))
        slot = sublane_is(rank[:, at], slots)
        out[:, at] = jnp.sum(jnp.where(slot, picked, 0.0), axis=0, keepdims=True)


def back_of(returned, owner, rank):
    return pl.pallas_call(
        back_kernel,
        in_specs=[vmem()] * 3,
        out_specs=vmem(),
        out_shape=jax.ShapeDtypeStruct(owner.shape, f32),
        compiler_params=params(16),
        cost_estimate=cost(6e6, 1e5),
        name="back",
    )(returned, owner, rank)


def between(low_face, high_face):
    count = lax.axis_size(AXES)
    upward = [(i, i + 1) for i in range(count - 1)]
    downward = [(target, source) for source, target in upward]
    return lax.ppermute(high_face, AXES, upward), lax.ppermute(low_face, AXES, downward)


def on_device(
    positions,
    particle_temp,
    pair_list,
    pair_count,
    ghost_particle,
    ghost_owner,
    ghost_cell,
    wall_seen,
    solid_temp,
    conduct,
):
    width = WIDTH
    depth, x_rows, span = solid_temp.shape
    particles = positions.shape[1]
    devices = lax.axis_size(AXES)
    ghosts = ghost_cell.shape[0]
    slots = max(2, 2 * ghosts // devices)
    sub_count = lax.axis_size("sub")
    lanes = span // SUB

    owner = ghost_owner.reshape(1, ghosts)
    own, rank = pack(positions, particle_temp.reshape(1, particles), owner, devices)
    near = lax.ppermute(own, "sub", [(i, (i - 1) % sub_count) for i in range(sub_count)])

    low_face, high_face = rim(solid_temp, conduct, near, width)
    low_c, high_c = between(low_face, high_face)

    particle_out, send = heat(
        pair_list.T,
        pair_count,
        own,
        near,
        ghost_particle.reshape(1, ghosts),
        owner,
        rank,
        ghost_cell.reshape(1, ghosts),
        wall_seen.reshape(1, ghosts),
        devices,
        slots,
    )
    received = lax.all_to_all(
        send.reshape(devices, 2 * slots), AXES, split_axis=0, concat_axis=0, tiled=True
    ).reshape(2 * devices, slots)
    source = surface_of(received, x_rows * SUB, lanes).reshape(x_rows, SUB, lanes)

    temp, coef = spread(solid_temp, conduct, source)
    own_rows, low, high = [temp], low_c, high_c
    rounds = SUBSTEPS // width
    for turn in range(rounds - 1):
        low_face, high_face = edge(
            own_rows, low, high, coef, low_c, high_c, width, cone if turn else source, turn == 0
        )
        low, high = between(low_face, high_face)
        if turn == 0:
            cone, scale = cone_of(temp, coef, low_c, high_c, width)
            source_low, source_high = low, high
        if turn == min(1, rounds - 2):
            reply, wall = reply_of(source, source_low, source_high, scale, cone, low_face, width * depth)
            answer = wall_of(received, wall.reshape(x_rows * SUB, lanes))
        own_rows = [low_face, inner(own_rows, coef, width), high_face]
    solid_out, answer = finish(own_rows, low, high, coef, low_c, high_c, reply, answer, width)
    returned = lax.all_to_all(answer, AXES, split_axis=0, concat_axis=0, tiled=True)
    ghost_temp = back_of(returned, owner, rank)
    return (particle_out.reshape(-1), solid_out, ghost_temp.reshape(-1))


def solution(mesh):
    placed = (
        P(None, AXES),
        P(AXES),
        P(AXES, None),
        P(AXES),
        P(AXES),
        P(AXES, None),
        P(AXES),
        P(AXES),
        P(None, AXES, None),
        P(None, AXES, None),
    )
    return jax.shard_map(
        on_device,
        mesh=mesh,
        in_specs=placed,
        out_specs=(P(AXES), P(None, AXES, None), P(AXES)),
        check_vma=False,
    )
```

```python
import functools

import jax
import jax.numpy as jnp
from jax import lax
from jax.experimental import pallas as pl
from jax.experimental.pallas import tpu as pltpu
from jax.sharding import PartitionSpec as P

TILE = 128
SUBSTEPS = 6
LANES = 128
SUB = 8
WIDTH = 2
FEATURES = 32
TOGETHER = 4
AXES = ("fluid", "sub")
MIB = 1 << 20

heat_rate = 0.004
wall_heat = 0.5

f32 = jnp.float32
bf16 = jnp.bfloat16
i32 = jnp.int32


def params(mib):
    return pltpu.CompilerParams(vmem_limit_bytes=mib * MIB)


def cost(flops, moved):
    return pl.CostEstimate(flops=int(flops), bytes_accessed=int(moved), transcendentals=0)


def vmem():
    return pl.BlockSpec(memory_space=pltpu.VMEM)


def hbm():
    return pl.BlockSpec(memory_space=pl.ANY)


def parts_of(value, count):
    parts = []
    for _ in range(count):
        part = value.astype(bf16).astype(f32)
        parts.append(part)
        value = value - part
    return parts


def dot(left, right):
    return lax.dot_general(left, right, (((1,), (0,)), ((), ())), preferred_element_type=f32)


def dot_lanes(left, right):
    return lax.dot_general(left, right, (((1,), (1,)), ((), ())), preferred_element_type=f32)


def sublane_is(row, count):
    return lax.broadcasted_iota(i32, (count, row.shape[1]), 0) == row


def z_sum(cur, lane_first, lane_last, sub_first, sub_last):
    left, right = cur[:, :LANES], cur[:, LANES:]
    left_up, right_up = pltpu.roll(left, 1, 1), pltpu.roll(right, 1, 1)
    left_down, right_down = pltpu.roll(left, LANES - 1, 1), pltpu.roll(right, LANES - 1, 1)
    carry_up = jnp.where(sub_first, 0.0, pltpu.roll(right_up, 1, 0))
    carry_down = jnp.where(sub_last, 0.0, pltpu.roll(left_down, SUB - 1, 0))
    first = jnp.where(lane_first, carry_up, left_up) + jnp.where(lane_last, right_down, left_down)
    second = jnp.where(lane_first, left_up, right_up) + jnp.where(lane_last, carry_down, right_down)
    return jnp.concatenate([first, second], axis=1)


def masks():
    lane = lax.broadcasted_iota(i32, (SUB, LANES), 1)
    sub = lax.broadcasted_iota(i32, (SUB, LANES), 0)
    return lane == 0, lane == LANES - 1, sub == 0, sub == SUB - 1


class Rows:
    def __init__(self, depth, *pieces):
        self.depth = depth
        self.pieces = pieces
        self.late = {}

    def find(self, row):
        for piece in self.pieces:
            if piece[0] <= row < piece[1]:
                return piece
        return None

    def tile(self, piece, row, layer):
        start, _, ref, base = piece
        if base is None:
            return ref[row - start, layer]
        value = ref[base + (row - start) * self.depth + layer]
        if layer == 0 and isinstance(row, int) and row in self.late:
            value = value + self.late[row]()
        return value


def sweep(temp, coef, source, start, stop, emit):
    depth = temp.depth

    def found_at(row):
        return temp.find(row - 1), temp.find(row), temp.find(row + 1), coef.find(row), source.find(row)

    def group(rows, found):
        marks = masks()
        count = len(rows)
        before = [None] * count
        cur = [temp.tile(found[i][1], rows[i], 0) for i in range(count)]
        for layer in range(depth):
            above = temp.tile(found[0][0], rows[0] - 1, layer)
            below = temp.tile(found[-1][2], rows[-1] + 1, layer)
            after = [None] * count
            if layer + 1 < depth:
                after = [temp.tile(found[i][1], rows[i], layer + 1) for i in range(count)]
            for i in range(count):
                up = above if i == 0 else cur[i - 1]
                down = below if i == count - 1 else cur[i + 1]
                total = up + down + z_sum(cur[i], *marks)
                for other in (before[i], after[i]):
                    if other is not None:
                        total = total + other
                value = cur[i] + coef.tile(found[i][3], rows[i], layer) * (total - 6.0 * cur[i])
                if layer == 0 and found[i][4] is not None:
                    value = value + source.tile(found[i][4], rows[i], 0)
                emit(rows[i], layer, value)
            before, cur = cur, after

    def run_of(row):
        end = row
        while end < stop and found_at(end) == found_at(row):
            end += 1
        return end - row

    row = start
    while row < stop:
        groups = run_of(row) // TOGETHER
        if groups > 1:
            found = [found_at(row)] * TOGETHER

            def body(number, carry, first=row, found=found):
                group([first + number * TOGETHER + i for i in range(TOGETHER)], found)
                return carry

            lax.fori_loop(0, groups, body, 0)
            row += groups * TOGETHER
            continue
        end = row + 1
        while end < min(stop, row + TOGETHER) and run_of(end) < 2 * TOGETHER:
            end += 1
        group(list(range(row, end)), [found_at(at) for at in range(row, end)])
        row = end


def several(temp, coef, source, width, start, stop, mids, emit, done=None):
    for step in range(1, width):
        first, last = start - (width - step), stop + (width - step)
        mid = mids[(step - 1) % len(mids)]

        def keep(row, layer, value, mid=mid, first=first):
            mid[row - first, layer] = value

        sweep(temp, coef, source, first, last, keep)
        temp = Rows(temp.depth, (first, last, mid, None))
    if done is None:
        sweep(temp, coef, source, start, stop, emit)
        return
    for row in range(start, stop, SUB):
        sweep(temp, coef, source, row, row + SUB, emit)
        done(row + SUB)


def mids_for(width, rows, depth, lanes):
    return [pltpu.VMEM((max(rows, 1), depth, SUB, lanes), f32) for _ in range(min(2, width - 1))]


def raw_rows(value):
    depth, x_rows, span = value.shape
    value = value.reshape(depth, x_rows // SUB, SUB, span // LANES, LANES)
    return value.transpose(0, 1, 3, 2, 4).reshape(depth * x_rows // SUB, span // LANES * SUB, LANES)


def chunk_copies(number, layers, groups, pairs, sems):
    at = pl.ds(number * layers * groups, layers * groups)
    return [
        pltpu.make_async_copy(source.at[at], buf.at[at], sems.at[which, number])
        for which, (source, buf) in enumerate(pairs)
    ]


def taken(ref, layer, row, groups):
    halves = ref.shape[1] // (SUB * SUB)
    group = layer * groups + row // SUB
    found = [ref[group, pl.ds(half * SUB + row % SUB, SUB, stride=SUB * halves), :] for half in range(halves)]
    return jnp.concatenate(found, axis=1)


def rim_kernel(width, x_rows, layers, temp_in, coef_in, _, low_out, high_out, temp_buf, coef_buf, sems):
    groups = x_rows // SUB
    depth = temp_in.shape[0] // groups
    chunks = depth // layers
    pairs = ((temp_in, temp_buf), (coef_in, coef_buf))
    for number in range(chunks):
        for copy in chunk_copies(number, layers, groups, pairs, sems):
            copy.start()

    @pl.loop(0, chunks)
    def _(number):
        for copy in chunk_copies(number, layers, groups, pairs, sems):
            copy.wait()
        for step in range(layers):
            layer = number * layers + step
            for ref, upward in ((low_out, False), (high_out, True)):
                for dist in range(1, width + 1):
                    row = x_rows - dist if upward else dist - 1
                    place = width - dist if upward else dist - 1
                    ref[place * depth + layer] = taken(temp_buf, layer, row, groups)
                    if dist < width:
                        place = width - 1 - dist if upward else dist - 1
                        ref[(width + place) * depth + layer] = taken(coef_buf, layer, row, groups)


def rim(temp, coef, after, width):
    depth, x_rows, span = temp.shape
    layers = 4
    face = jax.ShapeDtypeStruct(((2 * width - 1) * depth, SUB, span // SUB), f32)
    raw = pltpu.VMEM((depth * x_rows // SUB, span // LANES * SUB, LANES), f32)
    return pl.pallas_call(
        functools.partial(rim_kernel, width, x_rows, layers),
        in_specs=[hbm()] * 3,
        out_specs=[vmem()] * 2,
        out_shape=[face, face],
        scratch_shapes=[raw, raw, pltpu.SemaphoreType.DMA((2, depth // layers))],
        compiler_params=params(52),
        cost_estimate=cost(1e6, 10 * MIB),
        name="rim",
    )(raw_rows(temp), raw_rows(coef), after)


def spread_kernel(layers, temp_in, coef_in, _, temp_out, coef_out, temp_buf, coef_buf, sems):
    x_rows, depth = temp_out.shape[:2]
    groups = x_rows // SUB
    chunks = depth // layers
    pairs = ((temp_in, temp_buf), (coef_in, coef_buf))
    for number in range(chunks):
        for copy in chunk_copies(number, layers, groups, pairs, sems):
            copy.start()

    @pl.loop(0, chunks)
    def _(number):
        for copy in chunk_copies(number, layers, groups, pairs, sems):
            copy.wait()
        for step in range(layers):
            layer = number * layers + step
            for row in range(x_rows):
                temp_out[row, layer] = taken(temp_buf, layer, row, groups)
                coef_out[row, layer] = taken(coef_buf, layer, row, groups)


def spread(temp, coef, after):
    depth, x_rows, span = temp.shape
    layers = 4
    form = jax.ShapeDtypeStruct((x_rows, depth, SUB, span // SUB), f32)
    raw = pltpu.VMEM((depth * x_rows // SUB, span // LANES * SUB, LANES), f32)
    return pl.pallas_call(
        functools.partial(spread_kernel, layers),
        in_specs=[hbm()] * 3,
        out_specs=[vmem()] * 2,
        out_shape=[form, form],
        scratch_shapes=[raw, raw, pltpu.SemaphoreType.DMA((2, depth // layers))],
        compiler_params=params(44),
        cost_estimate=cost(1e6, 16 * MIB),
        name="spread",
    )(raw_rows(temp), raw_rows(coef), after)


def plate_rows(refs, x_rows, depth, width):
    if len(refs) == 1:
        return [(0, x_rows, refs[0], None)]
    low, inner, high = refs
    return [(0, width, low, 0), (width, x_rows - width, inner, None), (x_rows - width, x_rows, high, 0)]


def coef_rows(coef, low_c, high_c, width):
    x_rows, depth = coef.shape[:2]
    base = width * depth
    return Rows(
        depth,
        (1 - width, 0, low_c, base),
        (0, x_rows, coef, None),
        (x_rows, x_rows + width - 1, high_c, base),
    )


def plate(refs, owned, width, turn):
    own, refs = refs[:owned], refs[owned:]
    low, high, coef, low_c, high_c, source, low_s, high_s = refs[:8]
    x_rows, depth = coef.shape[:2]
    temp = Rows(
        depth,
        (-width, 0, low, 0),
        *plate_rows(own, x_rows, depth, width),
        (x_rows, x_rows + width, high, 0),
    )
    scale = coef_rows(coef, low_c, high_c, width)
    base = width * depth
    pieces = [(0, x_rows, source, 0)]
    if turn > 0:
        pieces += [(-1, 0, low_s, base), (x_rows, x_rows + 1, high_s, base)]
    heat_in = Rows(1, *pieces)
    if turn == 1 and width == 2:
        for row, other in ((0, -1), (-1, 0), (x_rows - 1, x_rows), (x_rows, x_rows - 1)):

            def missing(row=row, other=other):
                return scale.tile(scale.find(row), row, 0) * heat_in.tile(heat_in.find(other), other, 0)

            temp.late[row] = missing
    return temp, scale, heat_in, refs[8:]


def edge_kernel(width, owned, turn, *refs):
    temp, scale, heat_in, (low_out, high_out, *mids) = plate(refs, owned, width, turn)
    depth = temp.depth
    source = refs[owned + 5]
    x_rows = source.shape[0]
    for out, start in ((low_out, 0), (high_out, x_rows - width)):

        def emit(row, layer, value, out=out, start=start):
            out[(row - start) * depth + layer] = value

        several(temp, scale, heat_in, width, start, start + width, mids, emit)
    if turn == 0:
        low_out[width * depth] = source[0]
        high_out[width * depth] = source[x_rows - 1]


def edge(own, operands, width, turn):
    coef = operands[2]
    _, depth, _, lanes = coef.shape
    face = jax.ShapeDtypeStruct((width * depth + (turn == 0), SUB, lanes), f32)
    return pl.pallas_call(
        functools.partial(edge_kernel, width, len(own), turn),
        in_specs=[vmem()] * (len(own) + len(operands)),
        out_specs=[vmem()] * 2,
        out_shape=[face, face],
        scratch_shapes=mids_for(width, 3 * width - 2, depth, lanes),
        compiler_params=params(16),
        cost_estimate=cost(12 * 12 * depth * SUB * lanes, 4 * MIB),
        name="edge",
    )(*own, *operands)


def inner_kernel(width, owned, turn, *refs):
    temp, scale, heat_in, (out, *mids) = plate(refs, owned, width, turn)
    x_rows = refs[owned + 5].shape[0]

    def emit(row, layer, value):
        out[row - width, layer] = value

    several(temp, scale, heat_in, width, width, x_rows - width, mids, emit)


def inner(own, operands, width, turn):
    coef = operands[2]
    x_rows, depth, _, lanes = coef.shape
    return pl.pallas_call(
        functools.partial(inner_kernel, width, len(own), turn),
        in_specs=[vmem()] * (len(own) + len(operands)),
        out_specs=vmem(),
        out_shape=jax.ShapeDtypeStruct((x_rows - 2 * width, depth, SUB, lanes), f32),
        scratch_shapes=mids_for(width, x_rows - 2, depth, lanes),
        compiler_params=params(16),
        cost_estimate=cost(12 * 26 * depth * SUB * lanes, 12 * MIB),
        name="inner",
    )(*own, *operands)


def finish_kernel(width, owned, turn, *refs):
    temp, scale, heat_in, rest = plate(refs, owned, width, turn)
    out, wall, staged, out_sem, *mids = rest
    x_rows = wall.shape[0]
    halves = wall.shape[2] // LANES

    def emit(row, layer, value):
        if layer == 0:
            wall[row] = value
        group, place = row // SUB, row % SUB
        for half in range(halves):
            staged[layer, group, pl.ds(half * SUB + place, SUB, stride=SUB * halves), :] = value[
                :, half * LANES : (half + 1) * LANES
            ]

    copies = [
        pltpu.make_async_copy(staged.at[:, group], out.at[:, group], out_sem.at[group])
        for group in range(x_rows // SUB)
    ]

    def done(row):
        copies[row // SUB - 1].start()

    several(temp, scale, heat_in, width, 0, x_rows, mids, emit, done)
    for copy in copies:
        copy.wait()


def finish(own, operands, width, turn):
    coef = operands[2]
    x_rows, depth, _, lanes = coef.shape
    span = lanes * SUB
    groups = x_rows // SUB
    form = (depth, groups, span // LANES * SUB, LANES)
    out, wall = pl.pallas_call(
        functools.partial(finish_kernel, width, len(own), turn),
        in_specs=[vmem()] * (len(own) + len(operands)),
        out_specs=[hbm(), vmem()],
        out_shape=[jax.ShapeDtypeStruct(form, f32), jax.ShapeDtypeStruct((x_rows, SUB, lanes), f32)],
        scratch_shapes=[pltpu.VMEM(form, f32), pltpu.SemaphoreType.DMA((groups,))]
        + mids_for(width, x_rows + 2 * width - 2, depth, lanes),
        compiler_params=params(24),
        cost_estimate=cost(12 * 34 * depth * SUB * lanes, 16 * MIB),
        name="finish",
    )(*own, *operands)
    out = out.reshape(depth, groups, span // LANES, SUB, LANES).transpose(0, 1, 3, 2, 4)
    return out.reshape(depth, x_rows, span), wall


def pack_kernel(devices, far_pos, far_temps, far_owner, own_ref, rank_ref, positions, temps, owner_ref, sems):
    copies = [
        pltpu.make_async_copy(source, held, sems.at[number])
        for number, (source, held) in enumerate(
            ((far_pos, positions), (far_temps, temps), (far_owner, owner_ref))
        )
    ]
    for copy in copies:
        copy.start()
    for copy in copies:
        copy.wait()
    for tile in range(own_ref.shape[1]):
        at = slice(tile * TILE, (tile + 1) * TILE)
        for comp in range(3):
            own_ref[comp, tile : tile + 1, :] = positions[comp : comp + 1, at]
        own_ref[3, tile : tile + 1, :] = temps[:, at]

    ghosts = owner_ref.shape[1]
    block = 256
    before = lax.broadcasted_iota(i32, (block, block), 0) < lax.broadcasted_iota(i32, (block, block), 1)
    ramp = before.astype(f32).astype(bf16)
    carried = jnp.zeros((devices, 1), f32)
    for start in range(0, ghosts, block):
        named = sublane_is(owner_ref[:, start : start + block], devices)
        ones = named.astype(f32)
        counted = dot(ones.astype(bf16), ramp) + carried
        rank = jnp.sum(jnp.where(named, counted, 0.0), axis=0, keepdims=True)
        rank_ref[:, start : start + block] = rank.astype(i32)
        carried = carried + jnp.sum(ones, axis=1, keepdims=True)


def pack(positions, temps, owner, devices):
    return pl.pallas_call(
        functools.partial(pack_kernel, devices),
        in_specs=[pl.BlockSpec(memory_space=pltpu.HBM)] * 3,
        out_specs=[vmem()] * 2,
        out_shape=[
            jax.ShapeDtypeStruct((4, positions.shape[1] // TILE, TILE), f32),
            jax.ShapeDtypeStruct(owner.shape, i32),
        ],
        scratch_shapes=[
            pltpu.VMEM(positions.shape, f32),
            pltpu.VMEM(temps.shape, f32),
            pltpu.VMEM(owner.shape, i32),
            pltpu.SemaphoreType.DMA((3,)),
        ],
        compiler_params=params(52),
        cost_estimate=cost(4e6, 1e5),
        name="pack",
    )(positions, temps, owner)


def heat_kernel(
    devices,
    slots,
    together,
    pairs,
    live,
    own,
    near,
    particle,
    owner,
    rank,
    cell,
    seen,
    out,
    send,
    plain,
    left,
    right,
    turned,
    warm,
    total,
):
    tiles = own.shape[1]
    for side, ref in enumerate((own, near)):
        comps = [ref[comp] for comp in range(3)]
        square = comps[0] * comps[0] + comps[1] * comps[1] + comps[2] * comps[2]
        ones = jnp.ones_like(square)
        first, second = [], []
        for comp in comps:
            a, b, c = parts_of(comp, 3)
            first += [a, a, b, b, a, c]
            second += [2.0 * a, 2.0 * b, 2.0 * a, 2.0 * b, 2.0 * c, 2.0 * a]
        first += parts_of(1.0 - square, 3) + [ones] * 3
        second += [ones] * 3 + parts_of(-square, 3)
        blank = [jnp.zeros_like(square)] * (FEATURES - len(first))
        for number, row in enumerate(second + blank):
            right[pl.ds(side * tiles * FEATURES + number, tiles, stride=FEATURES), :] = row
        if side == 0:
            for number, row in enumerate(first + blank):
                plain[pl.ds(number, tiles, stride=FEATURES), :] = row
            left[...] = plain[...].astype(bf16)
        across = jnp.transpose(ref[3])
        for tile in range(tiles):
            warm[side * tiles + tile] = jnp.broadcast_to(across[:, tile : tile + 1], (TILE, TILE))
    for tile in range(2 * tiles):
        block = right[tile * FEATURES : (tile + 1) * FEATURES, :]
        turned[tile] = jnp.transpose(block).astype(bf16)
    total[...] = jnp.zeros(total.shape, f32)

    def several_pairs(number, carry):
        found = []
        for step in range(together):
            at = number * together + step
            first, second = pairs[0, at], pairs[1, at]
            features = left[pl.ds(pl.multiple_of(first * FEATURES, FEATURES), FEATURES), :]
            inside = jnp.maximum(dot(turned[second], features), 0.0)
            gained = (inside * inside) * (warm[second] - own[3, pl.ds(first, 1), :])
            gained = jnp.sum(gained.reshape(TILE // SUB, SUB, TILE), axis=0)
            found.append((jnp.where(at < live[0], first, tiles), gained))
        for place, gained in found:
            total[place] += gained
        return carry

    lax.fori_loop(0, (live[0] + together - 1) // together, several_pairs, 0)
    out[...] = own[3] + heat_rate * jnp.sum(total[:tiles], axis=1)

    pieces = [part.astype(bf16) for part in parts_of(jnp.transpose(out[...]), 3)]
    table = jnp.concatenate(pieces, axis=1)
    ghosts = particle.shape[1]
    packed = [jnp.zeros((2 * devices, slots), f32) for _ in range(3)]
    block = 512
    for start in range(0, ghosts, block):
        at = slice(start, start + block)
        mirrored = particle[:, at]
        high = sublane_is(mirrored // TILE, tiles).astype(f32).astype(bf16)
        picked = dot(table, jnp.concatenate([high] * 3, axis=0))
        low = sublane_is(mirrored % TILE, TILE)
        value = jnp.sum(jnp.where(low, picked, 0.0), axis=0, keepdims=True)
        flux = wall_heat * (value - seen[:, at])
        cells = cell[:, at]
        cell_parts = [((cells // 256) * 256).astype(f32), (cells % 256).astype(f32), jnp.zeros_like(flux)]
        line = lax.broadcasted_iota(i32, (2 * devices, block), 0)
        named = line // 2 == owner[:, at]
        is_cell = line % 2 == 1
        slot = sublane_is(rank[:, at], slots).astype(f32).astype(bf16)
        for number, part in enumerate(parts_of(flux, 3)):
            chosen = jnp.where(named, jnp.where(is_cell, cell_parts[number], part), 0.0)
            packed[number] = packed[number] + dot_lanes(chosen.astype(bf16), slot)
    send[...] = packed[0] + packed[1] + packed[2]


def heat(pairs, live, own, near, particle, owner, rank, cell, seen, devices, slots):
    tiles = own.shape[1]
    together = 16 if pairs.shape[1] % 16 == 0 else 1
    smem = pl.BlockSpec(memory_space=pltpu.SMEM)
    return pl.pallas_call(
        functools.partial(heat_kernel, devices, slots, together),
        in_specs=[smem, smem] + [vmem()] * 7,
        out_specs=[vmem(), vmem()],
        out_shape=[
            jax.ShapeDtypeStruct((tiles, TILE), f32),
            jax.ShapeDtypeStruct((2 * devices, slots), f32),
        ],
        scratch_shapes=[
            pltpu.VMEM((tiles * FEATURES, TILE), f32),
            pltpu.VMEM((tiles * FEATURES, TILE), bf16),
            pltpu.VMEM((2 * tiles * FEATURES, TILE), f32),
            pltpu.VMEM((2 * tiles, TILE, FEATURES), bf16),
            pltpu.VMEM((2 * tiles, TILE, TILE), f32),
            pltpu.VMEM((tiles + 1, SUB, TILE), f32),
        ],
        compiler_params=params(16),
        cost_estimate=cost(12 * 4.2e6, 1 * MIB),
        name="heat",
    )(pairs, live, own, near, particle, owner, rank, cell, seen)


def surface_kernel(received, out):
    devices = received.shape[0] // 2
    high_count, low_count = out.shape
    total = jnp.zeros((2 * high_count, low_count), f32)
    for device in range(devices):
        flux = received[2 * device : 2 * device + 1, :]
        cells = received[2 * device + 1 : 2 * device + 2, :].astype(i32)
        high = sublane_is(cells // low_count, high_count)
        low = sublane_is(cells % low_count, low_count).astype(f32).astype(bf16)
        chosen = [jnp.where(high, part, 0.0).astype(bf16) for part in parts_of(flux, 2)]
        total = total + dot_lanes(jnp.concatenate(chosen, axis=0), low)
    out[...] = (total[:high_count] + total[high_count:]) * (1.0 / SUBSTEPS)


def surface_of(received, high_count, low_count):
    return pl.pallas_call(
        surface_kernel,
        in_specs=[vmem()],
        out_specs=vmem(),
        out_shape=jax.ShapeDtypeStruct((high_count, low_count), f32),
        compiler_params=params(16),
        cost_estimate=cost(6e7, 2e5),
        name="surface",
    )(received)


def wall_kernel(received, wall, out):
    devices = received.shape[0] // 2
    high_count, low_count = wall.shape
    pieces = [part.astype(bf16) for part in parts_of(jnp.transpose(wall[...]), 2)]
    table = jnp.concatenate(pieces, axis=1)
    for device in range(devices):
        cells = received[2 * device + 1 : 2 * device + 2, :].astype(i32)
        high = sublane_is(cells // low_count, high_count).astype(f32).astype(bf16)
        picked = dot(table, jnp.concatenate([high, high], axis=0))
        low = sublane_is(cells % low_count, low_count)
        out[device : device + 1, :] = jnp.sum(jnp.where(low, picked, 0.0), axis=0, keepdims=True)


def wall_of(received, wall):
    return pl.pallas_call(
        wall_kernel,
        in_specs=[vmem()] * 2,
        out_specs=vmem(),
        out_shape=jax.ShapeDtypeStruct((received.shape[0] // 2, received.shape[1]), f32),
        compiler_params=params(16),
        cost_estimate=cost(6e7, 2e5),
        name="wall",
    )(received, wall)


def back_kernel(returned, owner, rank, out):
    devices, slots = returned.shape
    pieces = [part.astype(bf16) for part in parts_of(jnp.transpose(returned[...]), 3)]
    table = jnp.concatenate(pieces, axis=1)
    block = 512
    for start in range(0, owner.shape[1], block):
        at = slice(start, start + block)
        named = sublane_is(owner[:, at], devices).astype(f32).astype(bf16)
        picked = dot(table, jnp.concatenate([named] * 3, axis=0))
        slot = sublane_is(rank[:, at], slots)
        out[:, at] = jnp.sum(jnp.where(slot, picked, 0.0), axis=0, keepdims=True)


def back_of(returned, owner, rank):
    return pl.pallas_call(
        back_kernel,
        in_specs=[vmem()] * 3,
        out_specs=vmem(),
        out_shape=jax.ShapeDtypeStruct(owner.shape, f32),
        compiler_params=params(16),
        cost_estimate=cost(6e6, 1e5),
        name="back",
    )(returned, owner, rank)


def between(low_face, high_face):
    count = lax.axis_size(AXES)
    upward = [(i, i + 1) for i in range(count - 1)]
    downward = [(target, source) for source, target in upward]
    return lax.ppermute(high_face, AXES, upward), lax.ppermute(low_face, AXES, downward)


def on_device(
    positions,
    particle_temp,
    pair_list,
    pair_count,
    ghost_particle,
    ghost_owner,
    ghost_cell,
    wall_seen,
    solid_temp,
    conduct,
):
    width = WIDTH
    depth, x_rows, span = solid_temp.shape
    particles = positions.shape[1]
    devices = lax.axis_size(AXES)
    ghosts = ghost_cell.shape[0]
    slots = max(2, 2 * ghosts // devices)
    sub_count = lax.axis_size("sub")
    lanes = span // SUB

    owner = ghost_owner.reshape(1, ghosts)
    own, rank = pack(positions, particle_temp.reshape(1, particles), owner, devices)
    near = lax.ppermute(own, "sub", [(i, (i - 1) % sub_count) for i in range(sub_count)])

    low_face, high_face = rim(solid_temp, conduct, near, width)
    low_c, high_c = between(low_face, high_face)

    particle_out, send = heat(
        pair_list.T,
        pair_count,
        own,
        near,
        ghost_particle.reshape(1, ghosts),
        owner,
        rank,
        ghost_cell.reshape(1, ghosts),
        wall_seen.reshape(1, ghosts),
        devices,
        slots,
    )
    received = lax.all_to_all(
        send.reshape(devices, 2 * slots), AXES, split_axis=0, concat_axis=0, tiled=True
    ).reshape(2 * devices, slots)
    source = surface_of(received, x_rows * SUB, lanes).reshape(x_rows, SUB, lanes)

    temp, coef = spread(solid_temp, conduct, source)
    own_rows, low, high = [temp], low_c, high_c
    low_s, high_s = low_c, high_c
    last = SUBSTEPS // width - 1
    for turn in range(last):
        operands = [low, high, coef, low_c, high_c, source, low_s, high_s]
        low_face, high_face = edge(own_rows, operands, width, turn)
        own_rows = [low_face, inner(own_rows, operands, width, turn), high_face]
        low, high = between(low_face, high_face)
        if turn == 0:
            low_s, high_s = low, high
    solid_out, wall = finish(own_rows, [low, high, coef, low_c, high_c, source, low_s, high_s], width, last)
    answer = wall_of(received, wall.reshape(x_rows * SUB, lanes))
    returned = lax.all_to_all(answer, AXES, split_axis=0, concat_axis=0, tiled=True)
    ghost_temp = back_of(returned, owner, rank)
    return (particle_out.reshape(-1), solid_out, ghost_temp.reshape(-1))


def solution(mesh):
    placed = (
        P(None, AXES),
        P(AXES),
        P(AXES, None),
        P(AXES),
        P(AXES),
        P(AXES, None),
        P(AXES),
        P(AXES),
        P(None, AXES, None),
        P(None, AXES, None),
    )
    return jax.shard_map(
        on_device,
        mesh=mesh,
        in_specs=placed,
        out_specs=(P(AXES), P(None, AXES, None), P(AXES)),
        check_vma=False,
    )
```

```python
import functools

import jax
import jax.numpy as jnp
from jax import lax
from jax.experimental import pallas as pl
from jax.experimental.pallas import tpu as pltpu
from jax.sharding import PartitionSpec as P

TILE = 128
SUBSTEPS = 6
LANES = 128
SUB = 8
WIDTH = 2
FEATURES = 32
TOGETHER = 4
AXES = ("fluid", "sub")
MIB = 1 << 20

heat_rate = 0.004
wall_heat = 0.5

f32 = jnp.float32
bf16 = jnp.bfloat16
i32 = jnp.int32


def params(mib):
    return pltpu.CompilerParams(vmem_limit_bytes=mib * MIB)


def cost(flops, moved):
    return pl.CostEstimate(flops=int(flops), bytes_accessed=int(moved), transcendentals=0)


def vmem():
    return pl.BlockSpec(memory_space=pltpu.VMEM)


def hbm():
    return pl.BlockSpec(memory_space=pl.ANY)


def parts_of(value, count):
    parts = []
    for _ in range(count):
        part = value.astype(bf16).astype(f32)
        parts.append(part)
        value = value - part
    return parts


def dot(left, right):
    return lax.dot_general(left, right, (((1,), (0,)), ((), ())), preferred_element_type=f32)


def dot_lanes(left, right):
    return lax.dot_general(left, right, (((1,), (1,)), ((), ())), preferred_element_type=f32)


def sublane_is(row, count):
    return lax.broadcasted_iota(i32, (count, row.shape[1]), 0) == row


def z_sum(cur, lane_first, lane_last, sub_first, sub_last):
    left, right = cur[:, :LANES], cur[:, LANES:]
    left_up, right_up = pltpu.roll(left, 1, 1), pltpu.roll(right, 1, 1)
    left_down, right_down = pltpu.roll(left, LANES - 1, 1), pltpu.roll(right, LANES - 1, 1)
    carry_up = jnp.where(sub_first, 0.0, pltpu.roll(right_up, 1, 0))
    carry_down = jnp.where(sub_last, 0.0, pltpu.roll(left_down, SUB - 1, 0))
    first = jnp.where(lane_first, carry_up, left_up) + jnp.where(lane_last, right_down, left_down)
    second = jnp.where(lane_first, left_up, right_up) + jnp.where(lane_last, carry_down, right_down)
    return jnp.concatenate([first, second], axis=1)


def masks():
    lane = lax.broadcasted_iota(i32, (SUB, LANES), 1)
    sub = lax.broadcasted_iota(i32, (SUB, LANES), 0)
    return lane == 0, lane == LANES - 1, sub == 0, sub == SUB - 1


class Rows:
    def __init__(self, depth, *pieces):
        self.depth = depth
        self.pieces = pieces
        self.late = {}

    def find(self, row):
        for piece in self.pieces:
            if piece[0] <= row < piece[1]:
                return piece
        return None

    def tile(self, piece, row, layer):
        start, _, ref, base = piece
        if base is None:
            return ref[row - start, layer]
        value = ref[base + (row - start) * self.depth + layer]
        if layer == 0 and isinstance(row, int) and row in self.late:
            value = value + self.late[row]()
        return value


def sweep(temp, coef, source, start, stop, emit):
    depth = temp.depth

    def found_at(row):
        return temp.find(row - 1), temp.find(row), temp.find(row + 1), coef.find(row), source.find(row)

    def group(rows, found):
        marks = masks()
        count = len(rows)
        before = [None] * count
        cur = [temp.tile(found[i][1], rows[i], 0) for i in range(count)]
        for layer in range(depth):
            above = temp.tile(found[0][0], rows[0] - 1, layer)
            below = temp.tile(found[-1][2], rows[-1] + 1, layer)
            after = [None] * count
            if layer + 1 < depth:
                after = [temp.tile(found[i][1], rows[i], layer + 1) for i in range(count)]
            for i in range(count):
                up = above if i == 0 else cur[i - 1]
                down = below if i == count - 1 else cur[i + 1]
                total = up + down + z_sum(cur[i], *marks)
                for other in (before[i], after[i]):
                    if other is not None:
                        total = total + other
                value = cur[i] + coef.tile(found[i][3], rows[i], layer) * (total - 6.0 * cur[i])
                if layer == 0 and found[i][4] is not None:
                    value = value + source.tile(found[i][4], rows[i], 0)
                emit(rows[i], layer, value)
            before, cur = cur, after

    def run_of(row):
        end = row
        while end < stop and found_at(end) == found_at(row):
            end += 1
        return end - row

    row = start
    while row < stop:
        groups = run_of(row) // TOGETHER
        if groups > 1:
            found = [found_at(row)] * TOGETHER

            def body(number, carry, first=row, found=found):
                group([first + number * TOGETHER + i for i in range(TOGETHER)], found)
                return carry

            lax.fori_loop(0, groups, body, 0)
            row += groups * TOGETHER
            continue
        end = row + 1
        while end < min(stop, row + TOGETHER) and run_of(end) < 2 * TOGETHER:
            end += 1
        group(list(range(row, end)), [found_at(at) for at in range(row, end)])
        row = end


def several(temp, coef, source, width, start, stop, mids, emit, done=None):
    for step in range(1, width):
        first, last = start - (width - step), stop + (width - step)
        mid = mids[(step - 1) % len(mids)]

        def keep(row, layer, value, mid=mid, first=first):
            mid[row - first, layer] = value

        sweep(temp, coef, source, first, last, keep)
        temp = Rows(temp.depth, (first, last, mid, None))
    if done is None:
        sweep(temp, coef, source, start, stop, emit)
        return
    for row in range(start, stop, SUB):
        sweep(temp, coef, source, row, row + SUB, emit)
        done(row + SUB)


def mids_for(width, rows, depth, lanes):
    return [pltpu.VMEM((max(rows, 1), depth, SUB, lanes), f32) for _ in range(min(2, width - 1))]


def raw_rows(value):
    depth, x_rows, span = value.shape
    value = value.reshape(depth, x_rows // SUB, SUB, span // LANES, LANES)
    return value.transpose(0, 1, 3, 2, 4).reshape(depth * x_rows // SUB, span // LANES * SUB, LANES)


def chunk_copies(number, layers, groups, pairs, sems):
    at = pl.ds(number * layers * groups, layers * groups)
    return [
        pltpu.make_async_copy(source.at[at], buf.at[at], sems.at[which, number])
        for which, (source, buf) in enumerate(pairs)
    ]


def taken(ref, layer, row, groups):
    halves = ref.shape[1] // (SUB * SUB)
    group = layer * groups + row // SUB
    found = [ref[group, pl.ds(half * SUB + row % SUB, SUB, stride=SUB * halves), :] for half in range(halves)]
    return jnp.concatenate(found, axis=1)


def rim_kernel(
    width, x_rows, layers, temp_in, coef_in, _, __, low_out, high_out, low_strip, high_strip, temp_buf, coef_buf, sems
):
    groups = x_rows // SUB
    depth = temp_in.shape[0] // groups
    chunks = depth // layers
    pairs = ((temp_in, temp_buf), (coef_in, coef_buf))
    for number in range(chunks):
        for copy in chunk_copies(number, layers, groups, pairs, sems):
            copy.start()

    @pl.loop(0, chunks)
    def _(number):
        for copy in chunk_copies(number, layers, groups, pairs, sems):
            copy.wait()
        for step in range(layers):
            layer = number * layers + step
            for ref, upward in ((low_out, False), (high_out, True)):
                for dist in range(1, width + 1):
                    row = x_rows - dist if upward else dist - 1
                    place = width - dist if upward else dist - 1
                    ref[place * depth + layer] = taken(temp_buf, layer, row, groups)
                    if dist < width:
                        place = width - 1 - dist if upward else dist - 1
                        ref[(width + place) * depth + layer] = taken(coef_buf, layer, row, groups)
            for ref, first in ((low_strip, width), (high_strip, x_rows - 2 * width)):
                shift = -1 if first == width else 1
                for place in range(width):
                    ref[place * depth + layer] = taken(temp_buf, layer, first + place, groups)
                    ref[(width + place) * depth + layer] = taken(coef_buf, layer, first + shift + place, groups)


def rim(temp, coef, after, also, width):
    depth, x_rows, span = temp.shape
    layers = 4
    face = jax.ShapeDtypeStruct(((2 * width - 1) * depth, SUB, span // SUB), f32)
    strip = jax.ShapeDtypeStruct((2 * width * depth, SUB, span // SUB), f32)
    raw = pltpu.VMEM((depth * x_rows // SUB, span // LANES * SUB, LANES), f32)
    return pl.pallas_call(
        functools.partial(rim_kernel, width, x_rows, layers),
        in_specs=[hbm()] * 4,
        out_specs=[vmem()] * 4,
        out_shape=[face, face, strip, strip],
        scratch_shapes=[raw, raw, pltpu.SemaphoreType.DMA((2, depth // layers))],
        compiler_params=params(52),
        cost_estimate=cost(1e6, 10 * MIB),
        name="rim",
    )(raw_rows(temp), raw_rows(coef), after, also)


def spread_kernel(layers, temp_in, coef_in, _, temp_out, coef_out, temp_buf, coef_buf, sems):
    x_rows, depth = temp_out.shape[:2]
    groups = x_rows // SUB
    chunks = depth // layers
    pairs = ((temp_in, temp_buf), (coef_in, coef_buf))
    for number in range(chunks):
        for copy in chunk_copies(number, layers, groups, pairs, sems):
            copy.start()

    @pl.loop(0, chunks)
    def _(number):
        for copy in chunk_copies(number, layers, groups, pairs, sems):
            copy.wait()
        for step in range(layers):
            layer = number * layers + step
            for row in range(x_rows):
                temp_out[row, layer] = taken(temp_buf, layer, row, groups)
                coef_out[row, layer] = taken(coef_buf, layer, row, groups)


def spread(temp, coef, after):
    depth, x_rows, span = temp.shape
    layers = 4
    form = jax.ShapeDtypeStruct((x_rows, depth, SUB, span // SUB), f32)
    raw = pltpu.VMEM((depth * x_rows // SUB, span // LANES * SUB, LANES), f32)
    return pl.pallas_call(
        functools.partial(spread_kernel, layers),
        in_specs=[hbm()] * 3,
        out_specs=[vmem()] * 2,
        out_shape=[form, form],
        scratch_shapes=[raw, raw, pltpu.SemaphoreType.DMA((2, depth // layers))],
        compiler_params=params(44),
        cost_estimate=cost(1e6, 16 * MIB),
        name="spread",
    )(raw_rows(temp), raw_rows(coef), after)


def plate_rows(refs, x_rows, depth, width):
    if len(refs) == 1:
        return [(0, x_rows, refs[0], None)]
    low, inner, high = refs
    return [(0, width, low, 0), (width, x_rows - width, inner, None), (x_rows - width, x_rows, high, 0)]


def coef_rows(coef, low_c, high_c, width):
    x_rows, depth = coef.shape[:2]
    base = width * depth
    return Rows(
        depth,
        (1 - width, 0, low_c, base),
        (0, x_rows, coef, None),
        (x_rows, x_rows + width - 1, high_c, base),
    )


def plate(refs, owned, width, turn):
    own, refs = refs[:owned], refs[owned:]
    low, high, coef, low_c, high_c, source, low_s, high_s = refs[:8]
    x_rows, depth = coef.shape[:2]
    temp = Rows(
        depth,
        (-width, 0, low, 0),
        *plate_rows(own, x_rows, depth, width),
        (x_rows, x_rows + width, high, 0),
    )
    scale = coef_rows(coef, low_c, high_c, width)
    base = width * depth
    pieces = [(0, x_rows, source, 0)]
    if turn > 0:
        pieces += [(-1, 0, low_s, base), (x_rows, x_rows + 1, high_s, base)]
    heat_in = Rows(1, *pieces)
    if turn == 1 and width == 2:
        for row, other in ((0, -1), (-1, 0), (x_rows - 1, x_rows), (x_rows, x_rows - 1)):

            def missing(row=row, other=other):
                return scale.tile(scale.find(row), row, 0) * heat_in.tile(heat_in.find(other), other, 0)

            temp.late[row] = missing
    return temp, scale, heat_in, refs[8:]


def edge_faces(temp, scale, heat_in, width, x_rows, low_out, high_out, mids):
    depth = temp.depth
    for out, start in ((low_out, 0), (high_out, x_rows - width)):

        def emit(row, layer, value, out=out, start=start):
            out[(row - start) * depth + layer] = value

        several(temp, scale, heat_in, width, start, start + width, mids, emit)


def first_edge_kernel(
    width, depth, low, high, low_c, high_c, low_strip, high_strip, source, low_out, high_out, *mids
):
    x_rows = source.shape[0]
    base = width * depth
    temp = Rows(
        depth,
        (-width, 0, low_c, 0),
        (0, width, low, 0),
        (width, 2 * width, low_strip, 0),
        (x_rows - 2 * width, x_rows - width, high_strip, 0),
        (x_rows - width, x_rows, high, 0),
        (x_rows, x_rows + width, high_c, 0),
    )
    scale = Rows(
        depth,
        (1 - width, 0, low_c, base),
        (0, width - 1, low, base),
        (width - 1, 2 * width - 1, low_strip, base),
        (x_rows - 2 * width + 1, x_rows - width + 1, high_strip, base),
        (x_rows - width + 1, x_rows, high, base),
        (x_rows, x_rows + width - 1, high_c, base),
    )
    heat_in = Rows(1, (0, x_rows, source, 0))
    edge_faces(temp, scale, heat_in, width, x_rows, low_out, high_out, mids)
    low_out[base] = source[0]
    high_out[base] = source[x_rows - 1]


def first_edge(faces, strips, source, width, depth):
    lanes = source.shape[2]
    face = jax.ShapeDtypeStruct((width * depth + 1, SUB, lanes), f32)
    return pl.pallas_call(
        functools.partial(first_edge_kernel, width, depth),
        in_specs=[vmem()] * 7,
        out_specs=[vmem()] * 2,
        out_shape=[face, face],
        scratch_shapes=mids_for(width, 3 * width - 2, depth, lanes),
        compiler_params=params(16),
        cost_estimate=cost(12 * 12 * depth * SUB * lanes, 4 * MIB),
        name="edge",
    )(*faces, *strips, source)


def edge_kernel(width, owned, turn, *refs):
    temp, scale, heat_in, (low_out, high_out, *mids) = plate(refs, owned, width, turn)
    edge_faces(temp, scale, heat_in, width, refs[owned + 5].shape[0], low_out, high_out, mids)


def edge(own, operands, width, turn):
    coef = operands[2]
    _, depth, _, lanes = coef.shape
    face = jax.ShapeDtypeStruct((width * depth, SUB, lanes), f32)
    return pl.pallas_call(
        functools.partial(edge_kernel, width, len(own), turn),
        in_specs=[vmem()] * (len(own) + len(operands)),
        out_specs=[vmem()] * 2,
        out_shape=[face, face],
        scratch_shapes=mids_for(width, 3 * width - 2, depth, lanes),
        compiler_params=params(16),
        cost_estimate=cost(12 * 12 * depth * SUB * lanes, 4 * MIB),
        name="edge",
    )(*own, *operands)


def inner_kernel(width, owned, turn, *refs):
    temp, scale, heat_in, (out, *mids) = plate(refs, owned, width, turn)
    x_rows = refs[owned + 5].shape[0]

    def emit(row, layer, value):
        out[row - width, layer] = value

    several(temp, scale, heat_in, width, width, x_rows - width, mids, emit)


def inner(own, operands, width, turn):
    coef = operands[2]
    x_rows, depth, _, lanes = coef.shape
    return pl.pallas_call(
        functools.partial(inner_kernel, width, len(own), turn),
        in_specs=[vmem()] * (len(own) + len(operands)),
        out_specs=vmem(),
        out_shape=jax.ShapeDtypeStruct((x_rows - 2 * width, depth, SUB, lanes), f32),
        scratch_shapes=mids_for(width, x_rows - 2, depth, lanes),
        compiler_params=params(16),
        cost_estimate=cost(12 * 26 * depth * SUB * lanes, 12 * MIB),
        name="inner",
    )(*own, *operands)


def lay_out(staged, wall, halves):
    def emit(row, layer, value):
        if layer == 0:
            wall[row] = value
        group, place = row // SUB, row % SUB
        for half in range(halves):
            staged[layer, group, pl.ds(half * SUB + place, SUB, stride=SUB * halves), :] = value[
                :, half * LANES : (half + 1) * LANES
            ]

    return emit


def middle_kernel(width, owned, turn, *refs):
    temp, scale, heat_in, (staged, wall, *mids) = plate(refs, owned, width, turn)
    x_rows = wall.shape[0]
    emit = lay_out(staged, wall, wall.shape[2] // LANES)
    several(temp, scale, heat_in, width, width, x_rows - width, mids, emit)


def plate_form(coef):
    x_rows, depth, _, lanes = coef.shape
    return [
        jax.ShapeDtypeStruct((depth, x_rows // SUB, lanes // LANES * SUB * SUB, LANES), f32),
        jax.ShapeDtypeStruct((x_rows, SUB, lanes), f32),
    ]


def middle(own, operands, width, turn):
    coef = operands[2]
    x_rows, depth, _, lanes = coef.shape
    return pl.pallas_call(
        functools.partial(middle_kernel, width, len(own), turn),
        in_specs=[vmem()] * (len(own) + len(operands)),
        out_specs=[vmem()] * 2,
        out_shape=plate_form(coef),
        scratch_shapes=mids_for(width, x_rows - 2, depth, lanes),
        compiler_params=params(16),
        cost_estimate=cost(12 * 26 * depth * SUB * lanes, 12 * MIB),
        name="middle",
    )(*own, *operands)


def finish_kernel(width, owned, turn, *refs):
    temp, scale, heat_in, rest = plate(refs, owned, width, turn)
    _, _, out, staged, wall, out_sem, *mids = rest
    x_rows = wall.shape[0]
    emit = lay_out(staged, wall, wall.shape[2] // LANES)
    groups = x_rows // SUB
    copies = [
        pltpu.make_async_copy(staged.at[:, group], out.at[:, group], out_sem.at[group])
        for group in range(groups)
    ]
    for group in range(1, groups - 1):
        copies[group].start()
    several(temp, scale, heat_in, width, 0, width, mids, emit)
    if groups > 1:
        copies[0].start()
    several(temp, scale, heat_in, width, x_rows - width, x_rows, mids, emit)
    copies[-1].start()
    for copy in copies:
        copy.wait()


def finish(own, operands, staged, wall, width, turn):
    coef = operands[2]
    x_rows, depth, _, lanes = coef.shape
    count = len(own) + len(operands)
    form = plate_form(coef)
    out, _, wall = pl.pallas_call(
        functools.partial(finish_kernel, width, len(own), turn),
        in_specs=[vmem()] * (count + 2),
        out_specs=[hbm(), vmem(), vmem()],
        out_shape=[form[0], *form],
        scratch_shapes=[pltpu.SemaphoreType.DMA((x_rows // SUB,))] + mids_for(width, 3 * width - 2, depth, lanes),
        input_output_aliases={count: 1, count + 1: 2},
        compiler_params=params(16),
        cost_estimate=cost(12 * 12 * depth * SUB * lanes, 8 * MIB),
        name="finish",
    )(*own, *operands, staged, wall)
    span = lanes * SUB
    out = out.reshape(depth, x_rows // SUB, span // LANES, SUB, LANES).transpose(0, 1, 3, 2, 4)
    return out.reshape(depth, x_rows, span), wall


def pack_kernel(far_pos, far_temps, own_ref, positions, temps, sems):
    copies = [
        pltpu.make_async_copy(far_pos, positions, sems.at[0]),
        pltpu.make_async_copy(far_temps, temps, sems.at[1]),
    ]
    for copy in copies:
        copy.start()
    for copy in copies:
        copy.wait()
    for tile in range(own_ref.shape[1]):
        at = slice(tile * TILE, (tile + 1) * TILE)
        for comp in range(3):
            own_ref[comp, tile : tile + 1, :] = positions[comp : comp + 1, at]
        own_ref[3, tile : tile + 1, :] = temps[:, at]


def pack(positions, temps):
    return pl.pallas_call(
        pack_kernel,
        in_specs=[hbm()] * 2,
        out_specs=vmem(),
        out_shape=jax.ShapeDtypeStruct((4, positions.shape[1] // TILE, TILE), f32),
        scratch_shapes=[
            pltpu.VMEM(positions.shape, f32),
            pltpu.VMEM(temps.shape, f32),
            pltpu.SemaphoreType.DMA((2,)),
        ],
        compiler_params=params(58),
        cost_estimate=cost(1e4, 1e5),
        name="pack",
    )(positions, temps)


def tables(ref, right, turned, warm, first_tile):
    tiles = ref.shape[1]
    comps = [ref[comp] for comp in range(3)]
    square = comps[0] * comps[0] + comps[1] * comps[1] + comps[2] * comps[2]
    rows = []
    for comp in comps:
        a, b, c = parts_of(comp, 3)
        rows += [2.0 * a, 2.0 * b, 2.0 * a, 2.0 * b, 2.0 * c, 2.0 * a]
    rows += [jnp.ones_like(square)] * 3 + parts_of(-square, 3)
    rows += [jnp.zeros_like(square)] * (FEATURES - len(rows))
    for number, row in enumerate(rows):
        right[pl.ds(number, tiles, stride=FEATURES), :] = row
    across = jnp.transpose(ref[3])
    for tile in range(tiles):
        warm[first_tile + tile] = jnp.broadcast_to(across[:, tile : tile + 1], (TILE, TILE))
        block = right[tile * FEATURES : (tile + 1) * FEATURES, :]
        turned[first_tile + tile] = jnp.transpose(block).astype(bf16)


def prepare_kernel(devices, own, owner_ref, rank_ref, left, turned, warm, plain):
    ghosts = owner_ref.shape[1]
    block = 256
    before = lax.broadcasted_iota(i32, (block, block), 0) < lax.broadcasted_iota(i32, (block, block), 1)
    ramp = before.astype(f32).astype(bf16)
    carried = jnp.zeros((devices, 1), f32)
    for start in range(0, ghosts, block):
        named = sublane_is(owner_ref[:, start : start + block], devices)
        ones = named.astype(f32)
        counted = dot(ones.astype(bf16), ramp) + carried
        rank = jnp.sum(jnp.where(named, counted, 0.0), axis=0, keepdims=True)
        rank_ref[:, start : start + block] = rank.astype(i32)
        carried = carried + jnp.sum(ones, axis=1, keepdims=True)

    tables(own, plain, turned, warm, 0)
    tiles = own.shape[1]
    comps = [own[comp] for comp in range(3)]
    square = comps[0] * comps[0] + comps[1] * comps[1] + comps[2] * comps[2]
    rows = []
    for comp in comps:
        a, b, c = parts_of(comp, 3)
        rows += [a, a, b, b, a, c]
    rows += parts_of(1.0 - square, 3) + [jnp.ones_like(square)] * 3
    rows += [jnp.zeros_like(square)] * (FEATURES - len(rows))
    for number, row in enumerate(rows):
        plain[pl.ds(number, tiles, stride=FEATURES), :] = row
    left[...] = plain[...].astype(bf16)


def prepare(own, owner, devices):
    tiles = own.shape[1]
    return pl.pallas_call(
        functools.partial(prepare_kernel, devices),
        in_specs=[vmem()] * 2,
        out_specs=[vmem()] * 4,
        out_shape=[
            jax.ShapeDtypeStruct(owner.shape, i32),
            jax.ShapeDtypeStruct((tiles * FEATURES, TILE), bf16),
            jax.ShapeDtypeStruct((tiles, TILE, FEATURES), bf16),
            jax.ShapeDtypeStruct((tiles, TILE, TILE), f32),
        ],
        scratch_shapes=[pltpu.VMEM((tiles * FEATURES, TILE), f32)],
        compiler_params=params(16),
        cost_estimate=cost(8e6, 2e6),
        name="prepare",
    )(own, owner)


def heat_kernel(
    devices,
    slots,
    together,
    pairs,
    live,
    own,
    near,
    left,
    own_turned,
    own_warm,
    particle,
    owner,
    rank,
    cell,
    seen,
    out,
    send,
    right,
    turned,
    warm,
    total,
):
    tiles = own.shape[1]
    turned[:tiles] = own_turned[...]
    warm[:tiles] = own_warm[...]
    tables(near, right, turned, warm, tiles)
    total[...] = jnp.zeros(total.shape, f32)

    def several_pairs(number, carry):
        found = []
        for step in range(together):
            at = number * together + step
            first, second = pairs[0, at], pairs[1, at]
            features = left[pl.ds(pl.multiple_of(first * FEATURES, FEATURES), FEATURES), :]
            inside = jnp.maximum(dot(turned[second], features), 0.0)
            gained = (inside * inside) * (warm[second] - own[3, pl.ds(first, 1), :])
            gained = jnp.sum(gained.reshape(TILE // SUB, SUB, TILE), axis=0)
            found.append((jnp.where(at < live[0], first, tiles), gained))
        for place, gained in found:
            total[place] += gained
        return carry

    lax.fori_loop(0, (live[0] + together - 1) // together, several_pairs, 0)
    out[...] = own[3] + heat_rate * jnp.sum(total[:tiles], axis=1)

    pieces = [part.astype(bf16) for part in parts_of(jnp.transpose(out[...]), 3)]
    table = jnp.concatenate(pieces, axis=1)
    ghosts = particle.shape[1]
    packed = [jnp.zeros((2 * devices, slots), f32) for _ in range(3)]
    block = 512
    for start in range(0, ghosts, block):
        at = slice(start, start + block)
        mirrored = particle[:, at]
        high = sublane_is(mirrored // TILE, tiles).astype(f32).astype(bf16)
        picked = dot(table, jnp.concatenate([high] * 3, axis=0))
        low = sublane_is(mirrored % TILE, TILE)
        value = jnp.sum(jnp.where(low, picked, 0.0), axis=0, keepdims=True)
        flux = wall_heat * (value - seen[:, at])
        cells = cell[:, at]
        cell_parts = [((cells // 256) * 256).astype(f32), (cells % 256).astype(f32), jnp.zeros_like(flux)]
        line = lax.broadcasted_iota(i32, (2 * devices, block), 0)
        named = line // 2 == owner[:, at]
        is_cell = line % 2 == 1
        slot = sublane_is(rank[:, at], slots).astype(f32).astype(bf16)
        for number, part in enumerate(parts_of(flux, 3)):
            chosen = jnp.where(named, jnp.where(is_cell, cell_parts[number], part), 0.0)
            packed[number] = packed[number] + dot_lanes(chosen.astype(bf16), slot)
    send[...] = packed[0] + packed[1] + packed[2]


def heat(pairs, live, own, near, made, particle, owner, rank, cell, seen, devices, slots):
    tiles = own.shape[1]
    together = 16 if pairs.shape[1] % 16 == 0 else 1
    smem = pl.BlockSpec(memory_space=pltpu.SMEM)
    return pl.pallas_call(
        functools.partial(heat_kernel, devices, slots, together),
        in_specs=[smem, smem] + [vmem()] * 10,
        out_specs=[vmem(), vmem()],
        out_shape=[
            jax.ShapeDtypeStruct((tiles, TILE), f32),
            jax.ShapeDtypeStruct((2 * devices, slots), f32),
        ],
        scratch_shapes=[
            pltpu.VMEM((tiles * FEATURES, TILE), f32),
            pltpu.VMEM((2 * tiles, TILE, FEATURES), bf16),
            pltpu.VMEM((2 * tiles, TILE, TILE), f32),
            pltpu.VMEM((tiles + 1, SUB, TILE), f32),
        ],
        compiler_params=params(16),
        cost_estimate=cost(12 * 4.2e6, 1 * MIB),
        name="heat",
    )(pairs, live, own, near, *made, particle, owner, rank, cell, seen)


def surface_kernel(received, out):
    devices = received.shape[0] // 2
    high_count, low_count = out.shape
    total = jnp.zeros((2 * high_count, low_count), f32)
    for device in range(devices):
        flux = received[2 * device : 2 * device + 1, :]
        cells = received[2 * device + 1 : 2 * device + 2, :].astype(i32)
        high = sublane_is(cells // low_count, high_count)
        low = sublane_is(cells % low_count, low_count).astype(f32).astype(bf16)
        chosen = [jnp.where(high, part, 0.0).astype(bf16) for part in parts_of(flux, 2)]
        total = total + dot_lanes(jnp.concatenate(chosen, axis=0), low)
    out[...] = (total[:high_count] + total[high_count:]) * (1.0 / SUBSTEPS)


def surface_of(received, high_count, low_count):
    return pl.pallas_call(
        surface_kernel,
        in_specs=[vmem()],
        out_specs=vmem(),
        out_shape=jax.ShapeDtypeStruct((high_count, low_count), f32),
        compiler_params=params(16),
        cost_estimate=cost(6e7, 2e5),
        name="surface",
    )(received)


def wall_kernel(received, wall, out):
    devices = received.shape[0] // 2
    high_count, low_count = wall.shape
    pieces = [part.astype(bf16) for part in parts_of(jnp.transpose(wall[...]), 2)]
    table = jnp.concatenate(pieces, axis=1)
    for device in range(devices):
        cells = received[2 * device + 1 : 2 * device + 2, :].astype(i32)
        high = sublane_is(cells // low_count, high_count).astype(f32).astype(bf16)
        picked = dot(table, jnp.concatenate([high, high], axis=0))
        low = sublane_is(cells % low_count, low_count)
        out[device : device + 1, :] = jnp.sum(jnp.where(low, picked, 0.0), axis=0, keepdims=True)


def wall_of(received, wall):
    return pl.pallas_call(
        wall_kernel,
        in_specs=[vmem()] * 2,
        out_specs=vmem(),
        out_shape=jax.ShapeDtypeStruct((received.shape[0] // 2, received.shape[1]), f32),
        compiler_params=params(16),
        cost_estimate=cost(6e7, 2e5),
        name="wall",
    )(received, wall)


def back_kernel(returned, owner, rank, out):
    devices, slots = returned.shape
    pieces = [part.astype(bf16) for part in parts_of(jnp.transpose(returned[...]), 3)]
    table = jnp.concatenate(pieces, axis=1)
    block = 512
    for start in range(0, owner.shape[1], block):
        at = slice(start, start + block)
        named = sublane_is(owner[:, at], devices).astype(f32).astype(bf16)
        picked = dot(table, jnp.concatenate([named] * 3, axis=0))
        slot = sublane_is(rank[:, at], slots)
        out[:, at] = jnp.sum(jnp.where(slot, picked, 0.0), axis=0, keepdims=True)


def back_of(returned, owner, rank):
    return pl.pallas_call(
        back_kernel,
        in_specs=[vmem()] * 3,
        out_specs=vmem(),
        out_shape=jax.ShapeDtypeStruct(owner.shape, f32),
        compiler_params=params(16),
        cost_estimate=cost(6e6, 1e5),
        name="back",
    )(returned, owner, rank)


def between(low_face, high_face):
    count = lax.axis_size(AXES)
    upward = [(i, i + 1) for i in range(count - 1)]
    downward = [(target, source) for source, target in upward]
    return lax.ppermute(high_face, AXES, upward), lax.ppermute(low_face, AXES, downward)


def on_device(
    positions,
    particle_temp,
    pair_list,
    pair_count,
    ghost_particle,
    ghost_owner,
    ghost_cell,
    wall_seen,
    solid_temp,
    conduct,
):
    width = WIDTH
    depth, x_rows, span = solid_temp.shape
    particles = positions.shape[1]
    devices = lax.axis_size(AXES)
    ghosts = ghost_cell.shape[0]
    slots = max(2, 2 * ghosts // devices)
    sub_count = lax.axis_size("sub")
    lanes = span // SUB

    owner = ghost_owner.reshape(1, ghosts)
    own = pack(positions, particle_temp.reshape(1, particles))
    near = lax.ppermute(own, "sub", [(i, (i - 1) % sub_count) for i in range(sub_count)])

    rank, *made = prepare(own, owner, devices)

    low_face, high_face, *strips = rim(solid_temp, conduct, near, rank, width)
    low_c, high_c = between(low_face, high_face)

    particle_out, send = heat(
        pair_list.T,
        pair_count,
        own,
        near,
        made,
        ghost_particle.reshape(1, ghosts),
        owner,
        rank,
        ghost_cell.reshape(1, ghosts),
        wall_seen.reshape(1, ghosts),
        devices,
        slots,
    )
    received = lax.all_to_all(
        send.reshape(devices, 2 * slots), AXES, split_axis=0, concat_axis=0, tiled=True
    ).reshape(2 * devices, slots)
    source = surface_of(received, x_rows * SUB, lanes).reshape(x_rows, SUB, lanes)

    low_face, high_face = first_edge([low_face, high_face, low_c, high_c], strips, source, width, depth)
    low_s, high_s = low, high = between(low_face, high_face)
    temp, coef = spread(solid_temp, conduct, low_face)

    last = SUBSTEPS // width - 1
    inside = inner([temp], [low_c, high_c, coef, low_c, high_c, source, low_c, high_c], width, 0)
    own_rows = [low_face, inside, high_face]
    for turn in range(1, last):
        operands = [low, high, coef, low_c, high_c, source, low_s, high_s]
        low_face, high_face = edge(own_rows, operands, width, turn)
        inside = inner(own_rows, operands, width, turn)
        own_rows = [low_face, inside, high_face]
        low, high = between(low_face, high_face)
    staged, wall = middle(own_rows, [low_s, high_s, coef, low_c, high_c, source, low_s, high_s], width, last)
    operands = [low, high, coef, low_c, high_c, source, low_s, high_s]
    solid_out, wall = finish(own_rows, operands, staged, wall, width, last)
    answer = wall_of(received, wall.reshape(x_rows * SUB, lanes))
    returned = lax.all_to_all(answer, AXES, split_axis=0, concat_axis=0, tiled=True)
    ghost_temp = back_of(returned, owner, rank)
    return (particle_out.reshape(-1), solid_out, ghost_temp.reshape(-1))


def solution(mesh):
    placed = (
        P(None, AXES),
        P(AXES),
        P(AXES, None),
        P(AXES),
        P(AXES),
        P(AXES, None),
        P(AXES),
        P(AXES),
        P(None, AXES, None),
        P(None, AXES, None),
    )
    return jax.shard_map(
        on_device,
        mesh=mesh,
        in_specs=placed,
        out_specs=(P(AXES), P(None, AXES, None), P(AXES)),
        check_vma=False,
    )
```

```python
import functools

import jax
import jax.numpy as jnp
from jax import lax
from jax.experimental import pallas as pl
from jax.experimental.pallas import tpu as pltpu
from jax.sharding import PartitionSpec as P

TILE = 128
SUBSTEPS = 6
LANES = 128
SUB = 8
WIDTH = 2
FEATURES = 32
TOGETHER = 4
AXES = ("fluid", "sub")
MIB = 1 << 20

heat_rate = 0.004
wall_heat = 0.5

f32 = jnp.float32
bf16 = jnp.bfloat16
i32 = jnp.int32


def params(mib):
    return pltpu.CompilerParams(vmem_limit_bytes=mib * MIB)


def cost(flops, moved):
    return pl.CostEstimate(flops=int(flops), bytes_accessed=int(moved), transcendentals=0)


def vmem():
    return pl.BlockSpec(memory_space=pltpu.VMEM)


def hbm():
    return pl.BlockSpec(memory_space=pl.ANY)


def parts_of(value, count):
    parts = []
    for _ in range(count):
        part = value.astype(bf16).astype(f32)
        parts.append(part)
        value = value - part
    return parts


def dot(left, right):
    return lax.dot_general(left, right, (((1,), (0,)), ((), ())), preferred_element_type=f32)


def dot_lanes(left, right):
    return lax.dot_general(left, right, (((1,), (1,)), ((), ())), preferred_element_type=f32)


def sublane_is(row, count):
    return lax.broadcasted_iota(i32, (count, row.shape[1]), 0) == row


def z_sum(cur, lane_first, lane_last, sub_first, sub_last):
    left, right = cur[:, :LANES], cur[:, LANES:]
    left_up, right_up = pltpu.roll(left, 1, 1), pltpu.roll(right, 1, 1)
    left_down, right_down = pltpu.roll(left, LANES - 1, 1), pltpu.roll(right, LANES - 1, 1)
    carry_up = jnp.where(sub_first, 0.0, pltpu.roll(right_up, 1, 0))
    carry_down = jnp.where(sub_last, 0.0, pltpu.roll(left_down, SUB - 1, 0))
    first = jnp.where(lane_first, carry_up, left_up) + jnp.where(lane_last, right_down, left_down)
    second = jnp.where(lane_first, left_up, right_up) + jnp.where(lane_last, carry_down, right_down)
    return jnp.concatenate([first, second], axis=1)


def masks():
    lane = lax.broadcasted_iota(i32, (SUB, LANES), 1)
    sub = lax.broadcasted_iota(i32, (SUB, LANES), 0)
    return lane == 0, lane == LANES - 1, sub == 0, sub == SUB - 1


class Rows:
    def __init__(self, depth, *pieces):
        self.depth = depth
        self.pieces = pieces
        self.late = {}

    def find(self, row):
        for piece in self.pieces:
            if piece[0] <= row < piece[1]:
                return piece
        return None

    def tile(self, piece, row, layer):
        start, _, ref, base = piece
        if base is None:
            return ref[row - start, layer]
        value = ref[base + (row - start) * self.depth + layer]
        if layer == 0 and isinstance(row, int) and row in self.late:
            value = value + self.late[row]()
        return value


def sweep(temp, coef, source, start, stop, emit):
    depth = temp.depth

    def found_at(row):
        return temp.find(row - 1), temp.find(row), temp.find(row + 1), coef.find(row), source.find(row)

    def group(rows, found):
        marks = masks()
        count = len(rows)
        before = [None] * count
        cur = [temp.tile(found[i][1], rows[i], 0) for i in range(count)]
        for layer in range(depth):
            above = temp.tile(found[0][0], rows[0] - 1, layer)
            below = temp.tile(found[-1][2], rows[-1] + 1, layer)
            after = [None] * count
            if layer + 1 < depth:
                after = [temp.tile(found[i][1], rows[i], layer + 1) for i in range(count)]
            for i in range(count):
                up = above if i == 0 else cur[i - 1]
                down = below if i == count - 1 else cur[i + 1]
                total = up + down + z_sum(cur[i], *marks)
                for other in (before[i], after[i]):
                    if other is not None:
                        total = total + other
                value = cur[i] + coef.tile(found[i][3], rows[i], layer) * (total - 6.0 * cur[i])
                if layer == 0 and found[i][4] is not None:
                    value = value + source.tile(found[i][4], rows[i], 0)
                emit(rows[i], layer, value)
            before, cur = cur, after

    def run_of(row):
        end = row
        while end < stop and found_at(end) == found_at(row):
            end += 1
        return end - row

    row = start
    while row < stop:
        groups = run_of(row) // TOGETHER
        if groups > 1:
            found = [found_at(row)] * TOGETHER

            def body(number, carry, first=row, found=found):
                group([first + number * TOGETHER + i for i in range(TOGETHER)], found)
                return carry

            lax.fori_loop(0, groups, body, 0)
            row += groups * TOGETHER
            continue
        end = row + 1
        while end < min(stop, row + TOGETHER) and run_of(end) < 2 * TOGETHER:
            end += 1
        group(list(range(row, end)), [found_at(at) for at in range(row, end)])
        row = end


def several(temp, coef, source, width, start, stop, mids, emit, done=None):
    for step in range(1, width):
        first, last = start - (width - step), stop + (width - step)
        mid = mids[(step - 1) % len(mids)]

        def keep(row, layer, value, mid=mid, first=first):
            mid[row - first, layer] = value

        sweep(temp, coef, source, first, last, keep)
        temp = Rows(temp.depth, (first, last, mid, None))
    if done is None:
        sweep(temp, coef, source, start, stop, emit)
        return
    for row in range(start, stop, SUB):
        sweep(temp, coef, source, row, row + SUB, emit)
        done(row + SUB)


def mids_for(width, rows, depth, lanes):
    return [pltpu.VMEM((max(rows, 1), depth, SUB, lanes), f32) for _ in range(min(2, width - 1))]


def raw_rows(value):
    depth, x_rows, span = value.shape
    value = value.reshape(depth, x_rows // SUB, SUB, span // LANES, LANES)
    return value.transpose(0, 1, 3, 2, 4).reshape(depth * x_rows // SUB, span // LANES * SUB, LANES)


def chunk_copies(number, layers, groups, pairs, sems):
    at = pl.ds(number * layers * groups, layers * groups)
    return [
        pltpu.make_async_copy(source.at[at], buf.at[at], sems.at[which, number])
        for which, (source, buf) in enumerate(pairs)
    ]


def taken(ref, layer, row, groups):
    halves = ref.shape[1] // (SUB * SUB)
    group = layer * groups + row // SUB
    found = [ref[group, pl.ds(half * SUB + row % SUB, SUB, stride=SUB * halves), :] for half in range(halves)]
    return jnp.concatenate(found, axis=1)


def rim_kernel(
    width, x_rows, layers, temp_in, coef_in, _, __, low_out, high_out, low_strip, high_strip, temp_buf, coef_buf, sems
):
    groups = x_rows // SUB
    depth = temp_in.shape[0] // groups
    chunks = depth // layers
    pairs = ((temp_in, temp_buf), (coef_in, coef_buf))
    for number in range(chunks):
        for copy in chunk_copies(number, layers, groups, pairs, sems):
            copy.start()

    for number in range(chunks):
        for copy in chunk_copies(number, layers, groups, pairs, sems):
            copy.wait()
        for step in range(layers):
            layer = number * layers + step
            for ref, upward in ((low_out, False), (high_out, True)):
                for dist in range(1, width + 1):
                    row = x_rows - dist if upward else dist - 1
                    place = width - dist if upward else dist - 1
                    ref[place * depth + layer] = taken(temp_buf, layer, row, groups)
                    if dist < width:
                        place = width - 1 - dist if upward else dist - 1
                        ref[(width + place) * depth + layer] = taken(coef_buf, layer, row, groups)
            for ref, first in ((low_strip, width), (high_strip, x_rows - 2 * width)):
                shift = -1 if first == width else 1
                for place in range(width):
                    ref[place * depth + layer] = taken(temp_buf, layer, first + place, groups)
                    ref[(width + place) * depth + layer] = taken(coef_buf, layer, first + shift + place, groups)


def rim(temp, coef, after, also, width):
    depth, x_rows, span = temp.shape
    layers = 4
    face = jax.ShapeDtypeStruct(((2 * width - 1) * depth, SUB, span // SUB), f32)
    strip = jax.ShapeDtypeStruct((2 * width * depth, SUB, span // SUB), f32)
    raw = pltpu.VMEM((depth * x_rows // SUB, span // LANES * SUB, LANES), f32)
    return pl.pallas_call(
        functools.partial(rim_kernel, width, x_rows, layers),
        in_specs=[hbm()] * 4,
        out_specs=[vmem()] * 4,
        out_shape=[face, face, strip, strip],
        scratch_shapes=[raw, raw, pltpu.SemaphoreType.DMA((2, depth // layers))],
        compiler_params=params(52),
        cost_estimate=cost(1e6, 10 * MIB),
        name="rim",
    )(raw_rows(temp), raw_rows(coef), after, also)


def spread_kernel(layers, temp_in, coef_in, _, temp_out, coef_out, temp_buf, coef_buf, sems):
    x_rows, depth = temp_out.shape[:2]
    groups = x_rows // SUB
    chunks = depth // layers
    pairs = ((temp_in, temp_buf), (coef_in, coef_buf))
    for number in range(chunks):
        for copy in chunk_copies(number, layers, groups, pairs, sems):
            copy.start()

    for number in range(chunks):
        for copy in chunk_copies(number, layers, groups, pairs, sems):
            copy.wait()
        for step in range(layers):
            layer = number * layers + step
            for row in range(x_rows):
                temp_out[row, layer] = taken(temp_buf, layer, row, groups)
                coef_out[row, layer] = taken(coef_buf, layer, row, groups)


def spread(temp, coef, after):
    depth, x_rows, span = temp.shape
    layers = 4
    form = jax.ShapeDtypeStruct((x_rows, depth, SUB, span // SUB), f32)
    raw = pltpu.VMEM((depth * x_rows // SUB, span // LANES * SUB, LANES), f32)
    return pl.pallas_call(
        functools.partial(spread_kernel, layers),
        in_specs=[hbm()] * 3,
        out_specs=[vmem()] * 2,
        out_shape=[form, form],
        scratch_shapes=[raw, raw, pltpu.SemaphoreType.DMA((2, depth // layers))],
        compiler_params=params(44),
        cost_estimate=cost(1e6, 16 * MIB),
        name="spread",
    )(raw_rows(temp), raw_rows(coef), after)


def plate_rows(refs, x_rows, depth, width):
    if len(refs) == 1:
        return [(0, x_rows, refs[0], None)]
    low, inner, high = refs
    return [(0, width, low, 0), (width, x_rows - width, inner, None), (x_rows - width, x_rows, high, 0)]


def coef_rows(coef, low_c, high_c, width):
    x_rows, depth = coef.shape[:2]
    base = width * depth
    return Rows(
        depth,
        (1 - width, 0, low_c, base),
        (0, x_rows, coef, None),
        (x_rows, x_rows + width - 1, high_c, base),
    )


def plate(refs, owned, width, turn):
    own, refs = refs[:owned], refs[owned:]
    low, high, coef, low_c, high_c, source, low_s, high_s = refs[:8]
    x_rows, depth = coef.shape[:2]
    temp = Rows(
        depth,
        (-width, 0, low, 0),
        *plate_rows(own, x_rows, depth, width),
        (x_rows, x_rows + width, high, 0),
    )
    scale = coef_rows(coef, low_c, high_c, width)
    base = width * depth
    pieces = [(0, x_rows, source, 0)]
    if turn > 0:
        pieces += [(-1, 0, low_s, base), (x_rows, x_rows + 1, high_s, base)]
    heat_in = Rows(1, *pieces)
    if turn == 1 and width == 2:
        for row, other in ((0, -1), (-1, 0), (x_rows - 1, x_rows), (x_rows, x_rows - 1)):

            def missing(row=row, other=other):
                return scale.tile(scale.find(row), row, 0) * heat_in.tile(heat_in.find(other), other, 0)

            temp.late[row] = missing
    return temp, scale, heat_in, refs[8:]


def edge_faces(temp, scale, heat_in, width, x_rows, low_out, high_out, mids):
    depth = temp.depth
    for out, start in ((low_out, 0), (high_out, x_rows - width)):

        def emit(row, layer, value, out=out, start=start):
            out[(row - start) * depth + layer] = value

        several(temp, scale, heat_in, width, start, start + width, mids, emit)


def first_edge_kernel(
    width, depth, low, high, low_c, high_c, low_strip, high_strip, source, low_out, high_out, *mids
):
    x_rows = source.shape[0]
    base = width * depth
    temp = Rows(
        depth,
        (-width, 0, low_c, 0),
        (0, width, low, 0),
        (width, 2 * width, low_strip, 0),
        (x_rows - 2 * width, x_rows - width, high_strip, 0),
        (x_rows - width, x_rows, high, 0),
        (x_rows, x_rows + width, high_c, 0),
    )
    scale = Rows(
        depth,
        (1 - width, 0, low_c, base),
        (0, width - 1, low, base),
        (width - 1, 2 * width - 1, low_strip, base),
        (x_rows - 2 * width + 1, x_rows - width + 1, high_strip, base),
        (x_rows - width + 1, x_rows, high, base),
        (x_rows, x_rows + width - 1, high_c, base),
    )
    heat_in = Rows(1, (0, x_rows, source, 0))
    edge_faces(temp, scale, heat_in, width, x_rows, low_out, high_out, mids)
    low_out[base] = source[0]
    high_out[base] = source[x_rows - 1]


def first_edge(faces, strips, source, width, depth):
    lanes = source.shape[2]
    face = jax.ShapeDtypeStruct((width * depth + 1, SUB, lanes), f32)
    return pl.pallas_call(
        functools.partial(first_edge_kernel, width, depth),
        in_specs=[vmem()] * 7,
        out_specs=[vmem()] * 2,
        out_shape=[face, face],
        scratch_shapes=mids_for(width, 3 * width - 2, depth, lanes),
        compiler_params=params(16),
        cost_estimate=cost(12 * 12 * depth * SUB * lanes, 4 * MIB),
        name="edge",
    )(*faces, *strips, source)


def edge_kernel(width, owned, turn, *refs):
    temp, scale, heat_in, (low_out, high_out, *mids) = plate(refs, owned, width, turn)
    edge_faces(temp, scale, heat_in, width, refs[owned + 5].shape[0], low_out, high_out, mids)


def edge(own, operands, width, turn):
    coef = operands[2]
    _, depth, _, lanes = coef.shape
    face = jax.ShapeDtypeStruct((width * depth, SUB, lanes), f32)
    return pl.pallas_call(
        functools.partial(edge_kernel, width, len(own), turn),
        in_specs=[vmem()] * (len(own) + len(operands)),
        out_specs=[vmem()] * 2,
        out_shape=[face, face],
        scratch_shapes=mids_for(width, 3 * width - 2, depth, lanes),
        compiler_params=params(16),
        cost_estimate=cost(12 * 12 * depth * SUB * lanes, 4 * MIB),
        name="edge",
    )(*own, *operands)


def inner_kernel(width, owned, turn, *refs):
    temp, scale, heat_in, (out, *mids) = plate(refs, owned, width, turn)
    x_rows = refs[owned + 5].shape[0]

    def emit(row, layer, value):
        out[row - width, layer] = value

    several(temp, scale, heat_in, width, width, x_rows - width, mids, emit)


def inner(own, operands, width, turn):
    coef = operands[2]
    x_rows, depth, _, lanes = coef.shape
    return pl.pallas_call(
        functools.partial(inner_kernel, width, len(own), turn),
        in_specs=[vmem()] * (len(own) + len(operands)),
        out_specs=vmem(),
        out_shape=jax.ShapeDtypeStruct((x_rows - 2 * width, depth, SUB, lanes), f32),
        scratch_shapes=mids_for(width, x_rows - 2, depth, lanes),
        compiler_params=params(16),
        cost_estimate=cost(12 * 26 * depth * SUB * lanes, 12 * MIB),
        name="inner",
    )(*own, *operands)


def lay_out(staged, wall, halves):
    def emit(row, layer, value):
        if layer == 0:
            wall[row] = value
        group, place = row // SUB, row % SUB
        for half in range(halves):
            staged[layer, group, pl.ds(half * SUB + place, SUB, stride=SUB * halves), :] = value[
                :, half * LANES : (half + 1) * LANES
            ]

    return emit


def middle_kernel(width, owned, turn, *refs):
    temp, scale, heat_in, (staged, wall, *mids) = plate(refs, owned, width, turn)
    x_rows = wall.shape[0]
    emit = lay_out(staged, wall, wall.shape[2] // LANES)
    several(temp, scale, heat_in, width, width, x_rows - width, mids, emit)


def plate_form(coef):
    x_rows, depth, _, lanes = coef.shape
    return [
        jax.ShapeDtypeStruct((depth, x_rows // SUB, lanes // LANES * SUB * SUB, LANES), f32),
        jax.ShapeDtypeStruct((x_rows, SUB, lanes), f32),
    ]


def middle(own, operands, width, turn):
    coef = operands[2]
    x_rows, depth, _, lanes = coef.shape
    return pl.pallas_call(
        functools.partial(middle_kernel, width, len(own), turn),
        in_specs=[vmem()] * (len(own) + len(operands)),
        out_specs=[vmem()] * 2,
        out_shape=plate_form(coef),
        scratch_shapes=mids_for(width, x_rows - 2, depth, lanes),
        compiler_params=params(16),
        cost_estimate=cost(12 * 26 * depth * SUB * lanes, 12 * MIB),
        name="middle",
    )(*own, *operands)


def finish_kernel(width, owned, turn, *refs):
    temp, scale, heat_in, rest = plate(refs, owned, width, turn)
    _, _, out, staged, wall, out_sem, *mids = rest
    x_rows = wall.shape[0]
    depth = temp.depth
    put = lay_out(staged, wall, wall.shape[2] // LANES)
    groups = x_rows // SUB
    piece = depth // 4

    def copy_of(group, start, count, sem):
        at = pl.ds(start, count)
        return pltpu.make_async_copy(staged.at[at, group], out.at[at, group], out_sem.at[sem])

    copies = [copy_of(group, 0, depth, group) for group in range(groups - 1)]
    ends = [copy_of(groups - 1, start * piece, piece, groups + start) for start in range(4)]

    def emit(row, layer, value):
        put(row, layer, value)
        if row == x_rows - 1 and (layer + 1) % piece == 0:
            ends[layer // piece].start()

    for copy in copies[1:]:
        copy.start()
    several(temp, scale, heat_in, width, 0, width, mids, put)
    for copy in copies[:1]:
        copy.start()
    several(temp, scale, heat_in, width, x_rows - width, x_rows, mids, emit)
    for copy in copies + ends:
        copy.wait()


def finish(own, operands, staged, wall, width, turn):
    coef = operands[2]
    x_rows, depth, _, lanes = coef.shape
    count = len(own) + len(operands)
    form = plate_form(coef)
    out, _, wall = pl.pallas_call(
        functools.partial(finish_kernel, width, len(own), turn),
        in_specs=[vmem()] * (count + 2),
        out_specs=[hbm(), vmem(), vmem()],
        out_shape=[form[0], *form],
        scratch_shapes=[pltpu.SemaphoreType.DMA((x_rows // SUB + 4,))] + mids_for(width, 3 * width - 2, depth, lanes),
        input_output_aliases={count: 1, count + 1: 2},
        compiler_params=params(16),
        cost_estimate=cost(12 * 12 * depth * SUB * lanes, 8 * MIB),
        name="finish",
    )(*own, *operands, staged, wall)
    span = lanes * SUB
    out = out.reshape(depth, x_rows // SUB, span // LANES, SUB, LANES).transpose(0, 1, 3, 2, 4)
    return out.reshape(depth, x_rows, span), wall


def pack_kernel(far_pos, far_temps, own_ref, positions, temps, sems):
    copies = [
        pltpu.make_async_copy(far_pos, positions, sems.at[0]),
        pltpu.make_async_copy(far_temps, temps, sems.at[1]),
    ]
    for copy in copies:
        copy.start()
    for copy in copies:
        copy.wait()
    for tile in range(own_ref.shape[1]):
        at = slice(tile * TILE, (tile + 1) * TILE)
        for comp in range(3):
            own_ref[comp, tile : tile + 1, :] = positions[comp : comp + 1, at]
        own_ref[3, tile : tile + 1, :] = temps[:, at]


def pack(positions, temps):
    return pl.pallas_call(
        pack_kernel,
        in_specs=[hbm()] * 2,
        out_specs=vmem(),
        out_shape=jax.ShapeDtypeStruct((4, positions.shape[1] // TILE, TILE), f32),
        scratch_shapes=[
            pltpu.VMEM(positions.shape, f32),
            pltpu.VMEM(temps.shape, f32),
            pltpu.SemaphoreType.DMA((2,)),
        ],
        compiler_params=params(16),
        cost_estimate=cost(1e4, 1e5),
        name="pack",
    )(positions, temps)


def tables(ref, right, turned, warm, first_tile):
    tiles = ref.shape[1]
    comps = [ref[comp] for comp in range(3)]
    square = comps[0] * comps[0] + comps[1] * comps[1] + comps[2] * comps[2]
    rows = []
    for comp in comps:
        a, b, c = parts_of(comp, 3)
        rows += [2.0 * a, 2.0 * b, 2.0 * a, 2.0 * b, 2.0 * c, 2.0 * a]
    rows += [jnp.ones_like(square)] * 3 + parts_of(-square, 3)
    rows += [jnp.zeros_like(square)] * (FEATURES - len(rows))
    for number, row in enumerate(rows):
        right[pl.ds(number, tiles, stride=FEATURES), :] = row
    across = jnp.transpose(ref[3])
    for tile in range(tiles):
        warm[first_tile + tile] = jnp.broadcast_to(across[:, tile : tile + 1], (TILE, TILE))
        block = right[tile * FEATURES : (tile + 1) * FEATURES, :]
        turned[first_tile + tile] = jnp.transpose(block).astype(bf16)


def prepare_kernel(devices, own, owner_ref, rank_ref, left, turned, warm, plain):
    ghosts = owner_ref.shape[1]
    block = 256
    before = lax.broadcasted_iota(i32, (block, block), 0) < lax.broadcasted_iota(i32, (block, block), 1)
    ramp = before.astype(f32).astype(bf16)
    carried = jnp.zeros((devices, 1), f32)
    for start in range(0, ghosts, block):
        named = sublane_is(owner_ref[:, start : start + block], devices)
        ones = named.astype(f32)
        counted = dot(ones.astype(bf16), ramp) + carried
        rank = jnp.sum(jnp.where(named, counted, 0.0), axis=0, keepdims=True)
        rank_ref[:, start : start + block] = rank.astype(i32)
        carried = carried + jnp.sum(ones, axis=1, keepdims=True)

    tables(own, plain, turned, warm, 0)
    tiles = own.shape[1]
    comps = [own[comp] for comp in range(3)]
    square = comps[0] * comps[0] + comps[1] * comps[1] + comps[2] * comps[2]
    rows = []
    for comp in comps:
        a, b, c = parts_of(comp, 3)
        rows += [a, a, b, b, a, c]
    rows += parts_of(1.0 - square, 3) + [jnp.ones_like(square)] * 3
    rows += [jnp.zeros_like(square)] * (FEATURES - len(rows))
    for number, row in enumerate(rows):
        plain[pl.ds(number, tiles, stride=FEATURES), :] = row
    left[...] = plain[...].astype(bf16)


def prepare(own, owner, devices):
    tiles = own.shape[1]
    return pl.pallas_call(
        functools.partial(prepare_kernel, devices),
        in_specs=[vmem()] * 2,
        out_specs=[vmem()] * 4,
        out_shape=[
            jax.ShapeDtypeStruct(owner.shape, i32),
            jax.ShapeDtypeStruct((tiles * FEATURES, TILE), bf16),
            jax.ShapeDtypeStruct((tiles, TILE, FEATURES), bf16),
            jax.ShapeDtypeStruct((tiles, TILE, TILE), f32),
        ],
        scratch_shapes=[pltpu.VMEM((tiles * FEATURES, TILE), f32)],
        compiler_params=params(16),
        cost_estimate=cost(8e6, 2e6),
        name="prepare",
    )(own, owner)


def heat_kernel(
    devices,
    slots,
    together,
    pairs,
    live,
    own,
    near,
    left,
    own_turned,
    own_warm,
    particle,
    owner,
    rank,
    cell,
    seen,
    out,
    send,
    right,
    turned,
    warm,
    total,
):
    tiles = own.shape[1]
    turned[:tiles] = own_turned[...]
    warm[:tiles] = own_warm[...]
    tables(near, right, turned, warm, tiles)
    total[...] = jnp.zeros(total.shape, f32)

    def several_pairs(number, carry):
        found = []
        for step in range(together):
            at = number * together + step
            first, second = pairs[0, at], pairs[1, at]
            features = left[pl.ds(pl.multiple_of(first * FEATURES, FEATURES), FEATURES), :]
            inside = jnp.maximum(dot(turned[second], features), 0.0)
            gained = (inside * inside) * (warm[second] - own[3, pl.ds(first, 1), :])
            gained = jnp.sum(gained.reshape(TILE // SUB, SUB, TILE), axis=0)
            found.append((jnp.where(at < live[0], first, tiles), gained))
        for place, gained in found:
            total[place] += gained
        return carry

    lax.fori_loop(0, (live[0] + together - 1) // together, several_pairs, 0)
    out[...] = own[3] + heat_rate * jnp.sum(total[:tiles], axis=1)

    pieces = [part.astype(bf16) for part in parts_of(jnp.transpose(out[...]), 3)]
    table = jnp.concatenate(pieces, axis=1)
    ghosts = particle.shape[1]
    packed = [jnp.zeros((2 * devices, slots), f32) for _ in range(3)]
    block = 512
    for start in range(0, ghosts, block):
        at = slice(start, start + block)
        mirrored = particle[:, at]
        high = sublane_is(mirrored // TILE, tiles).astype(f32).astype(bf16)
        picked = dot(table, jnp.concatenate([high] * 3, axis=0))
        low = sublane_is(mirrored % TILE, TILE)
        value = jnp.sum(jnp.where(low, picked, 0.0), axis=0, keepdims=True)
        flux = wall_heat * (value - seen[:, at])
        cells = cell[:, at]
        cell_parts = [((cells // 256) * 256).astype(f32), (cells % 256).astype(f32), jnp.zeros_like(flux)]
        line = lax.broadcasted_iota(i32, (2 * devices, block), 0)
        named = line // 2 == owner[:, at]
        is_cell = line % 2 == 1
        slot = sublane_is(rank[:, at], slots).astype(f32).astype(bf16)
        for number, part in enumerate(parts_of(flux, 3)):
            chosen = jnp.where(named, jnp.where(is_cell, cell_parts[number], part), 0.0)
            packed[number] = packed[number] + dot_lanes(chosen.astype(bf16), slot)
    send[...] = packed[0] + packed[1] + packed[2]


def heat(pairs, live, own, near, made, particle, owner, rank, cell, seen, devices, slots):
    tiles = own.shape[1]
    together = 16 if pairs.shape[1] % 16 == 0 else 1
    smem = pl.BlockSpec(memory_space=pltpu.SMEM)
    return pl.pallas_call(
        functools.partial(heat_kernel, devices, slots, together),
        in_specs=[smem, smem] + [vmem()] * 10,
        out_specs=[vmem(), vmem()],
        out_shape=[
            jax.ShapeDtypeStruct((tiles, TILE), f32),
            jax.ShapeDtypeStruct((2 * devices, slots), f32),
        ],
        scratch_shapes=[
            pltpu.VMEM((tiles * FEATURES, TILE), f32),
            pltpu.VMEM((2 * tiles, TILE, FEATURES), bf16),
            pltpu.VMEM((2 * tiles, TILE, TILE), f32),
            pltpu.VMEM((tiles + 1, SUB, TILE), f32),
        ],
        compiler_params=params(16),
        cost_estimate=cost(12 * 4.2e6, 1 * MIB),
        name="heat",
    )(pairs, live, own, near, *made, particle, owner, rank, cell, seen)


def surface_kernel(received, _, out):
    devices = received.shape[0] // 2
    high_count, low_count = out.shape
    total = jnp.zeros((2 * high_count, low_count), f32)
    for device in range(devices):
        flux = received[2 * device : 2 * device + 1, :]
        cells = received[2 * device + 1 : 2 * device + 2, :].astype(i32)
        high = sublane_is(cells // low_count, high_count)
        low = sublane_is(cells % low_count, low_count).astype(f32).astype(bf16)
        chosen = [jnp.where(high, part, 0.0).astype(bf16) for part in parts_of(flux, 2)]
        total = total + dot_lanes(jnp.concatenate(chosen, axis=0), low)
    out[...] = (total[:high_count] + total[high_count:]) * (1.0 / SUBSTEPS)


def surface_of(received, after, high_count, low_count):
    return pl.pallas_call(
        surface_kernel,
        in_specs=[vmem(), hbm()],
        out_specs=vmem(),
        out_shape=jax.ShapeDtypeStruct((high_count, low_count), f32),
        compiler_params=params(16),
        cost_estimate=cost(6e7, 2e5),
        name="surface",
    )(received, after)


def wall_kernel(received, wall, out):
    devices = received.shape[0] // 2
    high_count, low_count = wall.shape
    pieces = [part.astype(bf16) for part in parts_of(jnp.transpose(wall[...]), 2)]
    table = jnp.concatenate(pieces, axis=1)
    for device in range(devices):
        cells = received[2 * device + 1 : 2 * device + 2, :].astype(i32)
        high = sublane_is(cells // low_count, high_count).astype(f32).astype(bf16)
        picked = dot(table, jnp.concatenate([high, high], axis=0))
        low = sublane_is(cells % low_count, low_count)
        out[device : device + 1, :] = jnp.sum(jnp.where(low, picked, 0.0), axis=0, keepdims=True)


def wall_of(received, wall):
    return pl.pallas_call(
        wall_kernel,
        in_specs=[vmem()] * 2,
        out_specs=vmem(),
        out_shape=jax.ShapeDtypeStruct((received.shape[0] // 2, received.shape[1]), f32),
        compiler_params=params(16),
        cost_estimate=cost(6e7, 2e5),
        name="wall",
    )(received, wall)


def back_kernel(returned, owner, rank, _, out):
    devices, slots = returned.shape
    pieces = [part.astype(bf16) for part in parts_of(jnp.transpose(returned[...]), 3)]
    table = jnp.concatenate(pieces, axis=1)
    block = 512
    for start in range(0, owner.shape[1], block):
        at = slice(start, start + block)
        named = sublane_is(owner[:, at], devices).astype(f32).astype(bf16)
        picked = dot(table, jnp.concatenate([named] * 3, axis=0))
        slot = sublane_is(rank[:, at], slots)
        out[:, at] = jnp.sum(jnp.where(slot, picked, 0.0), axis=0, keepdims=True)


def back_of(returned, owner, rank, after):
    return pl.pallas_call(
        back_kernel,
        in_specs=[vmem()] * 3 + [hbm()],
        out_specs=vmem(),
        out_shape=jax.ShapeDtypeStruct(owner.shape, f32),
        compiler_params=params(16),
        cost_estimate=cost(6e6, 1e5),
        name="back",
    )(returned, owner, rank, after)


def keep_kernel(value, _, out):
    out[...] = value[...]


def keep(value, after):
    return pl.pallas_call(
        keep_kernel,
        in_specs=[vmem(), hbm()],
        out_specs=vmem(),
        out_shape=jax.ShapeDtypeStruct(value.shape, value.dtype),
        compiler_params=params(16),
        cost_estimate=cost(1e5, 1e5),
        name="keep",
    )(value, after)


def between(low_face, high_face):
    count = lax.axis_size(AXES)
    upward = [(i, i + 1) for i in range(count - 1)]
    downward = [(target, source) for source, target in upward]
    return lax.ppermute(high_face, AXES, upward), lax.ppermute(low_face, AXES, downward)


def on_device(
    positions,
    particle_temp,
    pair_list,
    pair_count,
    ghost_particle,
    ghost_owner,
    ghost_cell,
    wall_seen,
    solid_temp,
    conduct,
):
    width = WIDTH
    depth, x_rows, span = solid_temp.shape
    particles = positions.shape[1]
    devices = lax.axis_size(AXES)
    ghosts = ghost_cell.shape[0]
    slots = max(2, 2 * ghosts // devices)
    sub_count = lax.axis_size("sub")
    lanes = span // SUB

    owner = ghost_owner.reshape(1, ghosts)
    own = pack(positions, particle_temp.reshape(1, particles))
    near = lax.ppermute(own, "sub", [(i, (i - 1) % sub_count) for i in range(sub_count)])

    rank, *made = prepare(own, owner, devices)

    low_face, high_face, *strips = rim(solid_temp, conduct, near, rank, width)
    low_c, high_c = between(low_face, high_face)

    particle_out, send = heat(
        pair_list.T,
        pair_count,
        own,
        near,
        made,
        ghost_particle.reshape(1, ghosts),
        owner,
        rank,
        ghost_cell.reshape(1, ghosts),
        wall_seen.reshape(1, ghosts),
        devices,
        slots,
    )
    received = lax.all_to_all(
        send.reshape(devices, 2 * slots), AXES, split_axis=0, concat_axis=0, tiled=True
    ).reshape(2 * devices, slots)
    rank = keep(rank, send)
    source = surface_of(received, rank, x_rows * SUB, lanes).reshape(x_rows, SUB, lanes)

    low_face, high_face = first_edge([low_face, high_face, low_c, high_c], strips, source, width, depth)
    low_s, high_s = low, high = between(low_face, high_face)
    temp, coef = spread(solid_temp, conduct, low_face)

    last = SUBSTEPS // width - 1
    inside = inner([temp], [low_c, high_c, coef, low_c, high_c, source, low_c, high_c], width, 0)
    own_rows = [low_face, inside, high_face]
    for turn in range(1, last):
        operands = [low, high, coef, low_c, high_c, source, low_s, high_s]
        low_face, high_face = edge(own_rows, operands, width, turn)
        inside = inner(own_rows, operands, width, turn)
        own_rows = [low_face, inside, high_face]
        low, high = between(low_face, high_face)
    staged, wall = middle(own_rows, [low_s, high_s, coef, low_c, high_c, source, low_s, high_s], width, last)
    operands = [low, high, coef, low_c, high_c, source, low_s, high_s]
    solid_out, wall = finish(own_rows, operands, staged, wall, width, last)
    answer = wall_of(received, wall.reshape(x_rows * SUB, lanes))
    returned = lax.all_to_all(answer, AXES, split_axis=0, concat_axis=0, tiled=True)
    particle_out = keep(particle_out, answer)
    ghost_temp = back_of(returned, owner, rank, particle_out)
    return (particle_out.reshape(-1), solid_out, ghost_temp.reshape(-1))


def solution(mesh):
    placed = (
        P(None, AXES),
        P(AXES),
        P(AXES, None),
        P(AXES),
        P(AXES),
        P(AXES, None),
        P(AXES),
        P(AXES),
        P(None, AXES, None),
        P(None, AXES, None),
    )
    return jax.shard_map(
        on_device,
        mesh=mesh,
        in_specs=placed,
        out_specs=(P(AXES), P(None, AXES, None), P(AXES)),
        check_vma=False,
    )
```

```python
import functools

import jax
import jax.numpy as jnp
from jax import lax
from jax.experimental import pallas as pl
from jax.experimental.pallas import tpu as pltpu
from jax.sharding import PartitionSpec as P

TILE = 128
SUBSTEPS = 6
LANES = 128
SUB = 8
WIDTH = 2
FEATURES = 32
TOGETHER = 4
AXES = ("fluid", "sub")
MIB = 1 << 20

heat_rate = 0.004
wall_heat = 0.5

f32 = jnp.float32
bf16 = jnp.bfloat16
i32 = jnp.int32


def params(mib):
    return pltpu.CompilerParams(vmem_limit_bytes=mib * MIB)


def cost(flops, moved):
    return pl.CostEstimate(flops=int(flops), bytes_accessed=int(moved), transcendentals=0)


def vmem():
    return pl.BlockSpec(memory_space=pltpu.VMEM)


def hbm():
    return pl.BlockSpec(memory_space=pl.ANY)


def parts_of(value, count):
    parts = []
    for _ in range(count):
        part = value.astype(bf16).astype(f32)
        parts.append(part)
        value = value - part
    return parts


def dot(left, right):
    return lax.dot_general(left, right, (((1,), (0,)), ((), ())), preferred_element_type=f32)


def dot_lanes(left, right):
    return lax.dot_general(left, right, (((1,), (1,)), ((), ())), preferred_element_type=f32)


def sublane_is(row, count):
    return lax.broadcasted_iota(i32, (count, row.shape[1]), 0) == row


def z_sum(cur, lane_first, lane_last, sub_first, sub_last):
    left, right = cur[:, :LANES], cur[:, LANES:]
    left_up, right_up = pltpu.roll(left, 1, 1), pltpu.roll(right, 1, 1)
    left_down, right_down = pltpu.roll(left, LANES - 1, 1), pltpu.roll(right, LANES - 1, 1)
    carry_up = jnp.where(sub_first, 0.0, pltpu.roll(right_up, 1, 0))
    carry_down = jnp.where(sub_last, 0.0, pltpu.roll(left_down, SUB - 1, 0))
    first = jnp.where(lane_first, carry_up, left_up) + jnp.where(lane_last, right_down, left_down)
    second = jnp.where(lane_first, left_up, right_up) + jnp.where(lane_last, carry_down, right_down)
    return jnp.concatenate([first, second], axis=1)


def masks():
    lane = lax.broadcasted_iota(i32, (SUB, LANES), 1)
    sub = lax.broadcasted_iota(i32, (SUB, LANES), 0)
    return lane == 0, lane == LANES - 1, sub == 0, sub == SUB - 1


class Rows:
    def __init__(self, depth, *pieces):
        self.depth = depth
        self.pieces = pieces
        self.late = {}

    def find(self, row):
        for piece in self.pieces:
            if piece[0] <= row < piece[1]:
                return piece
        return None

    def tile(self, piece, row, layer):
        start, _, ref, base = piece
        if base is None:
            return ref[row - start, layer]
        value = ref[base + (row - start) * self.depth + layer]
        if layer == 0 and isinstance(row, int) and row in self.late:
            value = value + self.late[row]()
        return value


def sweep(temp, coef, source, start, stop, emit):
    depth = temp.depth

    def found_at(row):
        return temp.find(row - 1), temp.find(row), temp.find(row + 1), coef.find(row), source.find(row)

    def group(rows, found):
        marks = masks()
        count = len(rows)
        before = [None] * count
        cur = [temp.tile(found[i][1], rows[i], 0) for i in range(count)]
        for layer in range(depth):
            above = temp.tile(found[0][0], rows[0] - 1, layer)
            below = temp.tile(found[-1][2], rows[-1] + 1, layer)
            after = [None] * count
            if layer + 1 < depth:
                after = [temp.tile(found[i][1], rows[i], layer + 1) for i in range(count)]
            for i in range(count):
                up = above if i == 0 else cur[i - 1]
                down = below if i == count - 1 else cur[i + 1]
                total = up + down + z_sum(cur[i], *marks)
                for other in (before[i], after[i]):
                    if other is not None:
                        total = total + other
                value = cur[i] + coef.tile(found[i][3], rows[i], layer) * (total - 6.0 * cur[i])
                if layer == 0 and found[i][4] is not None:
                    value = value + source.tile(found[i][4], rows[i], 0)
                emit(rows[i], layer, value)
            before, cur = cur, after

    def run_of(row):
        end = row
        while end < stop and found_at(end) == found_at(row):
            end += 1
        return end - row

    row = start
    while row < stop:
        groups = run_of(row) // TOGETHER
        if groups > 1:
            found = [found_at(row)] * TOGETHER

            def body(number, carry, first=row, found=found):
                group([first + number * TOGETHER + i for i in range(TOGETHER)], found)
                return carry

            lax.fori_loop(0, groups, body, 0)
            row += groups * TOGETHER
            continue
        end = row + 1
        while end < min(stop, row + TOGETHER) and run_of(end) < 2 * TOGETHER:
            end += 1
        group(list(range(row, end)), [found_at(at) for at in range(row, end)])
        row = end


def several(temp, coef, source, width, start, stop, mids, emit, done=None):
    for step in range(1, width):
        first, last = start - (width - step), stop + (width - step)
        mid = mids[(step - 1) % len(mids)]

        def keep(row, layer, value, mid=mid, first=first):
            mid[row - first, layer] = value

        sweep(temp, coef, source, first, last, keep)
        temp = Rows(temp.depth, (first, last, mid, None))
    if done is None:
        sweep(temp, coef, source, start, stop, emit)
        return
    for row in range(start, stop, SUB):
        sweep(temp, coef, source, row, row + SUB, emit)
        done(row + SUB)


def mids_for(width, rows, depth, lanes):
    return [pltpu.VMEM((max(rows, 1), depth, SUB, lanes), f32) for _ in range(min(2, width - 1))]


def raw_rows(value):
    depth, x_rows, span = value.shape
    value = value.reshape(depth, x_rows // SUB, SUB, span // LANES, LANES)
    return value.transpose(0, 1, 3, 2, 4).reshape(depth * x_rows // SUB, span // LANES * SUB, LANES)


def chunk_copies(number, layers, groups, pairs, sems):
    at = pl.ds(number * layers * groups, layers * groups)
    return [
        pltpu.make_async_copy(source.at[at], buf.at[at], sems.at[which, number])
        for which, (source, buf) in enumerate(pairs)
    ]


def taken(ref, layer, row, groups):
    halves = ref.shape[1] // (SUB * SUB)
    group = layer * groups + row // SUB
    found = [ref[group, pl.ds(half * SUB + row % SUB, SUB, stride=SUB * halves), :] for half in range(halves)]
    return jnp.concatenate(found, axis=1)


def rim_kernel(
    width, x_rows, layers, temp_in, coef_in, _, __, ___, low_out, high_out, low_strip, high_strip, temp_buf, coef_buf, sems
):
    groups = x_rows // SUB
    depth = temp_in.shape[0] // groups
    chunks = depth // layers
    pairs = ((temp_in, temp_buf), (coef_in, coef_buf))
    for number in range(chunks):
        for copy in chunk_copies(number, layers, groups, pairs, sems):
            copy.start()

    for number in range(chunks):
        for copy in chunk_copies(number, layers, groups, pairs, sems):
            copy.wait()
        for step in range(layers):
            layer = number * layers + step
            for ref, upward in ((low_out, False), (high_out, True)):
                for dist in range(1, width + 1):
                    row = x_rows - dist if upward else dist - 1
                    place = width - dist if upward else dist - 1
                    ref[place * depth + layer] = taken(temp_buf, layer, row, groups)
                    if dist < width:
                        place = width - 1 - dist if upward else dist - 1
                        ref[(width + place) * depth + layer] = taken(coef_buf, layer, row, groups)
            for ref, first in ((low_strip, width), (high_strip, x_rows - 2 * width)):
                shift = -1 if first == width else 1
                for place in range(width):
                    ref[place * depth + layer] = taken(temp_buf, layer, first + place, groups)
                    ref[(width + place) * depth + layer] = taken(coef_buf, layer, first + shift + place, groups)


def rim(temp, coef, one, two, three, width):
    depth, x_rows, span = temp.shape
    layers = 4
    face = jax.ShapeDtypeStruct(((2 * width - 1) * depth, SUB, span // SUB), f32)
    strip = jax.ShapeDtypeStruct((2 * width * depth, SUB, span // SUB), f32)
    raw = pltpu.VMEM((depth * x_rows // SUB, span // LANES * SUB, LANES), f32)
    return pl.pallas_call(
        functools.partial(rim_kernel, width, x_rows, layers),
        in_specs=[hbm()] * 5,
        out_specs=[vmem()] * 4,
        out_shape=[face, face, strip, strip],
        scratch_shapes=[raw, raw, pltpu.SemaphoreType.DMA((2, depth // layers))],
        compiler_params=params(52),
        cost_estimate=cost(1e6, 10 * MIB),
        name="rim",
    )(raw_rows(temp), raw_rows(coef), one, two, three)


def spread_kernel(layers, temp_in, coef_in, _, temp_out, coef_out, temp_buf, coef_buf, sems):
    x_rows, depth = temp_out.shape[:2]
    groups = x_rows // SUB
    chunks = depth // layers
    pairs = ((temp_in, temp_buf), (coef_in, coef_buf))
    for number in range(chunks):
        for copy in chunk_copies(number, layers, groups, pairs, sems):
            copy.start()

    for number in range(chunks):
        for copy in chunk_copies(number, layers, groups, pairs, sems):
            copy.wait()
        for step in range(layers):
            layer = number * layers + step
            for row in range(x_rows):
                temp_out[row, layer] = taken(temp_buf, layer, row, groups)
                coef_out[row, layer] = taken(coef_buf, layer, row, groups)


def spread(temp, coef, after):
    depth, x_rows, span = temp.shape
    layers = 4
    form = jax.ShapeDtypeStruct((x_rows, depth, SUB, span // SUB), f32)
    raw = pltpu.VMEM((depth * x_rows // SUB, span // LANES * SUB, LANES), f32)
    return pl.pallas_call(
        functools.partial(spread_kernel, layers),
        in_specs=[hbm()] * 3,
        out_specs=[vmem()] * 2,
        out_shape=[form, form],
        scratch_shapes=[raw, raw, pltpu.SemaphoreType.DMA((2, depth // layers))],
        compiler_params=params(44),
        cost_estimate=cost(1e6, 16 * MIB),
        name="spread",
    )(raw_rows(temp), raw_rows(coef), after)


def plate_rows(refs, x_rows, depth, width):
    if len(refs) == 1:
        return [(0, x_rows, refs[0], None)]
    low, inner, high = refs
    return [(0, width, low, 0), (width, x_rows - width, inner, None), (x_rows - width, x_rows, high, 0)]


def coef_rows(coef, low_c, high_c, width):
    x_rows, depth = coef.shape[:2]
    base = width * depth
    return Rows(
        depth,
        (1 - width, 0, low_c, base),
        (0, x_rows, coef, None),
        (x_rows, x_rows + width - 1, high_c, base),
    )


def plate(refs, owned, width, turn):
    own, refs = refs[:owned], refs[owned:]
    low, high, coef, low_c, high_c, source, low_s, high_s = refs[:8]
    x_rows, depth = coef.shape[:2]
    temp = Rows(
        depth,
        (-width, 0, low, 0),
        *plate_rows(own, x_rows, depth, width),
        (x_rows, x_rows + width, high, 0),
    )
    scale = coef_rows(coef, low_c, high_c, width)
    base = width * depth
    pieces = [(0, x_rows, source, 0)]
    if turn > 0:
        pieces += [(-1, 0, low_s, base), (x_rows, x_rows + 1, high_s, base)]
    heat_in = Rows(1, *pieces)
    if turn == 1 and width == 2:
        for row, other in ((0, -1), (-1, 0), (x_rows - 1, x_rows), (x_rows, x_rows - 1)):

            def missing(row=row, other=other):
                return scale.tile(scale.find(row), row, 0) * heat_in.tile(heat_in.find(other), other, 0)

            temp.late[row] = missing
    return temp, scale, heat_in, refs[8:]


def edge_faces(temp, scale, heat_in, width, x_rows, low_out, high_out, mids):
    depth = temp.depth
    for out, start in ((low_out, 0), (high_out, x_rows - width)):

        def emit(row, layer, value, out=out, start=start):
            out[(row - start) * depth + layer] = value

        several(temp, scale, heat_in, width, start, start + width, mids, emit)


def first_edge_kernel(
    width, depth, low, high, low_c, high_c, low_strip, high_strip, source, low_out, high_out, *mids
):
    x_rows = source.shape[0]
    base = width * depth
    temp = Rows(
        depth,
        (-width, 0, low_c, 0),
        (0, width, low, 0),
        (width, 2 * width, low_strip, 0),
        (x_rows - 2 * width, x_rows - width, high_strip, 0),
        (x_rows - width, x_rows, high, 0),
        (x_rows, x_rows + width, high_c, 0),
    )
    scale = Rows(
        depth,
        (1 - width, 0, low_c, base),
        (0, width - 1, low, base),
        (width - 1, 2 * width - 1, low_strip, base),
        (x_rows - 2 * width + 1, x_rows - width + 1, high_strip, base),
        (x_rows - width + 1, x_rows, high, base),
        (x_rows, x_rows + width - 1, high_c, base),
    )
    heat_in = Rows(1, (0, x_rows, source, 0))
    edge_faces(temp, scale, heat_in, width, x_rows, low_out, high_out, mids)
    low_out[base] = source[0]
    high_out[base] = source[x_rows - 1]


def first_edge(faces, strips, source, width, depth):
    lanes = source.shape[2]
    face = jax.ShapeDtypeStruct((width * depth + 1, SUB, lanes), f32)
    return pl.pallas_call(
        functools.partial(first_edge_kernel, width, depth),
        in_specs=[vmem()] * 7,
        out_specs=[vmem()] * 2,
        out_shape=[face, face],
        scratch_shapes=mids_for(width, 3 * width - 2, depth, lanes),
        compiler_params=params(16),
        cost_estimate=cost(12 * 12 * depth * SUB * lanes, 4 * MIB),
        name="edge",
    )(*faces, *strips, source)


def edge_kernel(width, owned, turn, *refs):
    temp, scale, heat_in, (low_out, high_out, *mids) = plate(refs, owned, width, turn)
    edge_faces(temp, scale, heat_in, width, refs[owned + 5].shape[0], low_out, high_out, mids)


def edge(own, operands, width, turn):
    coef = operands[2]
    _, depth, _, lanes = coef.shape
    face = jax.ShapeDtypeStruct((width * depth, SUB, lanes), f32)
    return pl.pallas_call(
        functools.partial(edge_kernel, width, len(own), turn),
        in_specs=[vmem()] * (len(own) + len(operands)),
        out_specs=[vmem()] * 2,
        out_shape=[face, face],
        scratch_shapes=mids_for(width, 3 * width - 2, depth, lanes),
        compiler_params=params(16),
        cost_estimate=cost(12 * 12 * depth * SUB * lanes, 4 * MIB),
        name="edge",
    )(*own, *operands)


def inner_kernel(width, owned, turn, *refs):
    temp, scale, heat_in, (out, *mids) = plate(refs, owned, width, turn)
    x_rows = refs[owned + 5].shape[0]

    def emit(row, layer, value):
        out[row - width, layer] = value

    several(temp, scale, heat_in, width, width, x_rows - width, mids, emit)


def inner(own, operands, width, turn):
    coef = operands[2]
    x_rows, depth, _, lanes = coef.shape
    return pl.pallas_call(
        functools.partial(inner_kernel, width, len(own), turn),
        in_specs=[vmem()] * (len(own) + len(operands)),
        out_specs=vmem(),
        out_shape=jax.ShapeDtypeStruct((x_rows - 2 * width, depth, SUB, lanes), f32),
        scratch_shapes=mids_for(width, x_rows - 2, depth, lanes),
        compiler_params=params(16),
        cost_estimate=cost(12 * 26 * depth * SUB * lanes, 12 * MIB),
        name="inner",
    )(*own, *operands)


def lay_out(staged, wall, halves):
    def emit(row, layer, value):
        if layer == 0:
            wall[row] = value
        group, place = row // SUB, row % SUB
        for half in range(halves):
            staged[layer, group, pl.ds(half * SUB + place, SUB, stride=SUB * halves), :] = value[
                :, half * LANES : (half + 1) * LANES
            ]

    return emit


def middle_kernel(width, owned, turn, *refs):
    temp, scale, heat_in, (staged, wall, *mids) = plate(refs, owned, width, turn)
    x_rows = wall.shape[0]
    emit = lay_out(staged, wall, wall.shape[2] // LANES)
    several(temp, scale, heat_in, width, width, x_rows - width, mids, emit)


def plate_form(coef):
    x_rows, depth, _, lanes = coef.shape
    return [
        jax.ShapeDtypeStruct((depth, x_rows // SUB, lanes // LANES * SUB * SUB, LANES), f32),
        jax.ShapeDtypeStruct((x_rows, SUB, lanes), f32),
    ]


def middle(own, operands, width, turn):
    coef = operands[2]
    x_rows, depth, _, lanes = coef.shape
    return pl.pallas_call(
        functools.partial(middle_kernel, width, len(own), turn),
        in_specs=[vmem()] * (len(own) + len(operands)),
        out_specs=[vmem()] * 2,
        out_shape=plate_form(coef),
        scratch_shapes=mids_for(width, x_rows - 2, depth, lanes),
        compiler_params=params(16),
        cost_estimate=cost(12 * 26 * depth * SUB * lanes, 12 * MIB),
        name="middle",
    )(*own, *operands)


def finish_kernel(width, owned, turn, *refs):
    temp, scale, heat_in, rest = plate(refs, owned, width, turn)
    _, _, out, staged, wall, out_sem, *mids = rest
    x_rows = wall.shape[0]
    depth = temp.depth
    put = lay_out(staged, wall, wall.shape[2] // LANES)
    groups = x_rows // SUB
    piece = depth // 4

    def copy_of(group, start, count, sem):
        at = pl.ds(start, count)
        return pltpu.make_async_copy(staged.at[at, group], out.at[at, group], out_sem.at[sem])

    copies = [copy_of(group, 0, depth, group) for group in range(groups - 1)]
    ends = [copy_of(groups - 1, start * piece, piece, groups + start) for start in range(4)]

    def emit(row, layer, value):
        put(row, layer, value)
        if row == x_rows - 1 and (layer + 1) % piece == 0:
            ends[layer // piece].start()

    for copy in copies[1:]:
        copy.start()
    several(temp, scale, heat_in, width, 0, width, mids, put)
    for copy in copies[:1]:
        copy.start()
    several(temp, scale, heat_in, width, x_rows - width, x_rows, mids, emit)
    for copy in copies + ends:
        copy.wait()


def finish(own, operands, staged, wall, width, turn):
    coef = operands[2]
    x_rows, depth, _, lanes = coef.shape
    count = len(own) + len(operands)
    form = plate_form(coef)
    out, _, wall = pl.pallas_call(
        functools.partial(finish_kernel, width, len(own), turn),
        in_specs=[vmem()] * (count + 2),
        out_specs=[hbm(), vmem(), vmem()],
        out_shape=[form[0], *form],
        scratch_shapes=[pltpu.SemaphoreType.DMA((x_rows // SUB + 4,))] + mids_for(width, 3 * width - 2, depth, lanes),
        input_output_aliases={count: 1, count + 1: 2},
        compiler_params=params(16),
        cost_estimate=cost(12 * 12 * depth * SUB * lanes, 8 * MIB),
        name="finish",
    )(*own, *operands, staged, wall)
    span = lanes * SUB
    out = out.reshape(depth, x_rows // SUB, span // LANES, SUB, LANES).transpose(0, 1, 3, 2, 4)
    return out.reshape(depth, x_rows, span), wall


def gather_tiles(positions, temps, out):
    for tile in range(out.shape[1]):
        at = slice(tile * TILE, (tile + 1) * TILE)
        for comp in range(3):
            out[comp, tile : tile + 1, :] = positions[comp : comp + 1, at]
        out[3, tile : tile + 1, :] = temps[:, at]


def tables(ref, right, turned, warm, first_tile):
    tiles = ref.shape[1]
    comps = [ref[comp] for comp in range(3)]
    square = comps[0] * comps[0] + comps[1] * comps[1] + comps[2] * comps[2]
    rows = []
    for comp in comps:
        a, b, c = parts_of(comp, 3)
        rows += [2.0 * a, 2.0 * b, 2.0 * a, 2.0 * b, 2.0 * c, 2.0 * a]
    rows += [jnp.ones_like(square)] * 3 + parts_of(-square, 3)
    rows += [jnp.zeros_like(square)] * (FEATURES - len(rows))
    for number, row in enumerate(rows):
        right[pl.ds(number, tiles, stride=FEATURES), :] = row
    across = jnp.transpose(ref[3])
    for tile in range(tiles):
        warm[first_tile + tile] = jnp.broadcast_to(across[:, tile : tile + 1], (TILE, TILE))
        block = right[tile * FEATURES : (tile + 1) * FEATURES, :]
        turned[first_tile + tile] = jnp.transpose(block).astype(bf16)


def prepare_kernel(devices, positions, temps, owner_ref, own, rank_ref, left, turned, warm, plain):
    gather_tiles(positions, temps, own)
    ghosts = owner_ref.shape[1]
    block = 256
    before = lax.broadcasted_iota(i32, (block, block), 0) < lax.broadcasted_iota(i32, (block, block), 1)
    ramp = before.astype(f32).astype(bf16)
    carried = jnp.zeros((devices, 1), f32)
    for start in range(0, ghosts, block):
        named = sublane_is(owner_ref[:, start : start + block], devices)
        ones = named.astype(f32)
        counted = dot(ones.astype(bf16), ramp) + carried
        rank = jnp.sum(jnp.where(named, counted, 0.0), axis=0, keepdims=True)
        rank_ref[:, start : start + block] = rank.astype(i32)
        carried = carried + jnp.sum(ones, axis=1, keepdims=True)

    tables(own, plain, turned, warm, 0)
    tiles = own.shape[1]
    comps = [own[comp] for comp in range(3)]
    square = comps[0] * comps[0] + comps[1] * comps[1] + comps[2] * comps[2]
    rows = []
    for comp in comps:
        a, b, c = parts_of(comp, 3)
        rows += [a, a, b, b, a, c]
    rows += parts_of(1.0 - square, 3) + [jnp.ones_like(square)] * 3
    rows += [jnp.zeros_like(square)] * (FEATURES - len(rows))
    for number, row in enumerate(rows):
        plain[pl.ds(number, tiles, stride=FEATURES), :] = row
    left[...] = plain[...].astype(bf16)


def prepare(positions, temps, owner, devices):
    tiles = positions.shape[1] // TILE
    return pl.pallas_call(
        functools.partial(prepare_kernel, devices),
        in_specs=[vmem()] * 3,
        out_specs=[vmem()] * 5,
        out_shape=[
            jax.ShapeDtypeStruct((4, tiles, TILE), f32),
            jax.ShapeDtypeStruct(owner.shape, i32),
            jax.ShapeDtypeStruct((tiles * FEATURES, TILE), bf16),
            jax.ShapeDtypeStruct((tiles, TILE, FEATURES), bf16),
            jax.ShapeDtypeStruct((tiles, TILE, TILE), f32),
        ],
        scratch_shapes=[pltpu.VMEM((tiles * FEATURES, TILE), f32)],
        compiler_params=params(16),
        cost_estimate=cost(8e6, 2e6),
        name="prepare",
    )(positions, temps, owner)


def heat_kernel(
    devices,
    slots,
    together,
    far_pairs,
    live,
    own,
    near_pos,
    near_temps,
    left,
    own_turned,
    own_warm,
    particle,
    owner,
    rank,
    cell,
    seen,
    out,
    send,
    near,
    right,
    turned,
    warm,
    total,
    pairs,
    sem,
):
    tiles = own.shape[1]
    listed = pltpu.make_async_copy(far_pairs, pairs, sem)
    listed.start()
    gather_tiles(near_pos, near_temps, near)
    turned[:tiles] = own_turned[...]
    warm[:tiles] = own_warm[...]
    tables(near, right, turned, warm, tiles)
    total[...] = jnp.zeros(total.shape, f32)
    listed.wait()

    def several_pairs(number, carry):
        found = []
        for step in range(together):
            at = number * together + step
            first, second = pairs[0, at], pairs[1, at]
            features = left[pl.ds(pl.multiple_of(first * FEATURES, FEATURES), FEATURES), :]
            inside = jnp.maximum(dot(turned[second], features), 0.0)
            gained = (inside * inside) * (warm[second] - own[3, pl.ds(first, 1), :])
            gained = jnp.sum(gained.reshape(TILE // SUB, SUB, TILE), axis=0)
            found.append((jnp.where(at < live[0], first, tiles), gained))
        for place, gained in found:
            total[place] += gained
        return carry

    lax.fori_loop(0, (live[0] + together - 1) // together, several_pairs, 0)
    out[...] = own[3] + heat_rate * jnp.sum(total[:tiles], axis=1)

    pieces = [part.astype(bf16) for part in parts_of(jnp.transpose(out[...]), 3)]
    table = jnp.concatenate(pieces, axis=1)
    ghosts = particle.shape[1]
    packed = [jnp.zeros((2 * devices, slots), f32) for _ in range(3)]
    block = 512
    for start in range(0, ghosts, block):
        at = slice(start, start + block)
        mirrored = particle[:, at]
        high = sublane_is(mirrored // TILE, tiles).astype(f32).astype(bf16)
        picked = dot(table, jnp.concatenate([high] * 3, axis=0))
        low = sublane_is(mirrored % TILE, TILE)
        value = jnp.sum(jnp.where(low, picked, 0.0), axis=0, keepdims=True)
        flux = wall_heat * (value - seen[:, at])
        cells = cell[:, at]
        cell_parts = [((cells // 256) * 256).astype(f32), (cells % 256).astype(f32), jnp.zeros_like(flux)]
        line = lax.broadcasted_iota(i32, (2 * devices, block), 0)
        named = line // 2 == owner[:, at]
        is_cell = line % 2 == 1
        slot = sublane_is(rank[:, at], slots).astype(f32).astype(bf16)
        for number, part in enumerate(parts_of(flux, 3)):
            chosen = jnp.where(named, jnp.where(is_cell, cell_parts[number], part), 0.0)
            packed[number] = packed[number] + dot_lanes(chosen.astype(bf16), slot)
    send[...] = packed[0] + packed[1] + packed[2]


def heat(pairs, live, own, near_pos, near_temps, made, particle, owner, rank, cell, seen, devices, slots):
    tiles = own.shape[1]
    together = 16 if pairs.shape[1] % 16 == 0 else 1
    smem = pl.BlockSpec(memory_space=pltpu.SMEM)
    return pl.pallas_call(
        functools.partial(heat_kernel, devices, slots, together),
        in_specs=[hbm(), smem] + [vmem()] * 11,
        out_specs=[vmem(), vmem()],
        out_shape=[
            jax.ShapeDtypeStruct((tiles, TILE), f32),
            jax.ShapeDtypeStruct((2 * devices, slots), f32),
        ],
        scratch_shapes=[
            pltpu.VMEM((4, tiles, TILE), f32),
            pltpu.VMEM((tiles * FEATURES, TILE), f32),
            pltpu.VMEM((2 * tiles, TILE, FEATURES), bf16),
            pltpu.VMEM((2 * tiles, TILE, TILE), f32),
            pltpu.VMEM((tiles + 1, SUB, TILE), f32),
            pltpu.SMEM(pairs.shape, i32),
            pltpu.SemaphoreType.DMA,
        ],
        compiler_params=params(16),
        cost_estimate=cost(12 * 4.2e6, 1 * MIB),
        name="heat",
    )(pairs, live, own, near_pos, near_temps, *made, particle, owner, rank, cell, seen)


def ghost_lanes(received, first, count, comp):
    rows = [received[2 * device + comp : 2 * device + comp + 1, :] for device in range(first, first + count)]
    return rows[0] if count == 1 else jnp.concatenate(rows, axis=1)


def devices_together(devices, slots):
    return 2 if slots == LANES and devices % 2 == 0 else 1


def surface_kernel(received, out):
    devices = received.shape[0] // 2
    count = devices_together(devices, received.shape[1])
    high_count, low_count = out.shape
    total = jnp.zeros((2 * high_count, low_count), f32)
    for device in range(0, devices, count):
        flux = ghost_lanes(received, device, count, 0)
        cells = ghost_lanes(received, device, count, 1).astype(i32)
        high = sublane_is(cells // low_count, high_count)
        low = sublane_is(cells % low_count, low_count).astype(f32).astype(bf16)
        chosen = [jnp.where(high, part, 0.0).astype(bf16) for part in parts_of(flux, 2)]
        total = total + dot_lanes(jnp.concatenate(chosen, axis=0), low)
    out[...] = (total[:high_count] + total[high_count:]) * (1.0 / SUBSTEPS)


def surface_of(received, high_count, low_count):
    return pl.pallas_call(
        surface_kernel,
        in_specs=[vmem()],
        out_specs=vmem(),
        out_shape=jax.ShapeDtypeStruct((high_count, low_count), f32),
        compiler_params=params(16),
        cost_estimate=cost(6e7, 2e5),
        name="surface",
    )(received)


def wall_kernel(received, wall, out):
    devices = received.shape[0] // 2
    high_count, low_count = wall.shape
    pieces = [part.astype(bf16) for part in parts_of(jnp.transpose(wall[...]), 2)]
    table = jnp.concatenate(pieces, axis=1)
    slots = received.shape[1]
    count = devices_together(devices, slots)
    for device in range(0, devices, count):
        cells = ghost_lanes(received, device, count, 1).astype(i32)
        high = sublane_is(cells // low_count, high_count).astype(f32).astype(bf16)
        picked = dot(table, jnp.concatenate([high, high], axis=0))
        low = sublane_is(cells % low_count, low_count)
        found = jnp.sum(jnp.where(low, picked, 0.0), axis=0, keepdims=True)
        for number in range(count):
            out[device + number : device + number + 1, :] = found[:, number * slots : (number + 1) * slots]


def wall_of(received, wall):
    return pl.pallas_call(
        wall_kernel,
        in_specs=[vmem()] * 2,
        out_specs=vmem(),
        out_shape=jax.ShapeDtypeStruct((received.shape[0] // 2, received.shape[1]), f32),
        compiler_params=params(16),
        cost_estimate=cost(6e7, 2e5),
        name="wall",
    )(received, wall)


def back_kernel(returned, owner, rank, out):
    devices, slots = returned.shape
    pieces = [part.astype(bf16) for part in parts_of(jnp.transpose(returned[...]), 3)]
    table = jnp.concatenate(pieces, axis=1)
    block = 512
    for start in range(0, owner.shape[1], block):
        at = slice(start, start + block)
        named = sublane_is(owner[:, at], devices).astype(f32).astype(bf16)
        picked = dot(table, jnp.concatenate([named] * 3, axis=0))
        slot = sublane_is(rank[:, at], slots)
        out[:, at] = jnp.sum(jnp.where(slot, picked, 0.0), axis=0, keepdims=True)


def back_of(returned, owner, rank):
    return pl.pallas_call(
        back_kernel,
        in_specs=[vmem()] * 3,
        out_specs=vmem(),
        out_shape=jax.ShapeDtypeStruct(owner.shape, f32),
        compiler_params=params(16),
        cost_estimate=cost(6e6, 1e5),
        name="back",
    )(returned, owner, rank)


def between(low_face, high_face):
    count = lax.axis_size(AXES)
    upward = [(i, i + 1) for i in range(count - 1)]
    downward = [(target, source) for source, target in upward]
    return lax.ppermute(high_face, AXES, upward), lax.ppermute(low_face, AXES, downward)


def on_device(
    positions,
    particle_temp,
    pair_list,
    pair_count,
    ghost_particle,
    ghost_owner,
    ghost_cell,
    wall_seen,
    solid_temp,
    conduct,
):
    width = WIDTH
    depth, x_rows, span = solid_temp.shape
    particles = positions.shape[1]
    devices = lax.axis_size(AXES)
    ghosts = ghost_cell.shape[0]
    slots = max(2, 2 * ghosts // devices)
    sub_count = lax.axis_size("sub")
    lanes = span // SUB

    owner = ghost_owner.reshape(1, ghosts)
    temps = particle_temp.reshape(1, particles)
    backward = [(i, (i - 1) % sub_count) for i in range(sub_count)]
    near_pos = lax.ppermute(positions, "sub", backward)
    near_temps = lax.ppermute(temps, "sub", backward)
    own, rank, *made = prepare(positions, temps, owner, devices)

    low_face, high_face, *strips = rim(solid_temp, conduct, near_pos, near_temps, rank, width)
    low_c, high_c = between(low_face, high_face)

    particle_out, send = heat(
        pair_list.T,
        pair_count,
        own,
        near_pos,
        near_temps,
        made,
        ghost_particle.reshape(1, ghosts),
        owner,
        rank,
        ghost_cell.reshape(1, ghosts),
        wall_seen.reshape(1, ghosts),
        devices,
        slots,
    )
    received = lax.all_to_all(
        send.reshape(devices, 2 * slots), AXES, split_axis=0, concat_axis=0, tiled=True
    ).reshape(2 * devices, slots)
    source = surface_of(received, x_rows * SUB, lanes).reshape(x_rows, SUB, lanes)

    low_face, high_face = first_edge([low_face, high_face, low_c, high_c], strips, source, width, depth)
    low_s, high_s = low, high = between(low_face, high_face)
    temp, coef = spread(solid_temp, conduct, low_face)

    last = SUBSTEPS // width - 1
    inside = inner([temp], [low_c, high_c, coef, low_c, high_c, source, low_c, high_c], width, 0)
    own_rows = [low_face, inside, high_face]
    for turn in range(1, last):
        operands = [low, high, coef, low_c, high_c, source, low_s, high_s]
        low_face, high_face = edge(own_rows, operands, width, turn)
        inside = inner(own_rows, operands, width, turn)
        own_rows = [low_face, inside, high_face]
        low, high = between(low_face, high_face)
    staged, wall = middle(own_rows, [low_s, high_s, coef, low_c, high_c, source, low_s, high_s], width, last)
    operands = [low, high, coef, low_c, high_c, source, low_s, high_s]
    solid_out, wall = finish(own_rows, operands, staged, wall, width, last)
    answer = wall_of(received, wall.reshape(x_rows * SUB, lanes))
    returned = lax.all_to_all(answer, AXES, split_axis=0, concat_axis=0, tiled=True)
    ghost_temp = back_of(returned, owner, rank)
    return (particle_out.reshape(-1), solid_out, ghost_temp.reshape(-1))


def solution(mesh):
    placed = (
        P(None, AXES),
        P(AXES),
        P(AXES, None),
        P(AXES),
        P(AXES),
        P(AXES, None),
        P(AXES),
        P(AXES),
        P(None, AXES, None),
        P(None, AXES, None),
    )
    return jax.shard_map(
        on_device,
        mesh=mesh,
        in_specs=placed,
        out_specs=(P(AXES), P(None, AXES, None), P(AXES)),
        check_vma=False,
    )
```

```python
import functools

import jax
import jax.numpy as jnp
from jax import lax
from jax.experimental import pallas as pl
from jax.experimental.pallas import tpu as pltpu
from jax.sharding import PartitionSpec as P

TILE = 128
SUBSTEPS = 6
LANES = 128
SUB = 8
WIDTH = 2
FEATURES = 32
TOGETHER = 4
AXES = ("fluid", "sub")
MIB = 1 << 20

heat_rate = 0.004
wall_heat = 0.5

f32 = jnp.float32
bf16 = jnp.bfloat16
i32 = jnp.int32


def params(mib):
    return pltpu.CompilerParams(vmem_limit_bytes=mib * MIB)


def cost(flops, moved):
    return pl.CostEstimate(flops=int(flops), bytes_accessed=int(moved), transcendentals=0)


def vmem():
    return pl.BlockSpec(memory_space=pltpu.VMEM)


def hbm():
    return pl.BlockSpec(memory_space=pl.ANY)


def parts_of(value, count):
    parts = []
    for _ in range(count):
        part = value.astype(bf16).astype(f32)
        parts.append(part)
        value = value - part
    return parts


def dot(left, right):
    return lax.dot_general(left, right, (((1,), (0,)), ((), ())), preferred_element_type=f32)


def dot_lanes(left, right):
    return lax.dot_general(left, right, (((1,), (1,)), ((), ())), preferred_element_type=f32)


def sublane_is(row, count):
    return lax.broadcasted_iota(i32, (count, row.shape[1]), 0) == row


def z_sum(cur, lane_first, lane_last, sub_first, sub_last):
    left, right = cur[:, :LANES], cur[:, LANES:]
    left_up, right_up = pltpu.roll(left, 1, 1), pltpu.roll(right, 1, 1)
    left_down, right_down = pltpu.roll(left, LANES - 1, 1), pltpu.roll(right, LANES - 1, 1)
    carry_up = jnp.where(sub_first, 0.0, pltpu.roll(right_up, 1, 0))
    carry_down = jnp.where(sub_last, 0.0, pltpu.roll(left_down, SUB - 1, 0))
    first = jnp.where(lane_first, carry_up, left_up) + jnp.where(lane_last, right_down, left_down)
    second = jnp.where(lane_first, left_up, right_up) + jnp.where(lane_last, carry_down, right_down)
    return jnp.concatenate([first, second], axis=1)


def masks():
    lane = lax.broadcasted_iota(i32, (SUB, LANES), 1)
    sub = lax.broadcasted_iota(i32, (SUB, LANES), 0)
    return lane == 0, lane == LANES - 1, sub == 0, sub == SUB - 1


class Rows:
    def __init__(self, depth, *pieces):
        self.depth = depth
        self.pieces = pieces
        self.late = {}

    def find(self, row):
        for piece in self.pieces:
            if piece[0] <= row < piece[1]:
                return piece
        return None

    def tile(self, piece, row, layer):
        start, _, ref, base = piece
        if base is None:
            return ref[row - start, layer]
        value = ref[base + (row - start) * self.depth + layer]
        if layer == 0 and isinstance(row, int) and row in self.late:
            value = value + self.late[row]()
        return value


def sweep(temp, coef, source, start, stop, emit):
    depth = temp.depth

    def found_at(row):
        return temp.find(row - 1), temp.find(row), temp.find(row + 1), coef.find(row), source.find(row)

    def group(rows, found):
        marks = masks()
        count = len(rows)
        before = [None] * count
        cur = [temp.tile(found[i][1], rows[i], 0) for i in range(count)]
        for layer in range(depth):
            above = temp.tile(found[0][0], rows[0] - 1, layer)
            below = temp.tile(found[-1][2], rows[-1] + 1, layer)
            after = [None] * count
            if layer + 1 < depth:
                after = [temp.tile(found[i][1], rows[i], layer + 1) for i in range(count)]
            for i in range(count):
                up = above if i == 0 else cur[i - 1]
                down = below if i == count - 1 else cur[i + 1]
                total = up + down + z_sum(cur[i], *marks)
                for other in (before[i], after[i]):
                    if other is not None:
                        total = total + other
                value = cur[i] + coef.tile(found[i][3], rows[i], layer) * (total - 6.0 * cur[i])
                if layer == 0 and found[i][4] is not None:
                    value = value + source.tile(found[i][4], rows[i], 0)
                emit(rows[i], layer, value)
            before, cur = cur, after

    def run_of(row):
        end = row
        while end < stop and found_at(end) == found_at(row):
            end += 1
        return end - row

    row = start
    while row < stop:
        groups = run_of(row) // TOGETHER
        if groups > 1:
            found = [found_at(row)] * TOGETHER

            def body(number, carry, first=row, found=found):
                group([first + number * TOGETHER + i for i in range(TOGETHER)], found)
                return carry

            lax.fori_loop(0, groups, body, 0)
            row += groups * TOGETHER
            continue
        end = row + 1
        while end < min(stop, row + TOGETHER) and run_of(end) < 2 * TOGETHER:
            end += 1
        group(list(range(row, end)), [found_at(at) for at in range(row, end)])
        row = end


def several(temp, coef, source, width, start, stop, mids, emit, done=None):
    for step in range(1, width):
        first, last = start - (width - step), stop + (width - step)
        mid = mids[(step - 1) % len(mids)]

        def keep(row, layer, value, mid=mid, first=first):
            mid[row - first, layer] = value

        sweep(temp, coef, source, first, last, keep)
        temp = Rows(temp.depth, (first, last, mid, None))
    if done is None:
        sweep(temp, coef, source, start, stop, emit)
        return
    for row in range(start, stop, SUB):
        sweep(temp, coef, source, row, row + SUB, emit)
        done(row + SUB)


def mids_for(width, rows, depth, lanes):
    return [pltpu.VMEM((max(rows, 1), depth, SUB, lanes), f32) for _ in range(min(2, width - 1))]


def raw_rows(value):
    depth, x_rows, span = value.shape
    value = value.reshape(depth, x_rows // SUB, SUB, span // LANES, LANES)
    return value.transpose(0, 1, 3, 2, 4).reshape(depth * x_rows // SUB, span // LANES * SUB, LANES)


def chunk_copies(number, layers, groups, pairs, sems):
    at = pl.ds(number * layers * groups, layers * groups)
    return [
        pltpu.make_async_copy(source.at[at], buf.at[at], sems.at[which, number])
        for which, (source, buf) in enumerate(pairs)
    ]


def taken(ref, layer, row, groups):
    halves = ref.shape[1] // (SUB * SUB)
    group = layer * groups + row // SUB
    found = [ref[group, pl.ds(half * SUB + row % SUB, SUB, stride=SUB * halves), :] for half in range(halves)]
    return jnp.concatenate(found, axis=1)


def rim_kernel(
    width, x_rows, layers, temp_in, coef_in, _, __, low_out, high_out, far_strip, strip, temp_buf, coef_buf, sems, out_sems
):
    groups = x_rows // SUB
    depth = temp_in.shape[0] // groups
    chunks = depth // layers
    pairs = ((temp_in, temp_buf), (coef_in, coef_buf))

    def strips(number):
        at = pl.ds(number * layers, layers)
        return pltpu.make_async_copy(strip.at[:, at], far_strip.at[:, at], out_sems.at[number])

    for number in range(chunks):
        for copy in chunk_copies(number, layers, groups, pairs, sems):
            copy.start()

    for number in range(chunks):
        for copy in chunk_copies(number, layers, groups, pairs, sems):
            copy.wait()
        for step in range(layers):
            layer = number * layers + step
            for ref, upward in ((low_out, False), (high_out, True)):
                for dist in range(1, width + 1):
                    row = x_rows - dist if upward else dist - 1
                    place = width - dist if upward else dist - 1
                    ref[place * depth + layer] = taken(temp_buf, layer, row, groups)
                    if dist < width:
                        place = width - 1 - dist if upward else dist - 1
                        ref[(width + place) * depth + layer] = taken(coef_buf, layer, row, groups)
            for base, first, shift in ((0, width, -1), (2 * width, x_rows - 2 * width, 1)):
                for place in range(width):
                    strip[base + place, layer] = taken(temp_buf, layer, first + place, groups)
                    strip[base + width + place, layer] = taken(coef_buf, layer, first + shift + place, groups)
        strips(number).start()
    for number in range(chunks):
        strips(number).wait()


def rim(temp, coef, one, two, width):
    depth, x_rows, span = temp.shape
    layers = 4
    face = jax.ShapeDtypeStruct(((2 * width - 1) * depth, SUB, span // SUB), f32)
    strip = (4 * width, depth, SUB, span // SUB)
    raw = pltpu.VMEM((depth * x_rows // SUB, span // LANES * SUB, LANES), f32)
    return pl.pallas_call(
        functools.partial(rim_kernel, width, x_rows, layers),
        in_specs=[hbm()] * 4,
        out_specs=[vmem()] * 2 + [hbm()],
        out_shape=[face, face, jax.ShapeDtypeStruct(strip, f32)],
        scratch_shapes=[pltpu.VMEM(strip, f32), raw, raw]
        + [pltpu.SemaphoreType.DMA((2, depth // layers)), pltpu.SemaphoreType.DMA((depth // layers,))],
        compiler_params=params(52),
        cost_estimate=cost(1e6, 10 * MIB),
        name="rim",
    )(raw_rows(temp), raw_rows(coef), one, two)


def spread_kernel(layers, temp_in, coef_in, _, temp_out, coef_out, temp_buf, coef_buf, sems):
    x_rows, depth = temp_out.shape[:2]
    groups = x_rows // SUB
    chunks = depth // layers
    pairs = ((temp_in, temp_buf), (coef_in, coef_buf))
    for number in range(chunks):
        for copy in chunk_copies(number, layers, groups, pairs, sems):
            copy.start()

    for number in range(chunks):
        for copy in chunk_copies(number, layers, groups, pairs, sems):
            copy.wait()
        for step in range(layers):
            layer = number * layers + step
            for row in range(x_rows):
                temp_out[row, layer] = taken(temp_buf, layer, row, groups)
                coef_out[row, layer] = taken(coef_buf, layer, row, groups)


def spread(temp, coef, after):
    depth, x_rows, span = temp.shape
    layers = 4
    form = jax.ShapeDtypeStruct((x_rows, depth, SUB, span // SUB), f32)
    raw = pltpu.VMEM((depth * x_rows // SUB, span // LANES * SUB, LANES), f32)
    return pl.pallas_call(
        functools.partial(spread_kernel, layers),
        in_specs=[hbm()] * 3,
        out_specs=[vmem()] * 2,
        out_shape=[form, form],
        scratch_shapes=[raw, raw, pltpu.SemaphoreType.DMA((2, depth // layers))],
        compiler_params=params(44),
        cost_estimate=cost(1e6, 16 * MIB),
        name="spread",
    )(raw_rows(temp), raw_rows(coef), after)


def plate_rows(refs, x_rows, depth, width):
    if len(refs) == 1:
        return [(0, x_rows, refs[0], None)]
    low, inner, high = refs
    return [(0, width, low, 0), (width, x_rows - width, inner, None), (x_rows - width, x_rows, high, 0)]


def coef_rows(coef, low_c, high_c, width):
    x_rows, depth = coef.shape[:2]
    base = width * depth
    return Rows(
        depth,
        (1 - width, 0, low_c, base),
        (0, x_rows, coef, None),
        (x_rows, x_rows + width - 1, high_c, base),
    )


def plate(refs, owned, width, turn):
    own, refs = refs[:owned], refs[owned:]
    low, high, coef, low_c, high_c, source, low_s, high_s = refs[:8]
    x_rows, depth = coef.shape[:2]
    temp = Rows(
        depth,
        (-width, 0, low, 0),
        *plate_rows(own, x_rows, depth, width),
        (x_rows, x_rows + width, high, 0),
    )
    scale = coef_rows(coef, low_c, high_c, width)
    base = width * depth
    pieces = [(0, x_rows, source, 0)]
    if turn > 0:
        pieces += [(-1, 0, low_s, base), (x_rows, x_rows + 1, high_s, base)]
    heat_in = Rows(1, *pieces)
    if turn == 1 and width == 2:
        for row, other in ((0, -1), (-1, 0), (x_rows - 1, x_rows), (x_rows, x_rows - 1)):

            def missing(row=row, other=other):
                return scale.tile(scale.find(row), row, 0) * heat_in.tile(heat_in.find(other), other, 0)

            temp.late[row] = missing
    return temp, scale, heat_in, refs[8:]


def edge_faces(temp, scale, heat_in, width, x_rows, low_out, high_out, mids):
    depth = temp.depth
    for out, start in ((low_out, 0), (high_out, x_rows - width)):

        def emit(row, layer, value, out=out, start=start):
            out[(row - start) * depth + layer] = value

        several(temp, scale, heat_in, width, start, start + width, mids, emit)


def first_edge_kernel(
    width, depth, low, high, low_c, high_c, strip, source, low_out, high_out, *mids
):
    x_rows = source.shape[0]
    base = width * depth
    temp = Rows(
        depth,
        (-width, 0, low_c, 0),
        (0, width, low, 0),
        (width, 2 * width, strip, 0),
        (x_rows - 2 * width, x_rows - width, strip, 2 * base),
        (x_rows - width, x_rows, high, 0),
        (x_rows, x_rows + width, high_c, 0),
    )
    scale = Rows(
        depth,
        (1 - width, 0, low_c, base),
        (0, width - 1, low, base),
        (width - 1, 2 * width - 1, strip, base),
        (x_rows - 2 * width + 1, x_rows - width + 1, strip, 3 * base),
        (x_rows - width + 1, x_rows, high, base),
        (x_rows, x_rows + width - 1, high_c, base),
    )
    heat_in = Rows(1, (0, x_rows, source, 0))
    edge_faces(temp, scale, heat_in, width, x_rows, low_out, high_out, mids)
    low_out[base] = source[0]
    high_out[base] = source[x_rows - 1]


def first_edge(faces, strip, source, width, depth):
    lanes = source.shape[2]
    face = jax.ShapeDtypeStruct((width * depth + 1, SUB, lanes), f32)
    return pl.pallas_call(
        functools.partial(first_edge_kernel, width, depth),
        in_specs=[vmem()] * 6,
        out_specs=[vmem()] * 2,
        out_shape=[face, face],
        scratch_shapes=mids_for(width, 3 * width - 2, depth, lanes),
        compiler_params=params(16),
        cost_estimate=cost(12 * 12 * depth * SUB * lanes, 4 * MIB),
        name="edge",
    )(*faces, strip, source)


def edge_kernel(width, owned, turn, *refs):
    temp, scale, heat_in, (low_out, high_out, *mids) = plate(refs, owned, width, turn)
    edge_faces(temp, scale, heat_in, width, refs[owned + 5].shape[0], low_out, high_out, mids)


def edge(own, operands, width, turn):
    coef = operands[2]
    _, depth, _, lanes = coef.shape
    face = jax.ShapeDtypeStruct((width * depth, SUB, lanes), f32)
    return pl.pallas_call(
        functools.partial(edge_kernel, width, len(own), turn),
        in_specs=[vmem()] * (len(own) + len(operands)),
        out_specs=[vmem()] * 2,
        out_shape=[face, face],
        scratch_shapes=mids_for(width, 3 * width - 2, depth, lanes),
        compiler_params=params(16),
        cost_estimate=cost(12 * 12 * depth * SUB * lanes, 4 * MIB),
        name="edge",
    )(*own, *operands)


def inner_kernel(width, owned, turn, *refs):
    temp, scale, heat_in, (out, *mids) = plate(refs, owned, width, turn)
    x_rows = refs[owned + 5].shape[0]

    def emit(row, layer, value):
        out[row - width, layer] = value

    several(temp, scale, heat_in, width, width, x_rows - width, mids, emit)


def inner(own, operands, width, turn):
    coef = operands[2]
    x_rows, depth, _, lanes = coef.shape
    return pl.pallas_call(
        functools.partial(inner_kernel, width, len(own), turn),
        in_specs=[vmem()] * (len(own) + len(operands)),
        out_specs=vmem(),
        out_shape=jax.ShapeDtypeStruct((x_rows - 2 * width, depth, SUB, lanes), f32),
        scratch_shapes=mids_for(width, x_rows - 2, depth, lanes),
        compiler_params=params(16),
        cost_estimate=cost(12 * 26 * depth * SUB * lanes, 12 * MIB),
        name="inner",
    )(*own, *operands)


def lay_out(staged, wall, halves):
    def emit(row, layer, value):
        if layer == 0:
            wall[row] = value
        group, place = row // SUB, row % SUB
        for half in range(halves):
            staged[layer, group, pl.ds(half * SUB + place, SUB, stride=SUB * halves), :] = value[
                :, half * LANES : (half + 1) * LANES
            ]

    return emit


def middle_kernel(width, owned, turn, *refs):
    temp, scale, heat_in, (staged, wall, *mids) = plate(refs, owned, width, turn)
    x_rows = wall.shape[0]
    emit = lay_out(staged, wall, wall.shape[2] // LANES)
    several(temp, scale, heat_in, width, width, x_rows - width, mids, emit)


def plate_form(coef):
    x_rows, depth, _, lanes = coef.shape
    return [
        jax.ShapeDtypeStruct((depth, x_rows // SUB, lanes // LANES * SUB * SUB, LANES), f32),
        jax.ShapeDtypeStruct((x_rows, SUB, lanes), f32),
    ]


def middle(own, operands, width, turn):
    coef = operands[2]
    x_rows, depth, _, lanes = coef.shape
    return pl.pallas_call(
        functools.partial(middle_kernel, width, len(own), turn),
        in_specs=[vmem()] * (len(own) + len(operands)),
        out_specs=[vmem()] * 2,
        out_shape=plate_form(coef),
        scratch_shapes=mids_for(width, x_rows - 2, depth, lanes),
        compiler_params=params(16),
        cost_estimate=cost(12 * 26 * depth * SUB * lanes, 12 * MIB),
        name="middle",
    )(*own, *operands)


def finish_kernel(width, owned, turn, *refs):
    temp, scale, heat_in, rest = plate(refs, owned, width, turn)
    _, _, out, staged, wall, out_sem, *mids = rest
    x_rows = wall.shape[0]
    depth = temp.depth
    put = lay_out(staged, wall, wall.shape[2] // LANES)
    groups = x_rows // SUB
    piece = depth // 4

    def copy_of(group, start, count, sem):
        at = pl.ds(start, count)
        return pltpu.make_async_copy(staged.at[at, group], out.at[at, group], out_sem.at[sem])

    copies = [copy_of(group, 0, depth, group) for group in range(groups - 1)]
    ends = [copy_of(groups - 1, start * piece, piece, groups + start) for start in range(4)]

    def emit(row, layer, value):
        put(row, layer, value)
        if row == x_rows - 1 and (layer + 1) % piece == 0:
            ends[layer // piece].start()

    for copy in copies[1:]:
        copy.start()
    several(temp, scale, heat_in, width, 0, width, mids, put)
    for copy in copies[:1]:
        copy.start()
    several(temp, scale, heat_in, width, x_rows - width, x_rows, mids, emit)
    for copy in copies + ends:
        copy.wait()


def finish(own, operands, staged, wall, width, turn):
    coef = operands[2]
    x_rows, depth, _, lanes = coef.shape
    count = len(own) + len(operands)
    form = plate_form(coef)
    out, _, wall = pl.pallas_call(
        functools.partial(finish_kernel, width, len(own), turn),
        in_specs=[vmem()] * (count + 2),
        out_specs=[hbm(), vmem(), vmem()],
        out_shape=[form[0], *form],
        scratch_shapes=[pltpu.SemaphoreType.DMA((x_rows // SUB + 4,))] + mids_for(width, 3 * width - 2, depth, lanes),
        input_output_aliases={count: 1, count + 1: 2},
        compiler_params=params(16),
        cost_estimate=cost(12 * 12 * depth * SUB * lanes, 8 * MIB),
        name="finish",
    )(*own, *operands, staged, wall)
    span = lanes * SUB
    out = out.reshape(depth, x_rows // SUB, span // LANES, SUB, LANES).transpose(0, 1, 3, 2, 4)
    return out.reshape(depth, x_rows, span), wall


def gather_tiles(positions, temps, out):
    for tile in range(out.shape[1]):
        at = slice(tile * TILE, (tile + 1) * TILE)
        for comp in range(3):
            out[comp, tile : tile + 1, :] = positions[comp : comp + 1, at]
        out[3, tile : tile + 1, :] = temps[:, at]


def tables(ref, right, turned, warm, first_tile):
    tiles = ref.shape[1]
    comps = [ref[comp] for comp in range(3)]
    square = comps[0] * comps[0] + comps[1] * comps[1] + comps[2] * comps[2]
    rows = []
    for comp in comps:
        a, b, c = parts_of(comp, 3)
        rows += [2.0 * a, 2.0 * b, 2.0 * a, 2.0 * b, 2.0 * c, 2.0 * a]
    rows += [jnp.ones_like(square)] * 3 + parts_of(-square, 3)
    rows += [jnp.zeros_like(square)] * (FEATURES - len(rows))
    for number, row in enumerate(rows):
        right[pl.ds(number, tiles, stride=FEATURES), :] = row
    across = jnp.transpose(ref[3])
    for tile in range(tiles):
        warm[first_tile + tile] = jnp.broadcast_to(across[:, tile : tile + 1], (TILE, TILE))
        block = right[tile * FEATURES : (tile + 1) * FEATURES, :]
        turned[first_tile + tile] = jnp.transpose(block).astype(bf16)


def prepare_kernel(devices, positions, temps, owner_ref, _, own, rank_ref, left, turned, warm, plain):
    gather_tiles(positions, temps, own)
    ghosts = owner_ref.shape[1]
    block = 256
    before = lax.broadcasted_iota(i32, (block, block), 0) < lax.broadcasted_iota(i32, (block, block), 1)
    ramp = before.astype(f32).astype(bf16)
    carried = jnp.zeros((devices, 1), f32)
    for start in range(0, ghosts, block):
        named = sublane_is(owner_ref[:, start : start + block], devices)
        ones = named.astype(f32)
        counted = dot(ones.astype(bf16), ramp) + carried
        rank = jnp.sum(jnp.where(named, counted, 0.0), axis=0, keepdims=True)
        rank_ref[:, start : start + block] = rank.astype(i32)
        carried = carried + jnp.sum(ones, axis=1, keepdims=True)

    tables(own, plain, turned, warm, 0)
    tiles = own.shape[1]
    comps = [own[comp] for comp in range(3)]
    square = comps[0] * comps[0] + comps[1] * comps[1] + comps[2] * comps[2]
    rows = []
    for comp in comps:
        a, b, c = parts_of(comp, 3)
        rows += [a, a, b, b, a, c]
    rows += parts_of(1.0 - square, 3) + [jnp.ones_like(square)] * 3
    rows += [jnp.zeros_like(square)] * (FEATURES - len(rows))
    for number, row in enumerate(rows):
        plain[pl.ds(number, tiles, stride=FEATURES), :] = row
    left[...] = plain[...].astype(bf16)


def prepare(positions, temps, owner, after, devices):
    tiles = positions.shape[1] // TILE
    return pl.pallas_call(
        functools.partial(prepare_kernel, devices),
        in_specs=[vmem()] * 3 + [hbm()],
        out_specs=[vmem()] * 5,
        out_shape=[
            jax.ShapeDtypeStruct((4, tiles, TILE), f32),
            jax.ShapeDtypeStruct(owner.shape, i32),
            jax.ShapeDtypeStruct((tiles * FEATURES, TILE), bf16),
            jax.ShapeDtypeStruct((tiles, TILE, FEATURES), bf16),
            jax.ShapeDtypeStruct((tiles, TILE, TILE), f32),
        ],
        scratch_shapes=[pltpu.VMEM((tiles * FEATURES, TILE), f32)],
        compiler_params=params(16),
        cost_estimate=cost(8e6, 2e6),
        name="prepare",
    )(positions, temps, owner, after)


def heat_kernel(
    devices,
    slots,
    together,
    far_pairs,
    live,
    own,
    near_pos,
    near_temps,
    left,
    own_turned,
    own_warm,
    particle,
    owner,
    rank,
    cell,
    seen,
    out,
    send,
    near,
    right,
    turned,
    warm,
    total,
    pairs,
    sem,
):
    tiles = own.shape[1]
    listed = pltpu.make_async_copy(far_pairs, pairs, sem)
    listed.start()
    gather_tiles(near_pos, near_temps, near)
    turned[:tiles] = own_turned[...]
    warm[:tiles] = own_warm[...]
    tables(near, right, turned, warm, tiles)
    total[...] = jnp.zeros(total.shape, f32)
    listed.wait()

    def several_pairs(number, carry):
        found = []
        for step in range(together):
            at = number * together + step
            first, second = pairs[0, at], pairs[1, at]
            features = left[pl.ds(pl.multiple_of(first * FEATURES, FEATURES), FEATURES), :]
            inside = jnp.maximum(dot(turned[second], features), 0.0)
            gained = (inside * inside) * (warm[second] - own[3, pl.ds(first, 1), :])
            gained = jnp.sum(gained.reshape(TILE // SUB, SUB, TILE), axis=0)
            found.append((jnp.where(at < live[0], first, tiles), gained))
        for place, gained in found:
            total[place] += gained
        return carry

    lax.fori_loop(0, (live[0] + together - 1) // together, several_pairs, 0)
    out[...] = own[3] + heat_rate * jnp.sum(total[:tiles], axis=1)

    pieces = [part.astype(bf16) for part in parts_of(jnp.transpose(out[...]), 3)]
    table = jnp.concatenate(pieces, axis=1)
    ghosts = particle.shape[1]
    packed = [jnp.zeros((2 * devices, slots), f32) for _ in range(3)]
    block = 512
    for start in range(0, ghosts, block):
        at = slice(start, start + block)
        mirrored = particle[:, at]
        high = sublane_is(mirrored // TILE, tiles).astype(f32).astype(bf16)
        picked = dot(table, jnp.concatenate([high] * 3, axis=0))
        low = sublane_is(mirrored % TILE, TILE)
        value = jnp.sum(jnp.where(low, picked, 0.0), axis=0, keepdims=True)
        flux = wall_heat * (value - seen[:, at])
        cells = cell[:, at]
        cell_parts = [((cells // 256) * 256).astype(f32), (cells % 256).astype(f32), jnp.zeros_like(flux)]
        line = lax.broadcasted_iota(i32, (2 * devices, block), 0)
        named = line // 2 == owner[:, at]
        is_cell = line % 2 == 1
        slot = sublane_is(rank[:, at], slots).astype(f32).astype(bf16)
        for number, part in enumerate(parts_of(flux, 3)):
            chosen = jnp.where(named, jnp.where(is_cell, cell_parts[number], part), 0.0)
            packed[number] = packed[number] + dot_lanes(chosen.astype(bf16), slot)
    send[...] = packed[0] + packed[1] + packed[2]


def heat(pairs, live, own, near_pos, near_temps, made, particle, owner, rank, cell, seen, devices, slots):
    tiles = own.shape[1]
    together = 16 if pairs.shape[1] % 16 == 0 else 1
    smem = pl.BlockSpec(memory_space=pltpu.SMEM)
    return pl.pallas_call(
        functools.partial(heat_kernel, devices, slots, together),
        in_specs=[hbm(), smem] + [vmem()] * 11,
        out_specs=[vmem(), vmem()],
        out_shape=[
            jax.ShapeDtypeStruct((tiles, TILE), f32),
            jax.ShapeDtypeStruct((2 * devices, slots), f32),
        ],
        scratch_shapes=[
            pltpu.VMEM((4, tiles, TILE), f32),
            pltpu.VMEM((tiles * FEATURES, TILE), f32),
            pltpu.VMEM((2 * tiles, TILE, FEATURES), bf16),
            pltpu.VMEM((2 * tiles, TILE, TILE), f32),
            pltpu.VMEM((tiles + 1, SUB, TILE), f32),
            pltpu.SMEM(pairs.shape, i32),
            pltpu.SemaphoreType.DMA,
        ],
        compiler_params=params(16),
        cost_estimate=cost(12 * 4.2e6, 1 * MIB),
        name="heat",
    )(pairs, live, own, near_pos, near_temps, *made, particle, owner, rank, cell, seen)


def ghost_lanes(received, first, count, comp):
    rows = [received[2 * device + comp : 2 * device + comp + 1, :] for device in range(first, first + count)]
    return rows[0] if count == 1 else jnp.concatenate(rows, axis=1)


def devices_together(devices, slots):
    return 2 if slots == LANES and devices % 2 == 0 else 1


def surface_kernel(received, out):
    devices = received.shape[0] // 2
    count = devices_together(devices, received.shape[1])
    high_count, low_count = out.shape
    total = jnp.zeros((2 * high_count, low_count), f32)
    for device in range(0, devices, count):
        flux = ghost_lanes(received, device, count, 0)
        cells = ghost_lanes(received, device, count, 1).astype(i32)
        high = sublane_is(cells // low_count, high_count)
        low = sublane_is(cells % low_count, low_count).astype(f32).astype(bf16)
        chosen = [jnp.where(high, part, 0.0).astype(bf16) for part in parts_of(flux, 2)]
        total = total + dot_lanes(jnp.concatenate(chosen, axis=0), low)
    out[...] = (total[:high_count] + total[high_count:]) * (1.0 / SUBSTEPS)


def surface_of(received, high_count, low_count):
    return pl.pallas_call(
        surface_kernel,
        in_specs=[vmem()],
        out_specs=vmem(),
        out_shape=jax.ShapeDtypeStruct((high_count, low_count), f32),
        compiler_params=params(16),
        cost_estimate=cost(6e7, 2e5),
        name="surface",
    )(received)


def wall_kernel(received, wall, out):
    devices = received.shape[0] // 2
    high_count, low_count = wall.shape
    pieces = [part.astype(bf16) for part in parts_of(jnp.transpose(wall[...]), 2)]
    table = jnp.concatenate(pieces, axis=1)
    slots = received.shape[1]
    count = devices_together(devices, slots)
    for device in range(0, devices, count):
        cells = ghost_lanes(received, device, count, 1).astype(i32)
        high = sublane_is(cells // low_count, high_count).astype(f32).astype(bf16)
        picked = dot(table, jnp.concatenate([high, high], axis=0))
        low = sublane_is(cells % low_count, low_count)
        found = jnp.sum(jnp.where(low, picked, 0.0), axis=0, keepdims=True)
        for number in range(count):
            out[device + number : device + number + 1, :] = found[:, number * slots : (number + 1) * slots]


def wall_of(received, wall):
    return pl.pallas_call(
        wall_kernel,
        in_specs=[vmem()] * 2,
        out_specs=vmem(),
        out_shape=jax.ShapeDtypeStruct((received.shape[0] // 2, received.shape[1]), f32),
        compiler_params=params(16),
        cost_estimate=cost(6e7, 2e5),
        name="wall",
    )(received, wall)


def back_kernel(returned, owner, rank, out):
    devices, slots = returned.shape
    pieces = [part.astype(bf16) for part in parts_of(jnp.transpose(returned[...]), 3)]
    table = jnp.concatenate(pieces, axis=1)
    block = 512
    for start in range(0, owner.shape[1], block):
        at = slice(start, start + block)
        named = sublane_is(owner[:, at], devices).astype(f32).astype(bf16)
        picked = dot(table, jnp.concatenate([named] * 3, axis=0))
        slot = sublane_is(rank[:, at], slots)
        out[:, at] = jnp.sum(jnp.where(slot, picked, 0.0), axis=0, keepdims=True)


def back_of(returned, owner, rank):
    return pl.pallas_call(
        back_kernel,
        in_specs=[vmem()] * 3,
        out_specs=vmem(),
        out_shape=jax.ShapeDtypeStruct(owner.shape, f32),
        compiler_params=params(16),
        cost_estimate=cost(6e6, 1e5),
        name="back",
    )(returned, owner, rank)


def between(low_face, high_face):
    count = lax.axis_size(AXES)
    upward = [(i, i + 1) for i in range(count - 1)]
    downward = [(target, source) for source, target in upward]
    return lax.ppermute(high_face, AXES, upward), lax.ppermute(low_face, AXES, downward)


def on_device(
    positions,
    particle_temp,
    pair_list,
    pair_count,
    ghost_particle,
    ghost_owner,
    ghost_cell,
    wall_seen,
    solid_temp,
    conduct,
):
    width = WIDTH
    depth, x_rows, span = solid_temp.shape
    particles = positions.shape[1]
    devices = lax.axis_size(AXES)
    ghosts = ghost_cell.shape[0]
    slots = max(2, 2 * ghosts // devices)
    sub_count = lax.axis_size("sub")
    lanes = span // SUB

    owner = ghost_owner.reshape(1, ghosts)
    temps = particle_temp.reshape(1, particles)
    backward = [(i, (i - 1) % sub_count) for i in range(sub_count)]
    near_pos = lax.ppermute(positions, "sub", backward)
    near_temps = lax.ppermute(temps, "sub", backward)
    low_face, high_face, strip = rim(solid_temp, conduct, near_pos, near_temps, width)
    low_c, high_c = between(low_face, high_face)
    own, rank, *made = prepare(positions, temps, owner, low_face, devices)

    particle_out, send = heat(
        pair_list.T,
        pair_count,
        own,
        near_pos,
        near_temps,
        made,
        ghost_particle.reshape(1, ghosts),
        owner,
        rank,
        ghost_cell.reshape(1, ghosts),
        wall_seen.reshape(1, ghosts),
        devices,
        slots,
    )
    received = lax.all_to_all(
        send.reshape(devices, 2 * slots), AXES, split_axis=0, concat_axis=0, tiled=True
    ).reshape(2 * devices, slots)
    source = surface_of(received, x_rows * SUB, lanes).reshape(x_rows, SUB, lanes)

    low_face, high_face = first_edge(
        [low_face, high_face, low_c, high_c], strip.reshape(-1, SUB, lanes), source, width, depth
    )
    low_s, high_s = low, high = between(low_face, high_face)
    temp, coef = spread(solid_temp, conduct, low_face)

    last = SUBSTEPS // width - 1
    inside = inner([temp], [low_c, high_c, coef, low_c, high_c, source, low_c, high_c], width, 0)
    own_rows = [low_face, inside, high_face]
    for turn in range(1, last):
        operands = [low, high, coef, low_c, high_c, source, low_s, high_s]
        low_face, high_face = edge(own_rows, operands, width, turn)
        inside = inner(own_rows, operands, width, turn)
        own_rows = [low_face, inside, high_face]
        low, high = between(low_face, high_face)
    staged, wall = middle(own_rows, [low_s, high_s, coef, low_c, high_c, source, low_s, high_s], width, last)
    operands = [low, high, coef, low_c, high_c, source, low_s, high_s]
    solid_out, wall = finish(own_rows, operands, staged, wall, width, last)
    answer = wall_of(received, wall.reshape(x_rows * SUB, lanes))
    returned = lax.all_to_all(answer, AXES, split_axis=0, concat_axis=0, tiled=True)
    ghost_temp = back_of(returned, owner, rank)
    return (particle_out.reshape(-1), solid_out, ghost_temp.reshape(-1))


def solution(mesh):
    placed = (
        P(None, AXES),
        P(AXES),
        P(AXES, None),
        P(AXES),
        P(AXES),
        P(AXES, None),
        P(AXES),
        P(AXES),
        P(None, AXES, None),
        P(None, AXES, None),
    )
    return jax.shard_map(
        on_device,
        mesh=mesh,
        in_specs=placed,
        out_specs=(P(AXES), P(None, AXES, None), P(AXES)),
        check_vma=False,
    )
```
